32 devices in a mesh: grp: 2 (over y), adp: 4 (over z), tp: 4 (over x, core).
Axes of the slice: x: 2, y: 2, z: 4, core: 2. Of those that a mesh axis runs over, the one named last changes fastest.
Arguments:
- tokens: bfloat16 [6144, 8192], P(('grp', 'adp'), 'tp'), parts along dimension 0, may hold values from -6 to 6
- adapter_ids: int32 [6144, 1], P(('grp', 'adp')), parts along dimension 0, may hold values from 0 to 7; in each aligned block of 768 rows (0 to 767, 768 to 1535, ...) at most 192 rows name the same one
- base_weight: bfloat16 [8192, 1024], P('tp'), may hold values from -0.0625 to 0.0625
- channel_scale: float32 [1024], P('tp'), may hold values from 0.5 to 2
- adapter_down: bfloat16 [8, 8192, 64], P('adp', 'tp'), may hold values from -0.0625 to 0.0625
- adapter_up: bfloat16 [8, 64, 1024], P('adp', None, 'tp'), may hold values from -0.75 to 0.75
- sign_bits: int32 [128], replicated, may hold values from 0 to 1
Outputs:
- rotated_values: bfloat16 [6144, 1024], P(('grp', 'adp'), 'tp'), parts along dimension 0
The draws below stay inside these ranges and needn't reach their ends.
There are 2 independent parts, one for each index of `grp`. The reference program is written for one: setup_inputs(seed, part) draws one part's arguments, and reference() takes and returns one part's arrays. A program takes and returns all parts, laid end to end along the dimension named above; an argument that names none is the same for every part. Nothing has to cross between parts.
Inputs may be any that keep to these rules, and one draw needn't show every extreme that they name: `adapter_ids`: within each aligned block of 768 rows no adapter is named by more than 192 rows, a bound that some block reaches.
All inputs are finite; a program needn't handle non-finite values.
Results may differ from the reference program's by a relative error of at most 0.013.
Values may be sent and summed in bfloat16 or wider, within the bound.
No kernel may reach another device: no remote copies, remote signals or barrier semaphores. Data moves between devices by JAX's collectives and lax.ppermute only.
A program may use at most 64 MiB of HBM per device.

```python
import math
import jax
import jax.numpy as jnp
import numpy as np
from jax import lax

D = 8192
KV_HEADS = 8
HEAD_DIM = 128
RANK = 64
TOK_DEV = 768
KVW = 1024
ADAPTERS = 8
CAP = 192
TOKENS = 3072
N_ADP = 4
N_TP = 4


def plant(array, key, low, top_value):
    shape = array.shape
    spot = [jax.random.randint(jax.random.fold_in(key, axis), (), 0, shape[axis]) for axis in range(len(shape))]
    array = array.at[tuple(spot)].set(low)
    longest = shape.index(max(shape))
    spot[longest] = (spot[longest] + 1) % shape[longest]
    return array.at[tuple(spot)].set(top_value)


def level_of(key, extent, shards, smallest, top_value):
    def one(position, shards_of):
        steps = jax.random.uniform(jax.random.fold_in(jax.random.fold_in(key, 6), position), (shards_of,), jnp.float32, smallest / len(shards), top_value / len(shards))
        return jnp.repeat(jnp.exp(steps), extent[position] // shards_of).reshape((-1,) + (1,) * (len(extent) - position - 1))

    loudness = one(*shards[0])
    for cut in shards[1:]:
        loudness = loudness * one(*cut)
    return loudness


def deal_out(key, own, number, rows, count, top, most, lean):
    order = jax.random.permutation(key, count)
    heavy_load, common = portions_of(count, rows * top, most, lean, True), portions_of(count, rows * top, most, lean, False)
    places = jnp.arange(count)

    def named(tallies, rotation):
        used = int((tallies > 0).sum())
        fixed = max(1, used // 4)
        shifted = fixed + (places - fixed + rotation * (used - fixed)) % max(1, count - fixed)
        return jnp.zeros((count,), jnp.int32).at[order[jnp.where(places < fixed, places, shifted)]].set(jnp.asarray(tallies, jnp.int32))

    tallies = jnp.where(number % 4 == 0, named(heavy_load, number // 4), named(common, number - number // 4 - 1))
    mixed = jax.random.permutation(jax.random.fold_in(own, 3), count)
    source_of, taker = mixed[0:count // 2 * 2:2], mixed[1:count // 2 * 2:2]
    slack = jnp.minimum(tallies[source_of] - 1, most - tallies[taker]) // 2
    slack = jnp.where((source_of == order[0]) | (taker == order[0]) | (tallies[taker] == 0), 0, jnp.maximum(slack, 0))
    shifted = jax.random.randint(jax.random.fold_in(own, 4), (count // 2,), 0, 1 << 20) % (slack + 1)
    tallies = tallies.at[source_of].add(-shifted).at[taker].add(shifted)
    labels = jnp.searchsorted(jnp.cumsum(tallies), jnp.arange(rows * top), side="right").astype(jnp.int32)
    listing = labels.reshape(top, rows).T
    listing = listing[jax.random.permutation(jax.random.fold_in(own, 1), rows)]
    rotation = jax.random.randint(jax.random.fold_in(own, 2), (rows, 1), 0, top)
    return jnp.take_along_axis(listing, (jnp.arange(top)[None, :] + rotation) % top, axis=1)


def portions_of(amount, total, limit, skew, full):
    portions = [(1 << 20) // math.isqrt(rank ** skew) + 1 for rank in range(1, amount + 1)]
    largest = limit if full else min(limit, max(-(-total // amount), total * portions[0] // sum(portions)))
    least = 1 if total - largest >= amount - 1 else 0
    counts, surplus = [largest] + [least] * (amount - 1), total - largest - least * (amount - 1)
    while surplus > 0:
        free = [i for i in range(1, amount) if counts[i] < largest] or [i for i in range(1, amount) if counts[i] < limit]
        mass, left = sum([portions[i] for i in free]), surplus
        for i in free:
            more = min(limit - counts[i], max(1, left * portions[i] // mass), surplus)
            counts[i] = counts[i] + more
            surplus = surplus - more
    return np.array(counts)


def normal_values(stream_key, dims, deviation, most, shards=(), held_as=jnp.bfloat16):
    drawn = deviation * jax.random.normal(stream_key, dims, jnp.float32)
    if shards:
        drawn = drawn * level_of(stream_key, dims, shards, -0.22, 0.18)
    return jnp.clip(drawn, -most, most).astype(held_as)


def setup_inputs(seed: int = 0, part: int = 0) -> dict:
    arg_keys = jax.random.split(jax.random.key(seed), 8)
    part_splits = jax.random.split(jax.random.fold_in(arg_keys[7], part), 8)
    tokens = normal_values(part_splits[0], (TOKENS, D), 1.0, 6.0, ((0, 4), (1, 4)))
    adapter_ids_keys = jax.random.split(jax.random.fold_in(part_splits[1], 1), TOKENS // TOK_DEV)
    adapter_ids_turns = jax.random.permutation(jax.random.fold_in(part_splits[1], 3), TOKENS // TOK_DEV)
    adapter_ids = jax.vmap(lambda own, number: deal_out(jax.random.fold_in(part_splits[1], 2), own, number, TOK_DEV, ADAPTERS, 1, CAP, 2))(adapter_ids_keys, adapter_ids_turns).reshape((TOKENS, 1))
    base_weight = normal_values(arg_keys[2], (D, KVW), D ** -0.5, 0.0625, ((0, 4),))
    channel_scale = jnp.clip(jnp.exp(math.log(2.0) - 1.3862944 * jax.random.uniform(arg_keys[3], (KVW,), jnp.float32) ** level_of(arg_keys[3], (KVW,), ((0, 4),), -0.2, 0.2)), 0.5, 2.0)
    adapter_down = normal_values(arg_keys[4], (ADAPTERS, D, RANK), D ** -0.5, 0.0625, ((0, 4), (1, 4)))
    adapter_up = normal_values(arg_keys[5], (ADAPTERS, RANK, KVW), RANK ** -0.5, 0.75, ((0, 4), (2, 4)))
    sign_bits = plant(jax.random.randint(arg_keys[6], (HEAD_DIM,), 0, 2), jax.random.fold_in(arg_keys[6], 1), 0, 1).astype(jnp.int32)
    return dict(tokens=tokens, adapter_ids=adapter_ids, base_weight=base_weight, channel_scale=channel_scale, adapter_down=adapter_down, adapter_up=adapter_up, sign_bits=sign_bits)


def hadamard(size):
    first = jnp.arange(size, dtype=jnp.int32)[:, None]
    second = jnp.arange(size, dtype=jnp.int32)[None, :]
    shared = jnp.zeros((size, size), jnp.int32)
    for place in range(size.bit_length() - 1):
        shared = shared + jnp.bitwise_and(jnp.right_shift(first, place), 1) * jnp.bitwise_and(jnp.right_shift(second, place), 1)
    return (1 - 2 * (shared % 2)).astype(jnp.float32)

def slot_of(ids_block):
    onehot = (ids_block[:, None] == jnp.arange(ADAPTERS, dtype=jnp.int32)[None, :]).astype(jnp.int32)
    before = jnp.cumsum(onehot, axis=0, dtype=jnp.int32) - 1
    rank = lax.optimization_barrier(jnp.sum(onehot * before, axis=1, dtype=jnp.int32))
    return (ids_block * CAP + rank).astype(jnp.int32)

def reference(tokens, adapter_ids, base_weight, channel_scale, adapter_down, adapter_up, sign_bits):
    width = D // N_TP
    base = jnp.zeros((TOKENS, KVW), jnp.float32)
    for block in range(N_TP):
        part = jnp.dot(tokens[:, block * width:(block + 1) * width], base_weight[block * width:(block + 1) * width], preferred_element_type=jnp.float32)
        part = lax.optimization_barrier(part.astype(jnp.bfloat16)).astype(jnp.float32)
        base = base + part
    down32 = adapter_down.astype(jnp.float32)
    up32 = adapter_up.astype(jnp.float32)

    def one_block(pair):
        rows_in, ids_block = pair
        slot = slot_of(ids_block)
        buffer = jnp.zeros((ADAPTERS * CAP, D), jnp.float32).at[slot].set(rows_in.astype(jnp.float32))
        buffer = buffer.reshape(ADAPTERS, CAP, D)
        low = jnp.einsum('acd,adr->acr', buffer, down32, precision=lax.Precision.HIGHEST)
        low = lax.optimization_barrier(low.astype(jnp.bfloat16)).astype(jnp.float32)
        delta = jnp.einsum('acr,are->ace', low, up32, precision=lax.Precision.HIGHEST).astype(jnp.bfloat16)
        return delta.reshape(ADAPTERS * CAP, KVW)[slot]
    delta_rows = lax.map(one_block, (tokens.reshape(N_ADP, TOK_DEV, D), adapter_ids[:, 0].reshape(N_ADP, TOK_DEV)))
    value = base * channel_scale[None, :] + delta_rows.reshape(TOKENS, KVW).astype(jnp.float32)
    signed = value.reshape(TOKENS, KV_HEADS, HEAD_DIM) * (1 - 2 * sign_bits).astype(jnp.float32)[None, None, :]
    matrix = hadamard(HEAD_DIM) / jnp.sqrt(jnp.float32(HEAD_DIM))
    rotated = jnp.einsum('thd,de->the', signed, matrix, precision=lax.Precision.HIGHEST)
    return rotated.reshape(TOKENS, KVW).astype(jnp.bfloat16)
```

```python
import jax
import jax.numpy as jnp
from jax import lax
from jax.sharding import PartitionSpec as P


def hadamard(size):
    first = jnp.arange(size, dtype=jnp.int32)[:, None]
    second = jnp.arange(size, dtype=jnp.int32)[None, :]
    shared = jnp.zeros((size, size), jnp.int32)
    for place in range(size.bit_length() - 1):
        shared = shared + jnp.bitwise_and(jnp.right_shift(first, place), 1) * jnp.bitwise_and(
            jnp.right_shift(second, place), 1
        )
    return (1 - 2 * (shared % 2)).astype(jnp.float32)


def swap(x, axis, bit):
    return lax.ppermute(x, axis, [(i, i ^ bit) for i in range(lax.axis_size(axis))])


def gathered(own, groups, planes):
    held = {0: own}
    bit = planes // 2
    while bit:
        held.update({at | bit: swap(value, "adp", bit) for at, value in held.items()})
        bit //= 2
    every = []
    for at, value in held.items():
        if at:
            every.append((at, 0, value))
            every += [(at, off, swap(value, "grp", off)) for off in range(1, groups)]
    return every


def reduce_scatter(partial, width, parts):
    me = lax.axis_index("tp")
    rows = partial.shape[0]
    blocks = partial.reshape(rows, parts, width)
    bit = 1
    while bit < parts:
        mine = (me // bit) % 2
        pairs = blocks.reshape(rows, -1, 2, width)
        keep = lax.dynamic_index_in_dim(pairs, mine, 2, keepdims=False)
        give = lax.dynamic_index_in_dim(pairs, 1 - mine, 2, keepdims=False)
        blocks = keep + swap(give.astype(jnp.bfloat16), "tp", bit).astype(jnp.float32)
        bit *= 2
    return blocks.reshape(rows, width)


def local(tokens, adapter_ids, base_weight, channel_scale, adapter_down, adapter_up, sign_bits):
    planes, groups, parts = lax.axis_size("adp"), lax.axis_size("grp"), lax.axis_size("tp")
    z, g = lax.axis_index("adp"), lax.axis_index("grp")
    rows, features = tokens.shape
    here, _, rank = adapter_down.shape
    width = adapter_up.shape[2]
    head = sign_bits.shape[0]
    share = here // groups

    pieces = jnp.concatenate([jnp.swapaxes(adapter_down, 1, 2), adapter_up], axis=2)
    own = lax.dynamic_slice_in_dim(pieces, g * share, share, 0)
    every = [(0, off, lax.dynamic_slice_in_dim(pieces, (g ^ off) * share, share, 0)) for off in range(groups)]
    every += gathered(own, groups, planes)

    partial = jnp.dot(tokens, base_weight, preferred_element_type=jnp.float32)
    base = reduce_scatter(partial, width, parts)

    low = jnp.zeros((rank, rows), jnp.float32)
    masks = []
    for plane, off, piece in every:
        first = (z ^ plane) * here + (g ^ off) * share
        for k in range(share):
            mask = (adapter_ids == first + k).T
            product = lax.dot_general(
                piece[k, :, :features], tokens, (((1,), (1,)), ((), ())), preferred_element_type=jnp.float32
            )
            low = low + jnp.where(mask, product, 0.0)
            masks.append((mask, piece[k, :, features:]))
    bit = 1
    while bit < parts:
        sent = low.astype(jnp.bfloat16)
        low = sent.astype(jnp.float32) + swap(sent, "tp", bit).astype(jnp.float32)
        bit *= 2
    low = low.astype(jnp.bfloat16)

    spread = jnp.concatenate([jnp.where(mask, low, jnp.bfloat16(0)) for mask, _ in masks], axis=0)
    ups = jnp.concatenate([up for _, up in masks], axis=0)
    delta = lax.dot_general(spread, ups, (((0,), (0,)), ((), ())), preferred_element_type=jnp.float32)
    value = base * channel_scale[None, :] + delta
    signed = value.reshape(rows, width // head, head) * (1 - 2 * sign_bits).astype(jnp.float32)[None, None, :]
    matrix = hadamard(head) / jnp.sqrt(jnp.float32(head))
    rotated = jnp.einsum("thd,de->the", signed, matrix, precision=lax.Precision.HIGHEST)
    return rotated.reshape(rows, width).astype(jnp.bfloat16)


def solution(mesh):
    return jax.shard_map(
        local,
        mesh=mesh,
        in_specs=(
            P(("grp", "adp"), "tp"),
            P(("grp", "adp"), None),
            P("tp", None),
            P("tp"),
            P("adp", "tp", None),
            P("adp", None, "tp"),
            P(),
        ),
        out_specs=P(("grp", "adp"), "tp"),
        check_vma=False,
    )
```

```python
import functools

import jax
import jax.numpy as jnp
import numpy as np
from jax import lax
from jax.experimental import pallas as pl
from jax.experimental.pallas import tpu as pltpu
from jax.sharding import PartitionSpec as P

VMEM = pl.BlockSpec(memory_space=pltpu.VMEM)
SMEM = pl.BlockSpec(memory_space=pltpu.SMEM)
F32, BF16 = jnp.float32, jnp.bfloat16
LAST = (((1,), (1,)), ((), ()))


def params(mib):
    return pltpu.CompilerParams(vmem_limit_bytes=mib << 20)


def cost(flops, moved):
    return pl.CostEstimate(flops=flops, bytes_accessed=moved, transcendentals=0)


def hadamard(size):
    index = np.arange(size)
    shared = index[:, None] & index[None, :]
    parity = np.zeros_like(shared)
    while shared.any():
        parity, shared = parity ^ (shared & 1), shared >> 1
    return jnp.asarray(1 - 2 * parity, BF16)


def swap(x, axis, bit):
    return lax.ppermute(x, axis, [(i, i ^ bit) for i in range(lax.axis_size(axis))])


def rotate(value, signs, matrix):
    head = matrix.shape[0]
    scale = signs * (1.0 / np.sqrt(head))
    turned = []
    for at in range(0, value.shape[1], head):
        signed = value[:, at : at + head] * scale
        high = signed.astype(BF16)
        rest = (signed - high.astype(F32)).astype(BF16)
        turned.append(
            jnp.dot(high, matrix, preferred_element_type=F32) + jnp.dot(rest, matrix, preferred_element_type=F32)
        )
    return turned


def partial_kernel(me_ref, tokens_ref, weight_ref, give_ref, keep_ref):
    step, half = pl.program_id(0), pl.num_programs(0) // 2
    product = jnp.dot(tokens_ref[...], weight_ref[...], preferred_element_type=F32).astype(BF16)

    @pl.when(step < half)
    def _():
        give_ref[0] = product

    @pl.when(step >= half)
    def _():
        keep_ref[0] = product


def partials(me, tokens, weight, parts):
    rows, features = tokens.shape
    width = weight.shape[1] // parts
    half = parts // 2

    def offset(step):
        return jnp.where(step < half, 2 * step + 1, 2 * (step - half))

    block = jax.ShapeDtypeStruct((half, rows, width), BF16)
    return pl.pallas_call(
        partial_kernel,
        grid_spec=pltpu.PrefetchScalarGridSpec(
            num_scalar_prefetch=1,
            grid=(parts,),
            in_specs=[
                pl.BlockSpec((rows, features), lambda step, me: (0, 0)),
                pl.BlockSpec((features, width), lambda step, me: (0, jnp.bitwise_xor(me[0], offset(step)))),
            ],
            out_specs=[
                pl.BlockSpec((1, rows, width), lambda step, me: (jnp.minimum(step, half - 1), 0, 0)),
                pl.BlockSpec((1, rows, width), lambda step, me: (jnp.maximum(step - half, 0), 0, 0)),
            ],
        ),
        out_shape=[block, block],
        compiler_params=params(24),
        cost_estimate=cost(2 * rows * features * width * parts, 2 * (tokens.size + weight.size + rows * width * parts)),
        name="partials",
    )(me, tokens, weight)


def base_kernel(*refs):
    terms, (scale_ref, bits_ref, matrix_ref, out_ref) = refs[:-4], refs[-4:]
    total = terms[0][0].astype(F32)
    for term in terms[1:]:
        total = total + term[0].astype(F32)
    signs = (1 - 2 * bits_ref[...]).astype(F32)
    turned = rotate(total * scale_ref[...], signs, matrix_ref[...])
    out_ref[...] = jnp.concatenate(turned, axis=1)


def rotated_base(terms, scale, bits, matrix):
    _, rows, width = terms[0].shape
    whole = lambda shape: pl.BlockSpec(shape, lambda: (0,) * len(shape))
    return pl.pallas_call(
        base_kernel,
        in_specs=[whole((1, rows, width))] * len(terms) + [whole(a.shape) for a in (scale, bits, matrix)],
        out_specs=whole((rows, width)),
        out_shape=jax.ShapeDtypeStruct((rows, width), F32),
        compiler_params=params(16),
        cost_estimate=cost(4 * rows * width * matrix.shape[0], 2 * rows * width * (len(terms) + 2)),
        name="rotated_base",
    )(*terms, scale, bits, matrix)


def low_kernel(pieces, share, rank, ids_ref, named_ref, tokens_ref, *refs):
    refs, out_ref = refs[:-1], refs[-1]
    features = tokens_ref.shape[1]
    total = None if len(refs) == pieces else refs[pieces][...]
    rows = [refs[i][k, :, :features] for i in range(pieces) for k in range(share)]
    joined = rows[0] if len(rows) == 1 else jnp.concatenate(rows, axis=0)
    product = lax.dot_general(joined, tokens_ref[...], LAST, preferred_element_type=F32)
    for i in range(len(rows)):
        term = jnp.where(ids_ref[...] == named_ref[i], product[i * rank : (i + 1) * rank], 0.0)
        total = term if total is None else total + term
    out_ref[...] = total.astype(out_ref.dtype)


def low_rows(ids, named, tokens, pieces, before, dtype):
    share, rank, _ = pieces[0].shape
    rows, features = tokens.shape
    more = [] if before is None else [before]
    return pl.pallas_call(
        functools.partial(low_kernel, len(pieces), share, rank),
        in_specs=[VMEM, SMEM] + [VMEM] * (1 + len(pieces) + len(more)),
        out_specs=VMEM,
        out_shape=jax.ShapeDtypeStruct((rank, rows), dtype),
        compiler_params=params(24),
        cost_estimate=cost(2 * rows * features * rank * share * len(pieces), 2 * tokens.size),
        name="low_rows",
    )(ids, named, tokens, *pieces, *more)


def ups_kernel(pieces, share, rank, ids_ref, named_ref, bits_ref, matrix_ref, *refs):
    features = refs[0].shape[2] - refs[-2].shape[1]
    up_ref, mask_ref = refs[-2:]
    signs = (1 - 2 * bits_ref[...]).astype(F32)
    ids = jnp.broadcast_to(ids_ref[...], (rank, ids_ref.shape[1])).T
    for i in range(pieces):
        for k in range(share):
            at = (i * share + k) * rank
            turned = rotate(refs[i][k, :, features:].astype(F32), signs, matrix_ref[...])
            up_ref[at : at + rank, :] = jnp.concatenate(turned, axis=1).astype(BF16)
            mask_ref[:, at : at + rank] = jnp.where(ids == named_ref[i * share + k], 1.0, 0.0).astype(BF16)


def rotated_ups(ids, named, bits, matrix, pieces, width):
    share, rank, _ = pieces[0].shape
    rows = ids.shape[1]
    every = len(pieces) * share * rank
    return pl.pallas_call(
        functools.partial(ups_kernel, len(pieces), share, rank),
        in_specs=[VMEM, SMEM, VMEM, VMEM] + [VMEM] * len(pieces),
        out_specs=[VMEM, VMEM],
        out_shape=[jax.ShapeDtypeStruct((every, width), BF16), jax.ShapeDtypeStruct((rows, every), BF16)],
        compiler_params=params(32),
        cost_estimate=cost(4 * every * width * matrix.shape[0], 2 * every * (rows + width)),
        name="rotated_ups",
    )(ids, named, bits, matrix, *pieces)


def final_kernel(mine_ref, theirs_ref, base_ref, up_ref, mask_ref, out_ref):
    low = (mine_ref[...].astype(F32) + theirs_ref[...].astype(F32)).T.astype(BF16)
    every = mask_ref.shape[1]
    spread = jnp.concatenate([low] * (every // low.shape[1]), axis=1) * mask_ref[...]
    delta = jnp.dot(spread, up_ref[...], preferred_element_type=F32)
    out_ref[...] = (base_ref[...] + delta).astype(BF16)


def final(mine, theirs, base, up, mask):
    rows, width = base.shape
    return pl.pallas_call(
        final_kernel,
        in_specs=[VMEM] * 5,
        out_specs=VMEM,
        out_shape=jax.ShapeDtypeStruct((rows, width), BF16),
        compiler_params=params(32),
        cost_estimate=cost(2 * rows * width * up.shape[0], 6 * rows * width),
        name="final",
    )(mine, theirs, base, up, mask)


def local(tokens, adapter_ids, base_weight, channel_scale, adapter_down, adapter_up, sign_bits):
    planes, groups, parts = lax.axis_size("adp"), lax.axis_size("grp"), lax.axis_size("tp")
    z, g, me = lax.axis_index("adp"), lax.axis_index("grp"), lax.axis_index("tp")
    rows, features = tokens.shape
    here, _, rank = adapter_down.shape
    width = adapter_up.shape[2]
    share = here // groups
    matrix = hadamard(sign_bits.shape[0])
    bits, scale, ids = sign_bits[None, :], channel_scale[None, :], adapter_ids.T

    down = jnp.swapaxes(adapter_down, 1, 2)

    def own(off):
        at = (g ^ off) * share
        cut = [lax.dynamic_slice_in_dim(a, at, share, 0) for a in (down, adapter_up)]
        return jnp.concatenate(cut, axis=2)

    def names(held):
        firsts = [(z ^ plane) * here + (g ^ off) * share for plane, off, _ in held]
        return jnp.stack([first + k for first in firsts for k in range(share)]).astype(jnp.int32)

    home = [(0, off, own(off)) for off in range(groups)]
    mine = [(0, 0, home[0][2])]
    swapped = []
    bit = planes // 2
    while bit:
        new = [(plane | bit, 0, swap(piece, "adp", bit)) for plane, _, piece in mine]
        mine += new
        swapped += [(plane, off, swap(piece, "grp", off)) for plane, _, piece in new for off in range(1, groups)]
        bit //= 2

    give, keep = partials(me[None].astype(jnp.int32), tokens, base_weight, parts)
    come = swap(give, "tp", 1)
    terms = [keep[:1], come[:1]]
    bit, sums = 2, None
    while bit < parts:
        sums = keep.astype(F32) + come.astype(F32) if sums is None else sums[0::2] + come.astype(F32)
        come = swap(sums[1::2].astype(BF16), "tp", bit)
        terms.append(come[:1])
        bit *= 2
    base = rotated_base(terms, scale, bits, matrix)

    early = home + mine[1:-1] + swapped[:0]
    middle = [mine[-1]] + swapped[:-1]
    late = swapped[-1:]
    low = low_rows(ids, names(early), tokens, [p for _, _, p in early], None, F32)
    low = low_rows(ids, names(middle), tokens, [p for _, _, p in middle], low, F32)
    low = low_rows(ids, names(late), tokens, [p for _, _, p in late], low, BF16)
    bit = 1
    while bit < parts // 2:
        low = (low.astype(F32) + swap(low, "tp", bit).astype(F32)).astype(BF16)
        bit *= 2
    theirs = swap(low, "tp", bit)
    every = early + middle + late
    up, mask = rotated_ups(ids, names(every), bits, matrix, [p for _, _, p in every], width)
    return final(low, theirs, base, up, mask)


def solution(mesh):
    return jax.shard_map(
        local,
        mesh=mesh,
        in_specs=(
            P(("grp", "adp"), "tp"),
            P(("grp", "adp"), None),
            P("tp", None),
            P("tp"),
            P("adp", "tp", None),
            P("adp", None, "tp"),
            P(),
        ),
        out_specs=P(("grp", "adp"), "tp"),
        check_vma=False,
    )
```

```python
import functools

import jax
import jax.numpy as jnp
import numpy as np
from jax import lax
from jax.experimental import pallas as pl
from jax.experimental.pallas import tpu as pltpu
from jax.sharding import PartitionSpec as P

VMEM = pl.BlockSpec(memory_space=pltpu.VMEM)
SMEM = pl.BlockSpec(memory_space=pltpu.SMEM)
F32, BF16 = jnp.float32, jnp.bfloat16
LAST = (((1,), (1,)), ((), ()))


def params(mib):
    return pltpu.CompilerParams(vmem_limit_bytes=mib << 20)


COST = pl.CostEstimate(flops=1, bytes_accessed=1, transcendentals=0)


def hadamard(size):
    index = np.arange(size)
    shared = index[:, None] & index[None, :]
    parity = np.zeros_like(shared)
    while shared.any():
        parity, shared = parity ^ (shared & 1), shared >> 1
    return jnp.asarray(1 - 2 * parity, BF16)


def swap(x, axis, bit):
    return lax.ppermute(x, axis, [(i, i ^ bit) for i in range(lax.axis_size(axis))])


def after(value, *others):
    return lax.optimization_barrier((value, *others))[0]


def rotate(value, signs, matrix):
    head = matrix.shape[0]
    scale = signs * (1.0 / np.sqrt(head))
    turned = []
    for at in range(0, value.shape[1], head):
        signed = value[:, at : at + head] * scale
        high = signed.astype(BF16)
        rest = (signed - high.astype(F32)).astype(BF16)
        turned.append(
            jnp.dot(high, matrix, preferred_element_type=F32) + jnp.dot(rest, matrix, preferred_element_type=F32)
        )
    return turned


def pack_kernel(g_ref, down_ref, up_ref, out_ref):
    features = down_ref.shape[2]
    out_ref[:, :, :features] = down_ref[...]
    out_ref[:, :, features:] = up_ref[...]


def packed(g, down, up, share):
    _, rank, features = down.shape
    width = up.shape[2]
    return pl.pallas_call(
        pack_kernel,
        grid_spec=pltpu.PrefetchScalarGridSpec(
            num_scalar_prefetch=1,
            grid=(1,),
            in_specs=[
                pl.BlockSpec((share, rank, features), lambda i, g: (g[0], 0, 0)),
                pl.BlockSpec((share, rank, width), lambda i, g: (g[0], 0, 0)),
            ],
            out_specs=pl.BlockSpec((share, rank, features + width), lambda i, g: (0, 0, 0)),
        ),
        out_shape=jax.ShapeDtypeStruct((share, rank, features + width), BF16),
        compiler_params=params(8),
        cost_estimate=COST,
        name="packed",
    )(g, down, up)


def partial_kernel(me_ref, tokens_ref, weight_ref, give_ref, keep_ref):
    parts = 2 * give_ref.shape[0]
    width = give_ref.shape[2]
    for offset in range(parts):
        at = pl.multiple_of(jnp.bitwise_xor(me_ref[0], offset) * width, 128)
        product = jnp.dot(tokens_ref[...], weight_ref[:, pl.ds(at, width)], preferred_element_type=F32)
        (give_ref if offset % 2 else keep_ref)[offset // 2] = product.astype(BF16)


def partials(me, tokens, weight, parts):
    width = weight.shape[1] // parts
    block = jax.ShapeDtypeStruct((parts // 2, tokens.shape[0], width), BF16)
    return pl.pallas_call(
        partial_kernel,
        in_specs=[SMEM, VMEM, VMEM],
        out_specs=[VMEM, VMEM],
        out_shape=[block, block],
        compiler_params=params(24),
        cost_estimate=COST,
        name="partials",
    )(me, tokens, weight)


def add_kernel(*refs):
    total = refs[0][...].astype(F32)
    for term in refs[1:-1]:
        total = total + term[...].astype(F32)
    refs[-1][...] = total.astype(BF16)


def sum_blocks(keep, came):
    stage = len(came)
    _, rows, width = keep.shape
    count = keep.shape[0] >> stage

    def every(power):
        return pl.BlockSpec((1, rows, width), lambda j: ((2 * j + 1) << power, 0, 0))

    return pl.pallas_call(
        add_kernel,
        grid=(count,),
        in_specs=[every(stage - 1)] + [every(stage - 1 - r) for r in range(stage)],
        out_specs=pl.BlockSpec((1, rows, width), lambda j: (j, 0, 0)),
        out_shape=jax.ShapeDtypeStruct((count, rows, width), BF16),
        compiler_params=params(8),
        cost_estimate=COST,
        name="sum_blocks",
    )(keep, *came)


def base_kernel(*refs):
    terms, (scale_ref, bits_ref, matrix_ref, out_ref) = refs[:-4], refs[-4:]
    total = terms[0][0].astype(F32)
    for term in terms[1:]:
        total = total + term[0].astype(F32)
    signs = (1 - 2 * bits_ref[...]).astype(F32)
    turned = rotate(total * scale_ref[...], signs, matrix_ref[...])
    out_ref[...] = jnp.concatenate(turned, axis=1)


def rotated_base(terms, scale, bits, matrix):
    _, rows, width = terms[0].shape
    first = pl.BlockSpec((1, rows, width), lambda i: (0, 0, 0))
    whole = lambda shape: pl.BlockSpec(shape, lambda i: (0,) * len(shape))
    return pl.pallas_call(
        base_kernel,
        grid=(1,),
        in_specs=[first] * len(terms) + [whole(a.shape) for a in (scale, bits, matrix)],
        out_specs=whole((rows, width)),
        out_shape=jax.ShapeDtypeStruct((rows, width), F32),
        compiler_params=params(16),
        cost_estimate=COST,
        name="rotated_base",
    )(*terms, scale, bits, matrix)


def adapter(at_ref, here, share, name):
    if name[0] == "home":
        return at_ref[0] * here + name[1]
    plane, off, k = name
    return jnp.bitwise_xor(at_ref[0], plane) * here + jnp.bitwise_xor(at_ref[1], off) * share + k


def low_kernel(groups, here, share, rank, more, at_ref, ids_ref, tokens_ref, *refs):
    out_ref = refs[-1]
    total = refs[-2][...] if more else None
    for (start, stop), terms in groups:
        rows = [refs[i][k, :, cut : cut + stop - start] for i, k, cut, _ in terms]
        joined = rows[0] if len(rows) == 1 else jnp.concatenate(rows, axis=0)
        product = lax.dot_general(joined, tokens_ref[:, start:stop], LAST, preferred_element_type=F32)
        for n, (_, _, _, name) in enumerate(terms):
            mine = ids_ref[...] == adapter(at_ref, here, share, name)
            term = jnp.where(mine, product[n * rank : (n + 1) * rank], 0.0)
            total = term if total is None else total + term
    out_ref[...] = total.astype(out_ref.dtype)


def low_rows(at, ids, tokens, here, share, groups, arrays, before, dtype):
    rank = arrays[0].shape[1]
    more = [] if before is None else [before]
    return pl.pallas_call(
        functools.partial(low_kernel, groups, here, share, rank, bool(more)),
        in_specs=[SMEM] + [VMEM] * (2 + len(arrays) + len(more)),
        out_specs=VMEM,
        out_shape=jax.ShapeDtypeStruct((rank, tokens.shape[0]), dtype),
        compiler_params=params(24),
        cost_estimate=COST,
        name="low_rows",
    )(at, ids, tokens, *arrays, *more)


def ups_kernel(terms, here, share, rank, at_ref, ids_ref, bits_ref, matrix_ref, *refs):
    up_ref, mask_ref = refs[-2:]
    width = up_ref.shape[1]
    signs = (1 - 2 * bits_ref[...]).astype(F32)
    ids = jnp.broadcast_to(ids_ref[...], (rank, ids_ref.shape[1])).T
    for n, (i, k, cut, name) in enumerate(terms):
        turned = rotate(refs[i][k, :, cut : cut + width].astype(F32), signs, matrix_ref[...])
        up_ref[n * rank : (n + 1) * rank, :] = jnp.concatenate(turned, axis=1).astype(BF16)
        mine = ids == adapter(at_ref, here, share, name)
        mask_ref[:, n * rank : (n + 1) * rank] = jnp.where(mine, 1.0, 0.0).astype(BF16)


def rotated_ups(at, ids, bits, matrix, here, share, terms, arrays, width):
    rank, rows = arrays[0].shape[1], ids.shape[1]
    every = len(terms) * rank
    return pl.pallas_call(
        functools.partial(ups_kernel, terms, here, share, rank),
        in_specs=[SMEM] + [VMEM] * (3 + len(arrays)),
        out_specs=[VMEM, VMEM],
        out_shape=[jax.ShapeDtypeStruct((every, width), BF16), jax.ShapeDtypeStruct((rows, every), BF16)],
        compiler_params=params(32),
        cost_estimate=COST,
        name="rotated_ups",
    )(at, ids, bits, matrix, *arrays)


def final_kernel(mine_ref, theirs_ref, base_ref, up_ref, mask_ref, out_ref):
    low = (mine_ref[...].astype(F32) + theirs_ref[...].astype(F32)).T.astype(BF16)
    every = mask_ref.shape[1]
    spread = jnp.concatenate([low] * (every // low.shape[1]), axis=1) * mask_ref[...]
    delta = jnp.dot(spread, up_ref[...], preferred_element_type=F32)
    out_ref[...] = (base_ref[...] + delta).astype(BF16)


def final(mine, theirs, base, up, mask):
    rows, width = base.shape
    return pl.pallas_call(
        final_kernel,
        in_specs=[VMEM] * 5,
        out_specs=VMEM,
        out_shape=jax.ShapeDtypeStruct((rows, width), BF16),
        compiler_params=params(32),
        cost_estimate=COST,
        name="final",
    )(mine, theirs, base, up, mask)


def local(tokens, adapter_ids, base_weight, channel_scale, adapter_down, adapter_up, sign_bits):
    planes, groups, parts = lax.axis_size("adp"), lax.axis_size("grp"), lax.axis_size("tp")
    z, g, me = (lax.axis_index(axis).astype(jnp.int32) for axis in ("adp", "grp", "tp"))
    features = tokens.shape[1]
    here, _, rank = adapter_down.shape
    width = adapter_up.shape[2]
    share = here // groups
    split = (features + width) * 5 // 9 // 128 * 128
    matrix = hadamard(sign_bits.shape[0])
    bits, scale, ids = sign_bits[None, :], channel_scale[None, :], adapter_ids.T
    at = jnp.stack([z, g])
    down = jnp.swapaxes(adapter_down, 1, 2)

    own = packed(g[None], down, adapter_up, share)
    mine = [(0, own)]
    theirs = []
    bit = planes // 2
    while bit > 1:
        new = [(plane | bit, swap(piece, "adp", bit)) for plane, piece in mine]
        theirs += [(plane, off, swap(piece, "grp", off)) for plane, piece in new for off in range(1, groups)]
        mine += new
        bit //= 2
    new = [(plane | 1, swap(piece, "adp", 1)) for plane, piece in mine[:-1]]
    theirs += [(plane, off, swap(piece, "grp", off)) for plane, piece in new for off in range(1, groups)]
    last, piece = mine[-1]
    mine += new
    first = swap(piece[:, :, :split], "adp", 1)
    others = [p for plane, _, p in theirs if plane == last]
    if last == 0:
        others = [packed((g ^ off)[None], down, adapter_up, share) for off in range(1, groups)]
    rest = swap(jnp.concatenate([p[:, :, split:] for p in [piece] + others], axis=0), "adp", 1)
    firsts = [first] + [swap(first, "grp", off) for off in range(1, groups)]

    give, keep = partials(me[None], tokens, base_weight, parts)
    came = [swap(give, "tp", 1)]
    bit = 2
    while bit < parts:
        came.append(swap(sum_blocks(keep, came), "tp", bit))
        bit *= 2
    base = rotated_base([keep] + came, scale, bits, matrix)

    def terms(pieces, start):
        return [(start + i, k, 0, (plane, off, k)) for i, (plane, off, _) in enumerate(pieces) for k in range(share)]

    whole = (0, features)
    early = [(plane, 0, p) for plane, p in mine[1:]]
    home = [(0, k, 0, (0, 0, k)) for k in range(here)]
    first_call = [(whole, [(i, k, cut, ("home", k)) for i, k, cut, _ in home] + terms(early, 1))]
    low = low_rows(at, ids, tokens, here, share, first_call, [down] + [p for *_, p in early], None, F32)
    second = [(whole, terms(theirs, 0)), ((0, split), terms([(last | 1, 0, first)], len(theirs)))]
    low = low_rows(at, ids, tokens, here, share, second, [p for *_, p in theirs] + [first], low, F32)
    swapped = [(last | 1, off, p) for off, p in enumerate(firsts) if off]
    ends = [(len(swapped), off * share + k, 0, (last | 1, off, k)) for off in range(groups) for k in range(share)]
    third = [((0, split), terms(swapped, 0)), ((split, features), ends)]
    low = low_rows(at, ids, tokens, here, share, third, [p for *_, p in swapped] + [rest], low, BF16)
    bit = 1
    while bit < parts // 2:
        low = (low.astype(F32) + swap(low, "tp", bit).astype(F32)).astype(BF16)
        bit *= 2
    other = swap(low, "tp", bit)

    full = early + theirs
    every = [(0, k, 0, ("home", k)) for k in range(here)]
    every += [(1 + i, k, features, (plane, off, k)) for i, (plane, off, _) in enumerate(full) for k in range(share)]
    every += [(1 + len(full), i, features - split, name) for _, i, _, name in ends]
    up, mask = rotated_ups(
        at, ids, bits, matrix, here, share, every, [adapter_up] + [p for *_, p in full] + [rest], width
    )
    return final(low, other, base, up, mask)


def solution(mesh):
    return jax.shard_map(
        local,
        mesh=mesh,
        in_specs=(
            P(("grp", "adp"), "tp"),
            P(("grp", "adp"), None),
            P("tp", None),
            P("tp"),
            P("adp", "tp", None),
            P("adp", None, "tp"),
            P(),
        ),
        out_specs=P(("grp", "adp"), "tp"),
        check_vma=False,
    )
```

```python
import functools

import jax
import jax.numpy as jnp
import numpy as np
from jax import lax
from jax.experimental import pallas as pl
from jax.experimental.pallas import tpu as pltpu
from jax.sharding import PartitionSpec as P

VMEM = pl.BlockSpec(memory_space=pltpu.VMEM)
SMEM = pl.BlockSpec(memory_space=pltpu.SMEM)
F32, BF16 = jnp.float32, jnp.bfloat16
LAST = (((1,), (1,)), ((), ()))


def params(mib):
    return pltpu.CompilerParams(vmem_limit_bytes=mib << 20)


COST = pl.CostEstimate(flops=1, bytes_accessed=1, transcendentals=0)


def hadamard(size):
    index = np.arange(size)
    shared = index[:, None] & index[None, :]
    parity = np.zeros_like(shared)
    while shared.any():
        parity, shared = parity ^ (shared & 1), shared >> 1
    return jnp.asarray(1 - 2 * parity, BF16)


def swap(x, axis, bit):
    return lax.ppermute(x, axis, [(i, i ^ bit) for i in range(lax.axis_size(axis))])


def after(value, *others):
    return lax.optimization_barrier((value, *others))[0]


def rotate(value, signs, matrix):
    head = matrix.shape[0]
    scale = signs * (1.0 / np.sqrt(head))
    turned = []
    for at in range(0, value.shape[1], head):
        signed = value[:, at : at + head] * scale
        high = signed.astype(BF16)
        rest = (signed - high.astype(F32)).astype(BF16)
        turned.append(
            jnp.dot(high, matrix, preferred_element_type=F32) + jnp.dot(rest, matrix, preferred_element_type=F32)
        )
    return turned


def block(ref, index, width):
    return ref[:, pl.ds(pl.multiple_of(index * width, width), width)].astype(F32)


def add_kernel(stage, parts, me_ref, part_ref, pair_ref, *refs):
    out_ref = refs[-1]
    width = part_ref.shape[1] // parts
    for j in range(out_ref.shape[1] // width):
        offset = (2 * j + 1) << stage
        owner = jnp.bitwise_xor(me_ref[0], offset)
        total = block(part_ref, owner, width) + block(pair_ref, owner, width)
        for r, ref in enumerate(refs[:-1], 1):
            total = total + block(ref, offset >> (r + 1), width)
        out_ref[:, j * width : (j + 1) * width] = total.astype(BF16)


def sum_blocks(me, part, pair, came, parts):
    rows, columns = part.shape
    stage = 1 + len(came)
    return pl.pallas_call(
        functools.partial(add_kernel, stage, parts),
        in_specs=[SMEM] + [VMEM] * (2 + len(came)),
        out_specs=VMEM,
        out_shape=jax.ShapeDtypeStruct((rows, columns >> (stage + 1)), BF16),
        compiler_params=params(16),
        cost_estimate=COST,
        name="sum_blocks",
    )(me, part, pair, *came)


def base_kernel(parts, me_ref, part_ref, pair_ref, scale_ref, bits_ref, matrix_ref, *refs):
    out_ref = refs[-1]
    width = out_ref.shape[1]
    total = block(part_ref, me_ref[0], width) + block(pair_ref, me_ref[0], width)
    for ref in refs[:-1]:
        total = total + ref[:, :width].astype(F32)
    signs = (1 - 2 * bits_ref[...]).astype(F32)
    out_ref[...] = jnp.concatenate(rotate(total * scale_ref[...], signs, matrix_ref[...]), axis=1)


def rotated_base(me, part, pair, came, scale, bits, matrix, parts):
    rows, columns = part.shape
    return pl.pallas_call(
        functools.partial(base_kernel, parts),
        in_specs=[SMEM] + [VMEM] * (5 + len(came)),
        out_specs=VMEM,
        out_shape=jax.ShapeDtypeStruct((rows, columns // parts), F32),
        compiler_params=params(16),
        cost_estimate=COST,
        name="rotated_base",
    )(me, part, pair, scale, bits, matrix, *came)


def adapter(at_ref, here, share, name):
    if name[0] == "home":
        return at_ref[0] * here + name[1]
    if name[0] == "plane":
        return jnp.bitwise_xor(at_ref[0], name[1]) * here + name[2]
    plane, off, k = name
    return jnp.bitwise_xor(at_ref[0], plane) * here + jnp.bitwise_xor(at_ref[1], off) * share + k


def low_kernel(groups, here, share, rank, more, at_ref, ids_ref, tokens_ref, *refs):
    out_ref = refs[-1]
    total = refs[-2][...] if more else None
    for (start, stop), terms in groups:
        rows = [refs[i][k, :, cut : cut + stop - start] for i, k, cut, _ in terms]
        joined = rows[0] if len(rows) == 1 else jnp.concatenate(rows, axis=0)
        product = lax.dot_general(joined, tokens_ref[:, start:stop], LAST, preferred_element_type=F32)
        for n, (_, _, _, name) in enumerate(terms):
            mine = ids_ref[...] == adapter(at_ref, here, share, name)
            term = jnp.where(mine, product[n * rank : (n + 1) * rank], 0.0)
            total = term if total is None else total + term
    out_ref[...] = total.astype(out_ref.dtype)


def low_rows(at, ids, tokens, here, share, groups, arrays, before, dtype):
    rank = arrays[0].shape[1]
    more = [] if before is None else [before]
    return pl.pallas_call(
        functools.partial(low_kernel, groups, here, share, rank, bool(more)),
        in_specs=[SMEM] + [VMEM] * (2 + len(arrays) + len(more)),
        out_specs=VMEM,
        out_shape=jax.ShapeDtypeStruct((rank, tokens.shape[0]), dtype),
        compiler_params=params(24),
        cost_estimate=COST,
        name="low_rows",
    )(at, ids, tokens, *arrays, *more)


def ups_kernel(terms, here, share, rank, at_ref, ids_ref, bits_ref, matrix_ref, *refs):
    up_ref, mask_ref = refs[-2:]
    width = up_ref.shape[1]
    signs = (1 - 2 * bits_ref[...]).astype(F32)
    ids = jnp.broadcast_to(ids_ref[...], (rank, ids_ref.shape[1])).T
    for n, (i, k, cut, name) in enumerate(terms):
        turned = rotate(refs[i][k, :, cut : cut + width].astype(F32), signs, matrix_ref[...])
        up_ref[n * rank : (n + 1) * rank, :] = jnp.concatenate(turned, axis=1).astype(BF16)
        mine = ids == adapter(at_ref, here, share, name)
        mask_ref[:, n * rank : (n + 1) * rank] = jnp.where(mine, 1.0, 0.0).astype(BF16)


def rotated_ups(at, ids, bits, matrix, here, share, terms, arrays, width):
    rank, rows = arrays[0].shape[1], ids.shape[1]
    every = len(terms) * rank
    return pl.pallas_call(
        functools.partial(ups_kernel, terms, here, share, rank),
        in_specs=[SMEM] + [VMEM] * (3 + len(arrays)),
        out_specs=[VMEM, VMEM],
        out_shape=[jax.ShapeDtypeStruct((every, width), BF16), jax.ShapeDtypeStruct((rows, every), BF16)],
        compiler_params=params(32),
        cost_estimate=COST,
        name="rotated_ups",
    )(at, ids, bits, matrix, *arrays)


def final_kernel(mine_ref, theirs_ref, base_ref, up_ref, mask_ref, out_ref):
    low = (mine_ref[...].astype(F32) + theirs_ref[...].astype(F32)).T.astype(BF16)
    every = mask_ref.shape[1]
    spread = jnp.concatenate([low] * (every // low.shape[1]), axis=1) * mask_ref[...]
    delta = jnp.dot(spread, up_ref[...], preferred_element_type=F32)
    out_ref[...] = (base_ref[...] + delta).astype(BF16)


def final(mine, theirs, base, up, mask):
    rows, width = base.shape
    return pl.pallas_call(
        final_kernel,
        in_specs=[VMEM] * 5,
        out_specs=VMEM,
        out_shape=jax.ShapeDtypeStruct((rows, width), BF16),
        compiler_params=params(32),
        cost_estimate=COST,
        name="final",
    )(mine, theirs, base, up, mask)


def local(tokens, adapter_ids, base_weight, channel_scale, adapter_down, adapter_up, sign_bits):
    planes, groups, parts = lax.axis_size("adp"), lax.axis_size("grp"), lax.axis_size("tp")
    z, g, me = (lax.axis_index(axis).astype(jnp.int32) for axis in ("adp", "grp", "tp"))
    features = tokens.shape[1]
    here, _, rank = adapter_down.shape
    width = adapter_up.shape[2]
    share = here // groups
    matrix = hadamard(sign_bits.shape[0])
    bits, scale, ids, me = sign_bits[None, :], channel_scale[None, :], adapter_ids.T, me[None]
    at = jnp.stack([z, g])
    down = jnp.swapaxes(adapter_down, 1, 2)

    own = lax.dynamic_slice_in_dim(down, g * share, share, 0)
    part = jnp.dot(tokens, base_weight, preferred_element_type=F32).astype(BF16)
    pair = swap(part, "tp", 1)
    near = swap(own, "adp", 1)
    mine = [(0, own)]
    bit = planes // 2
    while bit > 1:
        mine += [(plane | bit, swap(piece, "adp", bit)) for plane, piece in mine]
        bit //= 2
    came = []
    pair = after(pair, near)
    bit = 2
    while bit < parts:
        came.append(swap(sum_blocks(me, part, pair, came, parts), "tp", bit))
        bit *= 2
    mine = mine[:1] + [(plane, after(piece, pair)) for plane, piece in mine[1:]]
    odd = [(1, after(near, part))] + [(plane | 1, swap(piece, "adp", 1)) for plane, piece in mine[1:]]

    def others(pieces):
        return [(plane, off, swap(piece, "grp", off)) for plane, piece in pieces for off in range(1, groups)]

    swapped = others(odd[:1]) + others(mine[1:]) + others(odd[1:])
    held = [(plane, 0, piece) for plane, piece in odd[:1] + mine[1:] + odd[1:]]

    ups = [(0, adapter_up)]
    bit = planes // 2
    while bit:
        ups += [(plane | bit, swap(after(up, mine[-1][1]), "adp", bit)) for plane, up in ups]
        bit //= 2

    base = rotated_base(me, part, pair, came, scale, bits, matrix, parts)

    def terms(pieces, start):
        return [(start + i, k, 0, (plane, off, k)) for i, (plane, off, _) in enumerate(pieces) for k in range(share)]

    whole = (0, features)
    early = held[: len(mine)] + swapped[:1]
    middle = held[len(mine) :] + swapped[1:-1]
    late = swapped[-1:]
    home = [(0, k, 0, ("home", k)) for k in range(here)]
    low = low_rows(at, ids, tokens, here, share, [(whole, home + terms(early, 1))], [down] + [p for *_, p in early], None, F32)
    low = low_rows(at, ids, tokens, here, share, [(whole, terms(middle, 0))], [p for *_, p in middle], low, F32)
    low = after(low, base)
    low = low_rows(at, ids, tokens, here, share, [(whole, terms(late, 0))], [p for *_, p in late], low, BF16)
    bit = 1
    while bit < parts // 2:
        low = (low.astype(F32) + swap(low, "tp", bit).astype(F32)).astype(BF16)
        bit *= 2
    other = swap(low, "tp", bit)

    every = [(i, k, 0, ("plane", plane, k)) for i, (plane, _) in enumerate(ups) for k in range(here)]
    up, mask = rotated_ups(at, ids, bits, matrix, here, share, every, [up for _, up in ups], width)
    return final(low, other, base, up, mask)


def solution(mesh):
    return jax.shard_map(
        local,
        mesh=mesh,
        in_specs=(
            P(("grp", "adp"), "tp"),
            P(("grp", "adp"), None),
            P("tp", None),
            P("tp"),
            P("adp", "tp", None),
            P("adp", None, "tp"),
            P(),
        ),
        out_specs=P(("grp", "adp"), "tp"),
        check_vma=False,
    )
```

```python
import functools

import jax
import jax.numpy as jnp
import numpy as np
from jax import lax
from jax.experimental import pallas as pl
from jax.experimental.pallas import tpu as pltpu
from jax.sharding import PartitionSpec as P

VMEM = pl.BlockSpec(memory_space=pltpu.VMEM)
SMEM = pl.BlockSpec(memory_space=pltpu.SMEM)
F32, BF16 = jnp.float32, jnp.bfloat16
LAST = (((1,), (1,)), ((), ()))


def params(mib):
    return pltpu.CompilerParams(vmem_limit_bytes=mib << 20)


COST = pl.CostEstimate(flops=1, bytes_accessed=1, transcendentals=0)


def hadamard(size):
    index = np.arange(size)
    shared = index[:, None] & index[None, :]
    parity = np.zeros_like(shared)
    while shared.any():
        parity, shared = parity ^ (shared & 1), shared >> 1
    return jnp.asarray(1 - 2 * parity, BF16)


def swap(x, axis, bit):
    return lax.ppermute(x, axis, [(i, i ^ bit) for i in range(lax.axis_size(axis))])


def after(value, *others):
    return lax.optimization_barrier((value, *others))[0]


def rotate(value, signs, matrix):
    head = matrix.shape[0]
    scale = signs * (1.0 / np.sqrt(head))
    turned = []
    for at in range(0, value.shape[1], head):
        signed = value[:, at : at + head] * scale
        high = signed.astype(BF16)
        rest = (signed - high.astype(F32)).astype(BF16)
        turned.append(
            jnp.dot(high, matrix, preferred_element_type=F32) + jnp.dot(rest, matrix, preferred_element_type=F32)
        )
    return turned


def partial_kernel(me_ref, tokens_ref, weight_ref, *outs):
    width = outs[0].shape[1]
    for n, out_ref in enumerate(outs):
        offset = (2 * n + 1) % len(outs) if n < len(outs) // 2 else 2 * n - len(outs)
        at = pl.multiple_of(jnp.bitwise_xor(me_ref[0], offset) * width, width)
        product = jnp.dot(tokens_ref[...], weight_ref[:, pl.ds(at, width)], preferred_element_type=F32)
        out_ref[...] = product.astype(BF16)


def partials(me, tokens, weight, parts):
    block = jax.ShapeDtypeStruct((tokens.shape[0], weight.shape[1] // parts), BF16)
    return pl.pallas_call(
        partial_kernel,
        in_specs=[SMEM, VMEM, VMEM],
        out_specs=[VMEM] * parts,
        out_shape=[block] * parts,
        compiler_params=params(24),
        cost_estimate=COST,
        name="partials",
    )(me, tokens, weight)


def add_kernel(*refs):
    total = refs[0][...].astype(F32)
    for ref in refs[1:-1]:
        total = total + ref[...].astype(F32)
    refs[-1][...] = total.astype(BF16)


def add(*terms):
    return pl.pallas_call(
        add_kernel,
        in_specs=[VMEM] * len(terms),
        out_specs=VMEM,
        out_shape=jax.ShapeDtypeStruct(terms[0].shape, BF16),
        compiler_params=params(16),
        cost_estimate=COST,
        name="add",
    )(*terms)


def base_kernel(scale_ref, bits_ref, matrix_ref, *refs):
    total = refs[0][...].astype(F32)
    for ref in refs[1:-1]:
        total = total + ref[...].astype(F32)
    signs = (1 - 2 * bits_ref[...]).astype(F32)
    refs[-1][...] = jnp.concatenate(rotate(total * scale_ref[...], signs, matrix_ref[...]), axis=1)


def rotated_base(terms, scale, bits, matrix):
    return pl.pallas_call(
        base_kernel,
        in_specs=[VMEM] * (3 + len(terms)),
        out_specs=VMEM,
        out_shape=jax.ShapeDtypeStruct(terms[0].shape, F32),
        compiler_params=params(16),
        cost_estimate=COST,
        name="rotated_base",
    )(scale, bits, matrix, *terms)


def adapter(at_ref, here, share, name):
    if name[0] == "home":
        return at_ref[0] * here + name[1]
    if name[0] == "plane":
        return jnp.bitwise_xor(at_ref[0], name[1]) * here + name[2]
    plane, off, k = name
    return jnp.bitwise_xor(at_ref[0], plane) * here + jnp.bitwise_xor(at_ref[1], off) * share + k


def low_kernel(groups, here, share, rank, more, at_ref, ids_ref, tokens_ref, *refs):
    out_ref = refs[-1]
    total = refs[-2][...] if more else None
    for (start, stop), terms in groups:
        rows = [refs[i][k, :, cut : cut + stop - start] for i, k, cut, _ in terms]
        joined = rows[0] if len(rows) == 1 else jnp.concatenate(rows, axis=0)
        product = lax.dot_general(joined, tokens_ref[:, start:stop], LAST, preferred_element_type=F32)
        for n, (_, _, _, name) in enumerate(terms):
            mine = ids_ref[...] == adapter(at_ref, here, share, name)
            term = jnp.where(mine, product[n * rank : (n + 1) * rank], 0.0)
            total = term if total is None else total + term
    out_ref[...] = total.astype(out_ref.dtype)


def low_rows(at, ids, tokens, here, share, groups, arrays, before, dtype):
    rank = arrays[0].shape[1]
    more = [] if before is None else [before]
    return pl.pallas_call(
        functools.partial(low_kernel, groups, here, share, rank, bool(more)),
        in_specs=[SMEM] + [VMEM] * (2 + len(arrays) + len(more)),
        out_specs=VMEM,
        out_shape=jax.ShapeDtypeStruct((rank, tokens.shape[0]), dtype),
        compiler_params=params(24),
        cost_estimate=COST,
        name="low_rows",
    )(at, ids, tokens, *arrays, *more)


def ups_kernel(terms, here, share, rank, at_ref, ids_ref, bits_ref, matrix_ref, *refs):
    up_ref, mask_ref = refs[-2:]
    width = up_ref.shape[1]
    signs = (1 - 2 * bits_ref[...]).astype(F32)
    ids = jnp.broadcast_to(ids_ref[...], (rank, ids_ref.shape[1])).T
    for n, (i, k, cut, name) in enumerate(terms):
        turned = rotate(refs[i][k, :, cut : cut + width].astype(F32), signs, matrix_ref[...])
        up_ref[n * rank : (n + 1) * rank, :] = jnp.concatenate(turned, axis=1).astype(BF16)
        mine = ids == adapter(at_ref, here, share, name)
        mask_ref[:, n * rank : (n + 1) * rank] = jnp.where(mine, 1.0, 0.0).astype(BF16)


def rotated_ups(at, ids, bits, matrix, here, share, terms, arrays, width):
    rank, rows = arrays[0].shape[1], ids.shape[1]
    every = len(terms) * rank
    return pl.pallas_call(
        functools.partial(ups_kernel, terms, here, share, rank),
        in_specs=[SMEM] + [VMEM] * (3 + len(arrays)),
        out_specs=[VMEM, VMEM],
        out_shape=[jax.ShapeDtypeStruct((every, width), BF16), jax.ShapeDtypeStruct((rows, every), BF16)],
        compiler_params=params(32),
        cost_estimate=COST,
        name="rotated_ups",
    )(at, ids, bits, matrix, *arrays)


def final_kernel(mine_ref, theirs_ref, base_ref, up_ref, mask_ref, out_ref):
    low = (mine_ref[...].astype(F32) + theirs_ref[...].astype(F32)).T.astype(BF16)
    every = mask_ref.shape[1]
    spread = jnp.concatenate([low] * (every // low.shape[1]), axis=1) * mask_ref[...]
    delta = jnp.dot(spread, up_ref[...], preferred_element_type=F32)
    out_ref[...] = (base_ref[...] + delta).astype(BF16)


def final(mine, theirs, base, up, mask):
    rows, width = base.shape
    return pl.pallas_call(
        final_kernel,
        in_specs=[VMEM] * 5,
        out_specs=VMEM,
        out_shape=jax.ShapeDtypeStruct((rows, width), BF16),
        compiler_params=params(32),
        cost_estimate=COST,
        name="final",
    )(mine, theirs, base, up, mask)


def local(tokens, adapter_ids, base_weight, channel_scale, adapter_down, adapter_up, sign_bits):
    planes, groups, parts = lax.axis_size("adp"), lax.axis_size("grp"), lax.axis_size("tp")
    z, g, me = (lax.axis_index(axis).astype(jnp.int32) for axis in ("adp", "grp", "tp"))
    features = tokens.shape[1]
    here, _, rank = adapter_down.shape
    width = adapter_up.shape[2]
    share = here // groups
    matrix = hadamard(sign_bits.shape[0])
    bits, scale, ids, me = sign_bits[None, :], channel_scale[None, :], adapter_ids.T, me[None]
    at = jnp.stack([z, g])
    down = jnp.swapaxes(adapter_down, 1, 2)

    own = lax.dynamic_slice_in_dim(down, g * share, share, 0)
    near = swap(own, "adp", 1)
    mine = [(0, own)]
    bit = planes // 2
    while bit > 1:
        mine += [(plane | bit, swap(piece, "adp", bit)) for plane, piece in mine]
        bit //= 2
    blocks = partials(me, tokens, base_weight, parts)
    half = parts // 2
    near = after(near, *blocks)
    mine = mine[:1] + [(plane, after(piece, near)) for plane, piece in mine[1:]]
    odd = [(1, near)] + [(plane | 1, swap(piece, "adp", 1)) for plane, piece in mine[1:]]

    def others(pieces):
        return [(plane, off, swap(piece, "grp", off)) for plane, piece in pieces for off in range(1, groups)]

    swapped = others(odd[:1]) + others(mine[1:]) + others(odd[1:])
    held = [(plane, 0, piece) for plane, piece in odd[:1] + mine[1:] + odd[1:]]

    last = mine[-1][1]
    came = [swap(block, "tp", 1) for block in blocks[:half]]
    sums = [[block, after(pair, last)] for block, pair in zip(blocks[half:], came)]
    bit = 2
    while bit < parts:
        came = [swap(add(*terms), "tp", bit) for terms in sums[1::2]]
        sums = [terms + [pair] for terms, pair in zip(sums[0::2], came)]
        bit *= 2
    base = rotated_base(sums[0], scale, bits, matrix)

    ups = [(0, after(adapter_up, held[-1][2]))]
    bit = planes // 2
    while bit:
        ups += [(plane | bit, swap(up, "adp", bit)) for plane, up in ups]
        bit //= 2
    every = [(i, k, 0, ("plane", plane, k)) for i, (plane, _) in enumerate(ups) for k in range(here)]
    up, mask = rotated_ups(at, ids, bits, matrix, here, share, every, [up for _, up in ups], width)

    def terms(pieces, start):
        return [(start + i, k, 0, (plane, off, k)) for i, (plane, off, _) in enumerate(pieces) for k in range(share)]

    whole = (0, features)
    early = held[: len(mine)]
    middle = held[len(mine) :] + swapped[:-1]
    late = swapped[-1:]
    home = [(0, k, 0, ("home", k)) for k in range(here)]
    low = low_rows(at, ids, tokens, here, share, [(whole, home + terms(early, 1))], [down] + [p for *_, p in early], None, F32)
    low = low_rows(at, ids, tokens, here, share, [(whole, terms(middle, 0))], [p for *_, p in middle], low, F32)
    low = after(low, base, up)
    low = low_rows(at, ids, tokens, here, share, [(whole, terms(late, 0))], [p for *_, p in late], low, BF16)
    bit = 1
    while bit < parts // 2:
        low = (low.astype(F32) + swap(low, "tp", bit).astype(F32)).astype(BF16)
        bit *= 2
    other = swap(low, "tp", bit)

    return final(low, other, base, up, mask)


def solution(mesh):
    return jax.shard_map(
        local,
        mesh=mesh,
        in_specs=(
            P(("grp", "adp"), "tp"),
            P(("grp", "adp"), None),
            P("tp", None),
            P("tp"),
            P("adp", "tp", None),
            P("adp", None, "tp"),
            P(),
        ),
        out_specs=P(("grp", "adp"), "tp"),
        check_vma=False,
    )
```

```python
import functools

import jax
import jax.numpy as jnp
import numpy as np
from jax import lax
from jax.experimental import pallas as pl
from jax.experimental.pallas import tpu as pltpu
from jax.sharding import PartitionSpec as P

VMEM = pl.BlockSpec(memory_space=pltpu.VMEM)
SMEM = pl.BlockSpec(memory_space=pltpu.SMEM)
F32, BF16 = jnp.float32, jnp.bfloat16
LAST = (((1,), (1,)), ((), ()))


def params(mib):
    return pltpu.CompilerParams(vmem_limit_bytes=mib << 20)


COST = pl.CostEstimate(flops=1, bytes_accessed=1, transcendentals=0)


def hadamard(size):
    index = np.arange(size)
    shared = index[:, None] & index[None, :]
    parity = np.zeros_like(shared)
    while shared.any():
        parity, shared = parity ^ (shared & 1), shared >> 1
    return jnp.asarray(1 - 2 * parity, BF16)


def swap(x, axis, bit):
    return lax.ppermute(x, axis, [(i, i ^ bit) for i in range(lax.axis_size(axis))])


def together(*values):
    return lax.optimization_barrier(values)


def rotate(value, signs, matrix):
    head = matrix.shape[0]
    scale = signs * (1.0 / np.sqrt(head))
    turned = []
    for at in range(0, value.shape[1], head):
        signed = value[:, at : at + head] * scale
        high = signed.astype(BF16)
        rest = (signed - high.astype(F32)).astype(BF16)
        turned.append(
            jnp.dot(high, matrix, preferred_element_type=F32) + jnp.dot(rest, matrix, preferred_element_type=F32)
        )
    return turned


def partial_kernel(tokens_ref, weight_ref, sign_ref, *outs):
    me, width = lax.axis_index("tp"), outs[0].shape[1]
    sign_ref[...] = jnp.zeros_like(sign_ref)
    for n, out_ref in enumerate(outs):
        offset = (2 * n + 1) % len(outs) if n < len(outs) // 2 else 2 * n - len(outs)
        at = pl.multiple_of(jnp.bitwise_xor(me, offset) * width, width)
        product = jnp.dot(tokens_ref[...], weight_ref[:, pl.ds(at, width)], preferred_element_type=F32)
        out_ref[...] = product.astype(BF16)


def partials(tokens, weight, parts):
    block = jax.ShapeDtypeStruct((tokens.shape[0], weight.shape[1] // parts), BF16)
    return pl.pallas_call(
        partial_kernel,
        in_specs=[VMEM, VMEM],
        out_specs=[VMEM] * (1 + parts),
        out_shape=[jax.ShapeDtypeStruct((8, 128), F32)] + [block] * parts,
        compiler_params=params(24),
        cost_estimate=COST,
        name="partials",
    )(tokens, weight)


def add_kernel(*refs):
    total = refs[0][...].astype(F32)
    for ref in refs[1:-1]:
        total = total + ref[...].astype(F32)
    refs[-1][...] = total.astype(BF16)


def add(*terms):
    return pl.pallas_call(
        add_kernel,
        in_specs=[VMEM] * len(terms),
        out_specs=VMEM,
        out_shape=jax.ShapeDtypeStruct(terms[0].shape, BF16),
        compiler_params=params(16),
        cost_estimate=COST,
        name="add",
    )(*terms)


def base_kernel(scale_ref, bits_ref, matrix_ref, *refs):
    total = refs[0][...].astype(F32)
    for ref in refs[1:-1]:
        total = total + ref[...].astype(F32)
    signs = (1 - 2 * bits_ref[...]).astype(F32)
    refs[-1][...] = jnp.concatenate(rotate(total * scale_ref[...], signs, matrix_ref[...]), axis=1)


def rotated_base(terms, scale, bits, matrix):
    return pl.pallas_call(
        base_kernel,
        in_specs=[VMEM] * (3 + len(terms)),
        out_specs=VMEM,
        out_shape=jax.ShapeDtypeStruct(terms[0].shape, F32),
        compiler_params=params(16),
        cost_estimate=COST,
        name="rotated_base",
    )(scale, bits, matrix, *terms)


def adapter(here, share, name):
    z = lax.axis_index("adp")
    if name[0] == "plane":
        return jnp.bitwise_xor(z, name[1]) * here + name[2]
    plane, off, k = name
    return jnp.bitwise_xor(z, plane) * here + jnp.bitwise_xor(lax.axis_index("grp"), off) * share + k


def low_kernel(groups, here, share, rank, more, ids_ref, tokens_ref, *refs):
    out_ref = refs[-1]
    total = refs[-2][...] if more else None
    for (start, stop), terms in groups:
        rows = [refs[i][k, :, cut : cut + stop - start] for i, k, cut, _ in terms]
        joined = rows[0] if len(rows) == 1 else jnp.concatenate(rows, axis=0)
        product = lax.dot_general(joined, tokens_ref[:, start:stop], LAST, preferred_element_type=F32)
        for n, (_, _, _, name) in enumerate(terms):
            mine = ids_ref[...] == adapter(here, share, name)
            term = jnp.where(mine, product[n * rank : (n + 1) * rank], 0.0)
            total = term if total is None else total + term
    out_ref[...] = total.astype(out_ref.dtype)


def low_rows(ids, tokens, here, share, groups, arrays, before, dtype):
    rank = arrays[0].shape[1]
    more = [] if before is None else [before]
    return pl.pallas_call(
        functools.partial(low_kernel, groups, here, share, rank, bool(more)),
        in_specs=[VMEM] * (2 + len(arrays) + len(more)),
        out_specs=VMEM,
        out_shape=jax.ShapeDtypeStruct((rank, tokens.shape[0]), dtype),
        compiler_params=params(24),
        cost_estimate=COST,
        name="low_rows",
    )(ids, tokens, *arrays, *more)


def ups_kernel(terms, here, share, rank, ids_ref, bits_ref, matrix_ref, *refs):
    up_ref, mask_ref = refs[-2:]
    width = up_ref.shape[1]
    signs = (1 - 2 * bits_ref[...]).astype(F32)
    ids = jnp.broadcast_to(ids_ref[...], (rank, ids_ref.shape[1])).T
    for n, (i, k, cut, name) in enumerate(terms):
        turned = rotate(refs[i][k, :, cut : cut + width].astype(F32), signs, matrix_ref[...])
        up_ref[n * rank : (n + 1) * rank, :] = jnp.concatenate(turned, axis=1).astype(BF16)
        mine = ids == adapter(here, share, name)
        mask_ref[:, n * rank : (n + 1) * rank] = jnp.where(mine, 1.0, 0.0).astype(BF16)


def rotated_ups(ids, bits, matrix, here, share, terms, arrays, width):
    rank, rows = arrays[0].shape[1], ids.shape[1]
    every = len(terms) * rank
    return pl.pallas_call(
        functools.partial(ups_kernel, terms, here, share, rank),
        in_specs=[VMEM] * (3 + len(arrays)),
        out_specs=[VMEM, VMEM],
        out_shape=[jax.ShapeDtypeStruct((every, width), BF16), jax.ShapeDtypeStruct((rows, every), BF16)],
        compiler_params=params(32),
        cost_estimate=COST,
        name="rotated_ups",
    )(ids, bits, matrix, *arrays)


def final_kernel(mine_ref, theirs_ref, base_ref, up_ref, mask_ref, out_ref):
    low = (mine_ref[...].astype(F32) + theirs_ref[...].astype(F32)).T.astype(BF16)
    every = mask_ref.shape[1]
    spread = jnp.concatenate([low] * (every // low.shape[1]), axis=1) * mask_ref[...]
    delta = jnp.dot(spread, up_ref[...], preferred_element_type=F32)
    out_ref[...] = (base_ref[...] + delta).astype(BF16)


def final(mine, theirs, base, up, mask):
    rows, width = base.shape
    return pl.pallas_call(
        final_kernel,
        in_specs=[VMEM] * 5,
        out_specs=VMEM,
        out_shape=jax.ShapeDtypeStruct((rows, width), BF16),
        compiler_params=params(32),
        cost_estimate=COST,
        name="final",
    )(mine, theirs, base, up, mask)


def local(tokens, adapter_ids, base_weight, channel_scale, adapter_down, adapter_up, sign_bits):
    planes, groups, parts = lax.axis_size("adp"), lax.axis_size("grp"), lax.axis_size("tp")
    features = tokens.shape[1]
    here, _, rank = adapter_down.shape
    width = adapter_up.shape[2]
    share = here // groups
    matrix = hadamard(sign_bits.shape[0])
    bits, scale, ids = sign_bits[None, :], channel_scale[None, :], adapter_ids.T
    down = jnp.swapaxes(adapter_down, 1, 2)

    own = lax.dynamic_slice_in_dim(down, lax.axis_index("grp") * share, share, 0)
    near = swap(own, "adp", 1)
    mine = [(0, own)]
    bit = planes // 2
    while bit > 1:
        mine += [(plane | bit, swap(piece, "adp", bit)) for plane, piece in mine]
        bit //= 2
    sign, *blocks = partials(tokens, base_weight, parts)
    half = parts // 2
    near, _, *far = together(near, sign, *(piece for _, piece in mine[1:]))
    mine = mine[:1] + [(plane, piece) for (plane, _), piece in zip(mine[1:], far)]
    odd = [(1, near)] + [(plane | 1, swap(piece, "adp", 1)) for plane, piece in mine[1:]]

    def others(pieces):
        return [(plane, off, swap(piece, "grp", off)) for plane, piece in pieces for off in range(1, groups)]

    swapped = others(odd[:1]) + others(mine[1:]) + others(odd[1:])
    held = [(plane, 0, piece) for plane, piece in odd[:1] + mine[1:] + odd[1:]]

    plane, off, piece = swapped[0]
    piece, *came = together(piece, *(swap(block, "tp", 1) for block in blocks[:half]))
    swapped[0] = plane, off, piece
    sums = [[block, pair] for block, pair in zip(blocks[half:], came)]
    bit = 2
    while bit < parts:
        came = [swap(add(*terms), "tp", bit) for terms in sums[1::2]]
        sums = [terms + [pair] for terms, pair in zip(sums[0::2], came)]
        bit *= 2
    base = rotated_base(sums[0], scale, bits, matrix)

    plane, off, piece = held[-1]
    piece, up = together(piece, adapter_up)
    held[-1] = plane, off, piece
    ups = [(0, up)]
    bit = planes // 2
    while bit:
        ups += [(plane | bit, swap(up, "adp", bit)) for plane, up in ups]
        bit //= 2
    every = [(i, k, 0, ("plane", plane, k)) for i, (plane, _) in enumerate(ups) for k in range(here)]
    up, mask = rotated_ups(ids, bits, matrix, here, share, every, [up for _, up in ups], width)

    def terms(pieces, start):
        return [(start + i, k, 0, (plane, off, k)) for i, (plane, off, _) in enumerate(pieces) for k in range(share)]

    whole = (0, features)
    early = held[: len(mine)]
    middle = held[len(mine) :] + swapped[:-1]
    late = swapped[-1:]
    home = [(0, k, 0, ("plane", 0, k)) for k in range(here)]
    low = low_rows(ids, tokens, here, share, [(whole, home + terms(early, 1))], [down] + [p for *_, p in early], None, F32)
    low = low_rows(ids, tokens, here, share, [(whole, terms(middle, 0))], [p for *_, p in middle], low, F32)
    low, base, up, mask = together(low, base, up, mask)
    low = low_rows(ids, tokens, here, share, [(whole, terms(late, 0))], [p for *_, p in late], low, BF16)
    bit = 1
    while bit < parts // 2:
        low = add(low, swap(low, "tp", bit))
        bit *= 2
    other = swap(low, "tp", bit)

    return final(low, other, base, up, mask)


def solution(mesh):
    return jax.shard_map(
        local,
        mesh=mesh,
        in_specs=(
            P(("grp", "adp"), "tp"),
            P(("grp", "adp"), None),
            P("tp", None),
            P("tp"),
            P("adp", "tp", None),
            P("adp", None, "tp"),
            P(),
        ),
        out_specs=P(("grp", "adp"), "tp"),
        check_vma=False,
    )
```

```python
import functools

import jax
import jax.numpy as jnp
import numpy as np
from jax import lax
from jax.experimental import pallas as pl
from jax.experimental.pallas import tpu as pltpu
from jax.sharding import PartitionSpec as P

VMEM = pl.BlockSpec(memory_space=pltpu.VMEM)
SMEM = pl.BlockSpec(memory_space=pltpu.SMEM)
F32, BF16 = jnp.float32, jnp.bfloat16
LAST = (((1,), (1,)), ((), ()))


def params(mib):
    return pltpu.CompilerParams(vmem_limit_bytes=mib << 20)


COST = pl.CostEstimate(flops=1, bytes_accessed=1, transcendentals=0)
SOME = pl.CostEstimate(flops=5_000_000_000, bytes_accessed=1, transcendentals=0)


def hadamard(size):
    index = np.arange(size)
    shared = index[:, None] & index[None, :]
    parity = np.zeros_like(shared)
    while shared.any():
        parity, shared = parity ^ (shared & 1), shared >> 1
    return jnp.asarray(1 - 2 * parity, BF16)


def swap(x, axis, bit):
    return lax.ppermute(x, axis, [(i, i ^ bit) for i in range(lax.axis_size(axis))])


def together(*values):
    return lax.optimization_barrier(values)


def rotate(value, signs, matrix):
    head = matrix.shape[0]
    scale = signs * (1.0 / np.sqrt(head))
    turned = []
    for at in range(0, value.shape[1], head):
        signed = value[:, at : at + head] * scale
        high = signed.astype(BF16)
        rest = (signed - high.astype(F32)).astype(BF16)
        turned.append(
            jnp.dot(high, matrix, preferred_element_type=F32) + jnp.dot(rest, matrix, preferred_element_type=F32)
        )
    return turned


def partial_kernel(tokens_ref, weight_ref, sign_ref, *outs):
    me, width = lax.axis_index("tp"), outs[0].shape[1]
    sign_ref[...] = jnp.zeros_like(sign_ref)
    for n, out_ref in enumerate(outs):
        offset = (2 * n + 1) % len(outs) if n < len(outs) // 2 else 2 * n - len(outs)
        at = pl.multiple_of(jnp.bitwise_xor(me, offset) * width, width)
        product = jnp.dot(tokens_ref[...], weight_ref[:, pl.ds(at, width)], preferred_element_type=F32)
        out_ref[...] = product.astype(BF16)


def partials(tokens, weight, parts):
    block = jax.ShapeDtypeStruct((tokens.shape[0], weight.shape[1] // parts), BF16)
    return pl.pallas_call(
        partial_kernel,
        in_specs=[VMEM, VMEM],
        out_specs=[VMEM] * (1 + parts),
        out_shape=[jax.ShapeDtypeStruct((8, 128), F32)] + [block] * parts,
        compiler_params=params(24),
        cost_estimate=COST,
        name="partials",
    )(tokens, weight)


def add_kernel(*refs):
    total = refs[0][...].astype(F32)
    for ref in refs[1:-1]:
        total = total + ref[...].astype(F32)
    refs[-1][...] = total.astype(BF16)


def add(*terms):
    return pl.pallas_call(
        add_kernel,
        in_specs=[VMEM] * len(terms),
        out_specs=VMEM,
        out_shape=jax.ShapeDtypeStruct(terms[0].shape, BF16),
        compiler_params=params(16),
        cost_estimate=COST,
        name="add",
    )(*terms)


def base_kernel(scale_ref, bits_ref, matrix_ref, *refs):
    total = refs[0][...].astype(F32)
    for ref in refs[1:-1]:
        total = total + ref[...].astype(F32)
    signs = (1 - 2 * bits_ref[...]).astype(F32)
    refs[-1][...] = jnp.concatenate(rotate(total * scale_ref[...], signs, matrix_ref[...]), axis=1)


def rotated_base(terms, scale, bits, matrix):
    return pl.pallas_call(
        base_kernel,
        in_specs=[VMEM] * (3 + len(terms)),
        out_specs=VMEM,
        out_shape=jax.ShapeDtypeStruct(terms[0].shape, F32),
        compiler_params=params(16),
        cost_estimate=COST,
        name="rotated_base",
    )(scale, bits, matrix, *terms)


def adapter(here, share, name):
    z = lax.axis_index("adp")
    if name[0] == "plane":
        return jnp.bitwise_xor(z, name[1]) * here + name[2]
    plane, off, k = name
    return jnp.bitwise_xor(z, plane) * here + jnp.bitwise_xor(lax.axis_index("grp"), off) * share + k


def low_kernel(groups, here, share, rank, more, ids_ref, tokens_ref, *refs):
    out_ref = refs[-1]
    total = refs[-2][...] if more else None
    for (start, stop), terms in groups:
        rows = [refs[i][k, :, cut : cut + stop - start] for i, k, cut, _ in terms]
        joined = rows[0] if len(rows) == 1 else jnp.concatenate(rows, axis=0)
        product = lax.dot_general(joined, tokens_ref[:, start:stop], LAST, preferred_element_type=F32)
        for n, (_, _, _, name) in enumerate(terms):
            mine = ids_ref[...] == adapter(here, share, name)
            term = jnp.where(mine, product[n * rank : (n + 1) * rank], 0.0)
            total = term if total is None else total + term
    out_ref[...] = total.astype(out_ref.dtype)


def low_rows(ids, tokens, here, share, groups, arrays, before, dtype, cost=COST):
    rank = arrays[0].shape[1]
    more = [] if before is None else [before]
    return pl.pallas_call(
        functools.partial(low_kernel, groups, here, share, rank, bool(more)),
        in_specs=[VMEM] * (2 + len(arrays) + len(more)),
        out_specs=VMEM,
        out_shape=jax.ShapeDtypeStruct((rank, tokens.shape[0]), dtype),
        compiler_params=params(24),
        cost_estimate=cost,
        name="low_rows",
    )(ids, tokens, *arrays, *more)


def ups_kernel(terms, here, share, rank, ids_ref, bits_ref, matrix_ref, *refs):
    up_ref, mask_ref = refs[-2:]
    width = up_ref.shape[1]
    signs = (1 - 2 * bits_ref[...]).astype(F32)
    ids = jnp.broadcast_to(ids_ref[...], (rank, ids_ref.shape[1])).T
    for n, (i, k, cut, name) in enumerate(terms):
        turned = rotate(refs[i][k, :, cut : cut + width].astype(F32), signs, matrix_ref[...])
        up_ref[n * rank : (n + 1) * rank, :] = jnp.concatenate(turned, axis=1).astype(BF16)
        mine = ids == adapter(here, share, name)
        mask_ref[:, n * rank : (n + 1) * rank] = jnp.where(mine, 1.0, 0.0).astype(BF16)


def rotated_ups(ids, bits, matrix, here, share, terms, arrays, width):
    rank, rows = arrays[0].shape[1], ids.shape[1]
    every = len(terms) * rank
    return pl.pallas_call(
        functools.partial(ups_kernel, terms, here, share, rank),
        in_specs=[VMEM] * (3 + len(arrays)),
        out_specs=[VMEM, VMEM],
        out_shape=[jax.ShapeDtypeStruct((every, width), BF16), jax.ShapeDtypeStruct((rows, every), BF16)],
        compiler_params=params(32),
        cost_estimate=COST,
        name="rotated_ups",
    )(ids, bits, matrix, *arrays)


def final_kernel(mine_ref, theirs_ref, base_ref, up_ref, mask_ref, out_ref):
    low = (mine_ref[...].astype(F32) + theirs_ref[...].astype(F32)).T.astype(BF16)
    every = mask_ref.shape[1]
    spread = jnp.concatenate([low] * (every // low.shape[1]), axis=1) * mask_ref[...]
    delta = jnp.dot(spread, up_ref[...], preferred_element_type=F32)
    out_ref[...] = (base_ref[...] + delta).astype(BF16)


def final(mine, theirs, base, up, mask):
    rows, width = base.shape
    return pl.pallas_call(
        final_kernel,
        in_specs=[VMEM] * 5,
        out_specs=VMEM,
        out_shape=jax.ShapeDtypeStruct((rows, width), BF16),
        compiler_params=params(32),
        cost_estimate=COST,
        name="final",
    )(mine, theirs, base, up, mask)


def local(tokens, adapter_ids, base_weight, channel_scale, adapter_down, adapter_up, sign_bits):
    planes, groups, parts = lax.axis_size("adp"), lax.axis_size("grp"), lax.axis_size("tp")
    features = tokens.shape[1]
    here, _, rank = adapter_down.shape
    width = adapter_up.shape[2]
    share = here // groups
    matrix = hadamard(sign_bits.shape[0])
    bits, scale, ids = sign_bits[None, :], channel_scale[None, :], adapter_ids.T
    down = jnp.swapaxes(adapter_down, 1, 2)

    own = lax.dynamic_slice_in_dim(down, lax.axis_index("grp") * share, share, 0)
    near = swap(own, "adp", 1)
    mine = [(0, own)]
    bit = planes // 2
    while bit > 1:
        mine += [(plane | bit, swap(piece, "adp", bit)) for plane, piece in mine]
        bit //= 2
    sign, *blocks = partials(tokens, base_weight, parts)
    half = parts // 2
    near, _, *far = together(near, sign, *(piece for _, piece in mine[1:]))
    mine = mine[:1] + [(plane, piece) for (plane, _), piece in zip(mine[1:], far)]
    odd = [(1, near)] + [(plane | 1, swap(piece, "adp", 1)) for plane, piece in mine[1:]]

    def others(pieces):
        return [(plane, off, swap(piece, "grp", off)) for plane, piece in pieces for off in range(1, groups)]

    swapped = others(odd[:1]) + others(mine[1:]) + others(odd[1:])
    held = [(plane, 0, piece) for plane, piece in odd[:1] + mine[1:] + odd[1:]]

    def terms(pieces, start):
        return [(start + i, k, 0, (plane, off, k)) for i, (plane, off, _) in enumerate(pieces) for k in range(share)]

    whole = (0, features)
    early = held[: len(mine)]
    middle = held[len(mine) :] + swapped[:-1]
    late = swapped[-1:]
    home = [(0, k, 0, ("plane", 0, k)) for k in range(here)]
    first = [(whole, home + terms(early, 1))]
    low = low_rows(ids, tokens, here, share, first, [down] + [p for *_, p in early], None, F32, SOME)

    low, *came = together(low, *(swap(block, "tp", 1) for block in blocks[:half]))
    sums = [[block, pair] for block, pair in zip(blocks[half:], came)]
    bit = 2
    while bit < parts:
        came = [swap(add(*terms), "tp", bit) for terms in sums[1::2]]
        sums = [terms + [pair] for terms, pair in zip(sums[0::2], came)]
        bit *= 2
    base = rotated_base(sums[0], scale, bits, matrix)

    plane, off, piece = middle[-len(swapped) + 1]
    piece, up = together(piece, adapter_up)
    middle[-len(swapped) + 1] = plane, off, piece
    ups = [(0, up)]
    bit = planes // 2
    while bit:
        ups += [(plane | bit, swap(up, "adp", bit)) for plane, up in ups]
        bit //= 2
    every = [(i, k, 0, ("plane", plane, k)) for i, (plane, _) in enumerate(ups) for k in range(here)]
    up, mask = rotated_ups(ids, bits, matrix, here, share, every, [up for _, up in ups], width)

    low = low_rows(ids, tokens, here, share, [(whole, terms(middle, 0))], [p for *_, p in middle], low, F32)
    low, base, up, mask = together(low, base, up, mask)
    low = low_rows(ids, tokens, here, share, [(whole, terms(late, 0))], [p for *_, p in late], low, BF16)
    bit = 1
    while bit < parts // 2:
        low = add(low, swap(low, "tp", bit))
        bit *= 2
    other = swap(low, "tp", bit)

    return final(low, other, base, up, mask)


def solution(mesh):
    return jax.shard_map(
        local,
        mesh=mesh,
        in_specs=(
            P(("grp", "adp"), "tp"),
            P(("grp", "adp"), None),
            P("tp", None),
            P("tp"),
            P("adp", "tp", None),
            P("adp", None, "tp"),
            P(),
        ),
        out_specs=P(("grp", "adp"), "tp"),
        check_vma=False,
    )
```

```python
import functools

import jax
import jax.numpy as jnp
import numpy as np
from jax import lax
from jax.experimental import pallas as pl
from jax.experimental.pallas import tpu as pltpu
from jax.sharding import PartitionSpec as P

VMEM = pl.BlockSpec(memory_space=pltpu.VMEM)
SMEM = pl.BlockSpec(memory_space=pltpu.SMEM)
F32, BF16 = jnp.float32, jnp.bfloat16
LAST = (((1,), (1,)), ((), ()))


def params(mib):
    return pltpu.CompilerParams(vmem_limit_bytes=mib << 20)


COST = pl.CostEstimate(flops=1, bytes_accessed=1, transcendentals=0)
SOME = pl.CostEstimate(flops=5_000_000_000, bytes_accessed=1, transcendentals=0)


def hadamard(size):
    index = np.arange(size)
    shared = index[:, None] & index[None, :]
    parity = np.zeros_like(shared)
    while shared.any():
        parity, shared = parity ^ (shared & 1), shared >> 1
    return jnp.asarray(1 - 2 * parity, BF16)


def swap(x, axis, bit):
    return lax.ppermute(x, axis, [(i, i ^ bit) for i in range(lax.axis_size(axis))])


def together(*values):
    return lax.optimization_barrier(values)


def rotate(value, signs, matrix):
    head = matrix.shape[0]
    scale = signs * (1.0 / np.sqrt(head))
    turned = []
    for at in range(0, value.shape[1], head):
        signed = value[:, at : at + head] * scale
        high = signed.astype(BF16)
        rest = (signed - high.astype(F32)).astype(BF16)
        turned.append(
            jnp.dot(high, matrix, preferred_element_type=F32) + jnp.dot(rest, matrix, preferred_element_type=F32)
        )
    return turned


def partial_kernel(here, ids_ref, tokens_ref, weight_ref, down_ref, low_ref, *outs):
    me, width = lax.axis_index("tp"), outs[0].shape[1]
    for n, out_ref in enumerate(outs):
        offset = 2 * n + 1 if n < len(outs) // 2 else 2 * n - len(outs)
        at = pl.multiple_of(jnp.bitwise_xor(me, offset) * width, width)
        product = jnp.dot(tokens_ref[...], weight_ref[:, pl.ds(at, width)], preferred_element_type=F32)
        out_ref[...] = product.astype(BF16)
    rank = down_ref.shape[1]
    joined = jnp.concatenate([down_ref[k] for k in range(here)], axis=0)
    product = lax.dot_general(joined, tokens_ref[...], LAST, preferred_element_type=F32)
    terms = [
        jnp.where(ids_ref[...] == adapter(here, 0, ("plane", 0, k)), product[k * rank : (k + 1) * rank], 0.0)
        for k in range(here)
    ]
    low_ref[...] = functools.reduce(jnp.add, terms)


def partials(ids, tokens, weight, down, parts):
    rows, width = tokens.shape[0], weight.shape[1] // parts
    here, rank, _ = down.shape
    return pl.pallas_call(
        functools.partial(partial_kernel, here),
        in_specs=[VMEM] * 4,
        out_specs=[VMEM] * (1 + parts),
        out_shape=[jax.ShapeDtypeStruct((rank, rows), F32)] + [jax.ShapeDtypeStruct((rows, width), BF16)] * parts,
        compiler_params=params(24),
        cost_estimate=COST,
        name="partials",
    )(ids, tokens, weight, down)


def add_kernel(*refs):
    total = refs[0][...].astype(F32)
    for ref in refs[1:-1]:
        total = total + ref[...].astype(F32)
    refs[-1][...] = total.astype(BF16)


def add(*terms):
    return pl.pallas_call(
        add_kernel,
        in_specs=[VMEM] * len(terms),
        out_specs=VMEM,
        out_shape=jax.ShapeDtypeStruct(terms[0].shape, BF16),
        compiler_params=params(16),
        cost_estimate=COST,
        name="add",
    )(*terms)


def base_kernel(scale_ref, bits_ref, matrix_ref, *refs):
    total = refs[0][...].astype(F32)
    for ref in refs[1:-1]:
        total = total + ref[...].astype(F32)
    signs = (1 - 2 * bits_ref[...]).astype(F32)
    refs[-1][...] = jnp.concatenate(rotate(total * scale_ref[...], signs, matrix_ref[...]), axis=1)


def rotated_base(terms, scale, bits, matrix):
    return pl.pallas_call(
        base_kernel,
        in_specs=[VMEM] * (3 + len(terms)),
        out_specs=VMEM,
        out_shape=jax.ShapeDtypeStruct(terms[0].shape, F32),
        compiler_params=params(16),
        cost_estimate=COST,
        name="rotated_base",
    )(scale, bits, matrix, *terms)


def adapter(here, share, name):
    z = lax.axis_index("adp")
    if name[0] == "plane":
        return jnp.bitwise_xor(z, name[1]) * here + name[2]
    plane, off, k = name
    return jnp.bitwise_xor(z, plane) * here + jnp.bitwise_xor(lax.axis_index("grp"), off) * share + k


def low_kernel(groups, here, share, rank, ids_ref, tokens_ref, *refs):
    out_ref = refs[-1]
    total = refs[-2][...]
    for (start, stop), terms in groups:
        rows = [refs[i][k, :, cut : cut + stop - start] for i, k, cut, _ in terms]
        joined = rows[0] if len(rows) == 1 else jnp.concatenate(rows, axis=0)
        product = lax.dot_general(joined, tokens_ref[:, start:stop], LAST, preferred_element_type=F32)
        for n, (_, _, _, name) in enumerate(terms):
            mine = ids_ref[...] == adapter(here, share, name)
            term = jnp.where(mine, product[n * rank : (n + 1) * rank], 0.0)
            total = total + term
    out_ref[...] = total.astype(out_ref.dtype)


def low_rows(ids, tokens, here, share, groups, arrays, before, dtype, cost=COST):
    rank = arrays[0].shape[1]
    return pl.pallas_call(
        functools.partial(low_kernel, groups, here, share, rank),
        in_specs=[VMEM] * (3 + len(arrays)),
        out_specs=VMEM,
        out_shape=jax.ShapeDtypeStruct((rank, tokens.shape[0]), dtype),
        compiler_params=params(24),
        cost_estimate=cost,
        name="low_rows",
    )(ids, tokens, *arrays, before)


def join_kernel(first_ref, second_ref, out_ref):
    out_ref[: first_ref.shape[0]] = first_ref[...]
    out_ref[first_ref.shape[0] :] = second_ref[...]


def joined(first, second):
    return pl.pallas_call(
        join_kernel,
        in_specs=[VMEM] * 2,
        out_specs=VMEM,
        out_shape=jax.ShapeDtypeStruct((2 * first.shape[0], *first.shape[1:]), BF16),
        compiler_params=params(16),
        cost_estimate=COST,
        name="joined",
    )(first, second)


def ups_kernel(terms, here, share, rank, ids_ref, bits_ref, matrix_ref, *refs):
    up_ref, mask_ref = refs[-2:]
    width = up_ref.shape[1]
    signs = (1 - 2 * bits_ref[...]).astype(F32)
    ids = jnp.broadcast_to(ids_ref[...], (rank, ids_ref.shape[1])).T
    for n, (i, k, cut, name) in enumerate(terms):
        turned = rotate(refs[i][k, :, cut : cut + width].astype(F32), signs, matrix_ref[...])
        up_ref[n * rank : (n + 1) * rank, :] = jnp.concatenate(turned, axis=1).astype(BF16)
        mine = ids == adapter(here, share, name)
        mask_ref[:, n * rank : (n + 1) * rank] = jnp.where(mine, 1.0, 0.0).astype(BF16)


def rotated_ups(ids, bits, matrix, here, share, terms, arrays, width):
    rank, rows = arrays[0].shape[1], ids.shape[1]
    every = len(terms) * rank
    return pl.pallas_call(
        functools.partial(ups_kernel, terms, here, share, rank),
        in_specs=[VMEM] * (3 + len(arrays)),
        out_specs=[VMEM, VMEM],
        out_shape=[jax.ShapeDtypeStruct((every, width), BF16), jax.ShapeDtypeStruct((rows, every), BF16)],
        compiler_params=params(32),
        cost_estimate=COST,
        name="rotated_ups",
    )(ids, bits, matrix, *arrays)


def final_kernel(mine_ref, theirs_ref, base_ref, up_ref, mask_ref, out_ref):
    low = (mine_ref[...].astype(F32) + theirs_ref[...].astype(F32)).T.astype(BF16)
    every = mask_ref.shape[1]
    spread = jnp.concatenate([low] * (every // low.shape[1]), axis=1) * mask_ref[...]
    delta = jnp.dot(spread, up_ref[...], preferred_element_type=F32)
    out_ref[...] = (base_ref[...] + delta).astype(BF16)


def final(mine, theirs, base, up, mask):
    rows, width = base.shape
    return pl.pallas_call(
        final_kernel,
        in_specs=[VMEM] * 5,
        out_specs=VMEM,
        out_shape=jax.ShapeDtypeStruct((rows, width), BF16),
        compiler_params=params(32),
        cost_estimate=COST,
        name="final",
    )(mine, theirs, base, up, mask)


def local(tokens, adapter_ids, base_weight, channel_scale, adapter_down, adapter_up, sign_bits):
    planes, groups, parts = lax.axis_size("adp"), lax.axis_size("grp"), lax.axis_size("tp")
    features = tokens.shape[1]
    here, _, rank = adapter_down.shape
    width = adapter_up.shape[2]
    share = here // groups
    matrix = hadamard(sign_bits.shape[0])
    bits, scale, ids = sign_bits[None, :], channel_scale[None, :], adapter_ids.T
    down = jnp.swapaxes(adapter_down, 1, 2)

    own = lax.dynamic_slice_in_dim(down, lax.axis_index("grp") * share, share, 0)
    near = swap(own, "adp", 1)
    mine = [(0, own)]
    bit = planes // 2
    while bit > 1:
        mine += [(plane | bit, swap(piece, "adp", bit)) for plane, piece in mine]
        bit //= 2
    low, *blocks = partials(ids, tokens, base_weight, down, parts)
    half = parts // 2
    near, low = together(near, low)
    close, up, *far = together(near, adapter_up, *(piece for _, piece in mine[1:]))
    mine = mine[:1] + [(plane, piece) for (plane, _), piece in zip(mine[1:], far)]
    odd = [(1, near)] + [(plane | 1, swap(piece, "adp", 1)) for plane, piece in mine[1:]]

    def others(pieces):
        return [(plane, off, swap(piece, "grp", off)) for plane, piece in pieces for off in range(1, groups)]

    swapped = others(odd[:1]) + others(mine[1:]) + others(odd[1:])
    held = [(plane, 0, piece) for plane, piece in [(1, close)] + mine[1:] + odd[1:]]

    def terms(pieces, start):
        return [(start + i, k, 0, (plane, off, k)) for i, (plane, off, _) in enumerate(pieces) for k in range(share)]

    whole = (0, features)
    early = held[: len(mine)] + swapped[:1]
    middle = held[len(mine) :] + swapped[1:-1]
    late = swapped[-1:]
    low = low_rows(ids, tokens, here, share, [(whole, terms(early, 0))], [p for *_, p in early], low, F32, SOME)

    ups, order = up, [0]
    bit = planes // 2
    while bit > 1:
        ups = joined(ups, swap(ups, "adp", bit))
        order += [plane | bit for plane in order]
        bit //= 2

    low, ups, *came = together(low, ups, *(swap(block, "tp", 1) for block in blocks[:half]))
    sums = [[block, pair] for block, pair in zip(blocks[half:], came)]
    bit = 2
    while bit < parts:
        came = [swap(add(*terms), "tp", bit) for terms in sums[1::2]]
        sums = [terms + [pair] for terms, pair in zip(sums[0::2], came)]
        bit *= 2
    base = rotated_base(sums[0], scale, bits, matrix)

    every = [(side, here * i + k, 0, ("plane", plane | side, k)) for side in (0, 1) for i, plane in enumerate(order) for k in range(here)]
    up, mask = rotated_ups(ids, bits, matrix, here, share, every, [ups, swap(ups, "adp", 1)], width)

    low = low_rows(ids, tokens, here, share, [(whole, terms(middle, 0))], [p for *_, p in middle], low, F32, SOME)
    low, base, up, mask = together(low, base, up, mask)
    low = low_rows(ids, tokens, here, share, [(whole, terms(late, 0))], [p for *_, p in late], low, BF16)
    bit = 1
    while bit < parts // 2:
        low = add(low, swap(low, "tp", bit))
        bit *= 2
    other = swap(low, "tp", bit)

    return final(low, other, base, up, mask)


def solution(mesh):
    return jax.shard_map(
        local,
        mesh=mesh,
        in_specs=(
            P(("grp", "adp"), "tp"),
            P(("grp", "adp"), None),
            P("tp", None),
            P("tp"),
            P("adp", "tp", None),
            P("adp", None, "tp"),
            P(),
        ),
        out_specs=P(("grp", "adp"), "tp"),
        check_vma=False,
    )
```

```python
import functools

import jax
import jax.numpy as jnp
import numpy as np
from jax import lax
from jax.experimental import pallas as pl
from jax.experimental.pallas import tpu as pltpu
from jax.sharding import PartitionSpec as P

VMEM = pl.BlockSpec(memory_space=pltpu.VMEM)
SMEM = pl.BlockSpec(memory_space=pltpu.SMEM)
F32, BF16 = jnp.float32, jnp.bfloat16
LAST = (((1,), (1,)), ((), ()))


def params(mib):
    return pltpu.CompilerParams(vmem_limit_bytes=mib << 20)


COST = pl.CostEstimate(flops=1, bytes_accessed=1, transcendentals=0)
SOME = pl.CostEstimate(flops=5_000_000_000, bytes_accessed=1, transcendentals=0)


def hadamard(size):
    index = np.arange(size)
    shared = index[:, None] & index[None, :]
    parity = np.zeros_like(shared)
    while shared.any():
        parity, shared = parity ^ (shared & 1), shared >> 1
    return jnp.asarray(1 - 2 * parity, BF16)


def swap(x, axis, bit):
    return lax.ppermute(x, axis, [(i, i ^ bit) for i in range(lax.axis_size(axis))])


def together(*values):
    return lax.optimization_barrier(values)


def rotate(value, signs, matrix):
    head = matrix.shape[0]
    scale = signs * (1.0 / np.sqrt(head))
    turned = []
    for at in range(0, value.shape[1], head):
        signed = value[:, at : at + head] * scale
        high = signed.astype(BF16)
        rest = (signed - high.astype(F32)).astype(BF16)
        turned.append(
            jnp.dot(high, matrix, preferred_element_type=F32) + jnp.dot(rest, matrix, preferred_element_type=F32)
        )
    return turned


def partial_kernel(here, ids_ref, tokens_ref, weight_ref, down_ref, low_ref, *outs):
    me, width = lax.axis_index("tp"), outs[0].shape[1]
    for n, out_ref in enumerate(outs):
        offset = 2 * n + 1 if n < len(outs) // 2 else 2 * n - len(outs)
        at = pl.multiple_of(jnp.bitwise_xor(me, offset) * width, width)
        product = jnp.dot(tokens_ref[...], weight_ref[:, pl.ds(at, width)], preferred_element_type=F32)
        out_ref[...] = product.astype(BF16)
    rank = down_ref.shape[1]
    joined = jnp.concatenate([down_ref[k] for k in range(here)], axis=0)
    product = lax.dot_general(joined, tokens_ref[...], LAST, preferred_element_type=F32)
    terms = [
        jnp.where(ids_ref[...] == adapter(here, 0, ("plane", 0, k)), product[k * rank : (k + 1) * rank], 0.0)
        for k in range(here)
    ]
    low_ref[...] = functools.reduce(jnp.add, terms)


def partials(ids, tokens, weight, down, parts):
    rows, width = tokens.shape[0], weight.shape[1] // parts
    here, rank, _ = down.shape
    return pl.pallas_call(
        functools.partial(partial_kernel, here),
        in_specs=[VMEM] * 4,
        out_specs=[VMEM] * (1 + parts),
        out_shape=[jax.ShapeDtypeStruct((rank, rows), F32)] + [jax.ShapeDtypeStruct((rows, width), BF16)] * parts,
        compiler_params=params(24),
        cost_estimate=COST,
        name="partials",
    )(ids, tokens, weight, down)


def add_kernel(*refs):
    total = refs[0][...].astype(F32)
    for ref in refs[1:-1]:
        total = total + ref[...].astype(F32)
    refs[-1][...] = total.astype(BF16)


def add(*terms):
    return pl.pallas_call(
        add_kernel,
        in_specs=[VMEM] * len(terms),
        out_specs=VMEM,
        out_shape=jax.ShapeDtypeStruct(terms[0].shape, BF16),
        compiler_params=params(16),
        cost_estimate=COST,
        name="add",
    )(*terms)


def base_kernel(scale_ref, bits_ref, matrix_ref, *refs):
    total = refs[0][...].astype(F32)
    for ref in refs[1:-1]:
        total = total + ref[...].astype(F32)
    signs = (1 - 2 * bits_ref[...]).astype(F32)
    refs[-1][...] = jnp.concatenate(rotate(total * scale_ref[...], signs, matrix_ref[...]), axis=1)


def rotated_base(terms, scale, bits, matrix):
    return pl.pallas_call(
        base_kernel,
        in_specs=[VMEM] * (3 + len(terms)),
        out_specs=VMEM,
        out_shape=jax.ShapeDtypeStruct(terms[0].shape, F32),
        compiler_params=params(16),
        cost_estimate=COST,
        name="rotated_base",
    )(scale, bits, matrix, *terms)


def adapter(here, share, name):
    z = lax.axis_index("adp")
    if name[0] == "plane":
        return jnp.bitwise_xor(z, name[1]) * here + name[2]
    plane, off, k = name
    return jnp.bitwise_xor(z, plane) * here + jnp.bitwise_xor(lax.axis_index("grp"), off) * share + k


def low_kernel(groups, here, share, rank, ids_ref, tokens_ref, *refs):
    out_ref = refs[-1]
    total = refs[-2][...]
    for (start, stop), terms in groups:
        rows = [refs[i][k, :, cut : cut + stop - start] for i, k, cut, _ in terms]
        joined = rows[0] if len(rows) == 1 else jnp.concatenate(rows, axis=0)
        product = lax.dot_general(joined, tokens_ref[:, start:stop], LAST, preferred_element_type=F32)
        for n, (_, _, _, name) in enumerate(terms):
            mine = ids_ref[...] == adapter(here, share, name)
            term = jnp.where(mine, product[n * rank : (n + 1) * rank], 0.0)
            total = total + term
    out_ref[...] = total.astype(out_ref.dtype)


def low_rows(ids, tokens, here, share, groups, arrays, before, dtype, cost=COST):
    rank = arrays[0].shape[1]
    return pl.pallas_call(
        functools.partial(low_kernel, groups, here, share, rank),
        in_specs=[VMEM] * (3 + len(arrays)),
        out_specs=VMEM,
        out_shape=jax.ShapeDtypeStruct((rank, tokens.shape[0]), dtype),
        compiler_params=params(24),
        cost_estimate=cost,
        name="low_rows",
    )(ids, tokens, *arrays, before)


def join_kernel(first_ref, second_ref, out_ref):
    out_ref[: first_ref.shape[0]] = first_ref[...]
    out_ref[first_ref.shape[0] :] = second_ref[...]


def joined(first, second):
    return pl.pallas_call(
        join_kernel,
        in_specs=[VMEM] * 2,
        out_specs=VMEM,
        out_shape=jax.ShapeDtypeStruct((2 * first.shape[0], *first.shape[1:]), BF16),
        compiler_params=params(16),
        cost_estimate=COST,
        name="joined",
    )(first, second)


def ups_kernel(terms, here, share, rank, ids_ref, bits_ref, matrix_ref, *refs):
    up_ref, mask_ref = refs[-2:]
    width = up_ref.shape[1]
    signs = (1 - 2 * bits_ref[...]).astype(F32)
    ids = jnp.broadcast_to(ids_ref[...], (rank, ids_ref.shape[1])).T
    for n, (i, k, cut, name) in enumerate(terms):
        turned = rotate(refs[i][k, :, cut : cut + width].astype(F32), signs, matrix_ref[...])
        up_ref[n * rank : (n + 1) * rank, :] = jnp.concatenate(turned, axis=1).astype(BF16)
        mine = ids == adapter(here, share, name)
        mask_ref[:, n * rank : (n + 1) * rank] = jnp.where(mine, 1.0, 0.0).astype(BF16)


def rotated_ups(ids, bits, matrix, here, share, terms, arrays, width):
    rank, rows = arrays[0].shape[1], ids.shape[1]
    every = len(terms) * rank
    return pl.pallas_call(
        functools.partial(ups_kernel, terms, here, share, rank),
        in_specs=[VMEM] * (3 + len(arrays)),
        out_specs=[VMEM, VMEM],
        out_shape=[jax.ShapeDtypeStruct((every, width), BF16), jax.ShapeDtypeStruct((rows, every), BF16)],
        compiler_params=params(32),
        cost_estimate=COST,
        name="rotated_ups",
    )(ids, bits, matrix, *arrays)


def final_kernel(mine_ref, theirs_ref, base_ref, up_ref, mask_ref, out_ref):
    low = (mine_ref[...].astype(F32) + theirs_ref[...].astype(F32)).T.astype(BF16)
    every = mask_ref.shape[1]
    spread = jnp.concatenate([low] * (every // low.shape[1]), axis=1) * mask_ref[...]
    delta = jnp.dot(spread, up_ref[...], preferred_element_type=F32)
    out_ref[...] = (base_ref[...] + delta).astype(BF16)


def final(mine, theirs, base, up, mask):
    rows, width = base.shape
    return pl.pallas_call(
        final_kernel,
        in_specs=[VMEM] * 5,
        out_specs=VMEM,
        out_shape=jax.ShapeDtypeStruct((rows, width), BF16),
        compiler_params=params(32),
        cost_estimate=COST,
        name="final",
    )(mine, theirs, base, up, mask)


def local(tokens, adapter_ids, base_weight, channel_scale, adapter_down, adapter_up, sign_bits):
    planes, groups, parts = lax.axis_size("adp"), lax.axis_size("grp"), lax.axis_size("tp")
    features = tokens.shape[1]
    here, _, rank = adapter_down.shape
    width = adapter_up.shape[2]
    share = here // groups
    matrix = hadamard(sign_bits.shape[0])
    bits, scale, ids = sign_bits[None, :], channel_scale[None, :], adapter_ids.T
    down = jnp.swapaxes(adapter_down, 1, 2)

    own = lax.dynamic_slice_in_dim(down, lax.axis_index("grp") * share, share, 0)
    near = swap(own, "adp", 1)
    mine = [(0, own)]
    bit = planes // 2
    while bit > 1:
        mine += [(plane | bit, swap(piece, "adp", bit)) for plane, piece in mine]
        bit //= 2
    low, *blocks = partials(ids, tokens, base_weight, down, parts)
    half = parts // 2
    near, low = together(near, low)
    close, *far = together(near, *(piece for _, piece in mine[1:]))
    mine = mine[:1] + [(plane, piece) for (plane, _), piece in zip(mine[1:], far)]
    odd = [(1, near)] + [(plane | 1, swap(piece, "adp", 1)) for plane, piece in mine[1:]]

    def others(pieces):
        return [(plane, off, swap(piece, "grp", off)) for plane, piece in pieces for off in range(1, groups)]

    swapped = others(odd[:1]) + others(mine[1:]) + others(odd[1:])
    held = [(plane, 0, piece) for plane, piece in [(1, close)] + mine[1:] + odd[1:]]

    def terms(pieces, start):
        return [(start + i, k, 0, (plane, off, k)) for i, (plane, off, _) in enumerate(pieces) for k in range(share)]

    whole = (0, features)
    early = held[: len(mine)] + swapped[:1]
    middle = held[len(mine) :] + swapped[1:-1]
    late = swapped[-1:]
    plane, off, piece = early[-1]
    piece, ups = together(piece, adapter_up)
    early[-1], order = (plane, off, piece), [0]
    bit = planes // 2
    while bit > 1:
        ups = joined(ups, swap(ups, "adp", bit))
        order += [plane | bit for plane in order]
        bit //= 2
    low = low_rows(ids, tokens, here, share, [(whole, terms(early, 0))], [p for *_, p in early], low, F32, SOME)

    low, *came = together(low, *(swap(block, "tp", 1) for block in blocks[:half]))
    sums = [[block, pair] for block, pair in zip(blocks[half:], came)]
    bit = 2
    while bit < parts:
        came = [swap(add(*terms), "tp", bit) for terms in sums[1::2]]
        sums = [terms + [pair] for terms, pair in zip(sums[0::2], came)]
        bit *= 2
    base = rotated_base(sums[0], scale, bits, matrix)

    every = [(side, here * i + k, 0, ("plane", plane | side, k)) for side in (0, 1) for i, plane in enumerate(order) for k in range(here)]
    up, mask = rotated_ups(ids, bits, matrix, here, share, every, [ups, swap(ups, "adp", 1)], width)

    low = low_rows(ids, tokens, here, share, [(whole, terms(middle, 0))], [p for *_, p in middle], low, F32, SOME)
    low, base, up, mask = together(low, base, up, mask)
    low = low_rows(ids, tokens, here, share, [(whole, terms(late, 0))], [p for *_, p in late], low, BF16)
    bit = 1
    while bit < parts // 2:
        low = add(low, swap(low, "tp", bit))
        bit *= 2
    other = swap(low, "tp", bit)

    return final(low, other, base, up, mask)


def solution(mesh):
    return jax.shard_map(
        local,
        mesh=mesh,
        in_specs=(
            P(("grp", "adp"), "tp"),
            P(("grp", "adp"), None),
            P("tp", None),
            P("tp"),
            P("adp", "tp", None),
            P("adp", None, "tp"),
            P(),
        ),
        out_specs=P(("grp", "adp"), "tp"),
        check_vma=False,
    )
```

```python
import functools

import jax
import jax.numpy as jnp
import numpy as np
from jax import lax
from jax.experimental import pallas as pl
from jax.experimental.pallas import tpu as pltpu
from jax.sharding import PartitionSpec as P

VMEM = pl.BlockSpec(memory_space=pltpu.VMEM)
SMEM = pl.BlockSpec(memory_space=pltpu.SMEM)
F32, BF16 = jnp.float32, jnp.bfloat16
LAST = (((1,), (1,)), ((), ()))


def params(mib):
    return pltpu.CompilerParams(vmem_limit_bytes=mib << 20)


COST = pl.CostEstimate(flops=1, bytes_accessed=1, transcendentals=0)


def lasting(microseconds):
    return pl.CostEstimate(flops=int(microseconds * 1e9), bytes_accessed=1, transcendentals=0)


def hadamard(size):
    index = np.arange(size)
    shared = index[:, None] & index[None, :]
    parity = np.zeros_like(shared)
    while shared.any():
        parity, shared = parity ^ (shared & 1), shared >> 1
    return jnp.asarray(1 - 2 * parity, BF16)


def swap(x, axis, bit):
    return lax.ppermute(x, axis, [(i, i ^ bit) for i in range(lax.axis_size(axis))])


def together(*values):
    return lax.optimization_barrier(values)


def rotate(value, signs, matrix):
    head = matrix.shape[0]
    scale = signs * (1.0 / np.sqrt(head))
    turned = []
    for at in range(0, value.shape[1], head):
        signed = value[:, at : at + head] * scale
        high = signed.astype(BF16)
        rest = (signed - high.astype(F32)).astype(BF16)
        turned.append(
            jnp.dot(high, matrix, preferred_element_type=F32) + jnp.dot(rest, matrix, preferred_element_type=F32)
        )
    return turned


def partial_kernel(offsets, parts, tokens_ref, weight_ref, before_ref, after_ref, *outs):
    me, width = lax.axis_index("tp"), weight_ref.shape[1] // parts
    for offset, out_ref in zip(offsets, outs):
        at = pl.multiple_of(jnp.bitwise_xor(me, offset) * width, width)
        product = jnp.dot(tokens_ref[...], weight_ref[:, pl.ds(at, width)], preferred_element_type=F32)
        out_ref[...] = product.astype(BF16)
    after_ref[...] = before_ref[...]


def partials(tokens, weight, parts, offsets, before, cost):
    block = jax.ShapeDtypeStruct((tokens.shape[0], weight.shape[1] // parts), BF16)
    return pl.pallas_call(
        functools.partial(partial_kernel, offsets, parts),
        in_specs=[VMEM] * 3,
        out_specs=[VMEM] * (1 + len(offsets)),
        out_shape=[jax.ShapeDtypeStruct(before.shape, before.dtype)] + [block] * len(offsets),
        compiler_params=params(24),
        cost_estimate=cost,
        name="partials",
    )(tokens, weight, before)


def add_kernel(*refs):
    total = refs[0][...].astype(F32)
    for ref in refs[1:-1]:
        total = total + ref[...].astype(F32)
    refs[-1][...] = total.astype(BF16)


def add(*terms):
    return pl.pallas_call(
        add_kernel,
        in_specs=[VMEM] * len(terms),
        out_specs=VMEM,
        out_shape=jax.ShapeDtypeStruct(terms[0].shape, BF16),
        compiler_params=params(16),
        cost_estimate=COST,
        name="add",
    )(*terms)


def base_kernel(scale_ref, bits_ref, matrix_ref, *refs):
    total = refs[0][...].astype(F32)
    for ref in refs[1:-1]:
        total = total + ref[...].astype(F32)
    signs = (1 - 2 * bits_ref[...]).astype(F32)
    refs[-1][...] = jnp.concatenate(rotate(total * scale_ref[...], signs, matrix_ref[...]), axis=1)


def rotated_base(terms, scale, bits, matrix):
    return pl.pallas_call(
        base_kernel,
        in_specs=[VMEM] * (3 + len(terms)),
        out_specs=VMEM,
        out_shape=jax.ShapeDtypeStruct(terms[0].shape, F32),
        compiler_params=params(16),
        cost_estimate=COST,
        name="rotated_base",
    )(scale, bits, matrix, *terms)


def adapter(here, share, name):
    z = lax.axis_index("adp")
    if name[0] == "plane":
        return jnp.bitwise_xor(z, name[1]) * here + name[2]
    plane, off, k = name
    return jnp.bitwise_xor(z, plane) * here + jnp.bitwise_xor(lax.axis_index("grp"), off) * share + k


def low_kernel(groups, here, share, rank, more, ids_ref, tokens_ref, *refs):
    out_ref = refs[-1]
    total = refs[-2][...] if more else None
    for (start, stop), terms in groups:
        rows = [refs[i][k, :, cut : cut + stop - start] for i, k, cut, _ in terms]
        joined = rows[0] if len(rows) == 1 else jnp.concatenate(rows, axis=0)
        product = lax.dot_general(joined, tokens_ref[:, start:stop], LAST, preferred_element_type=F32)
        for n, (_, _, _, name) in enumerate(terms):
            mine = ids_ref[...] == adapter(here, share, name)
            term = jnp.where(mine, product[n * rank : (n + 1) * rank], 0.0)
            total = term if total is None else total + term
    out_ref[...] = total.astype(out_ref.dtype)


def low_rows(ids, tokens, here, share, groups, arrays, before, dtype, cost=COST):
    rank = arrays[0].shape[1]
    more = [] if before is None else [before]
    return pl.pallas_call(
        functools.partial(low_kernel, groups, here, share, rank, bool(more)),
        in_specs=[VMEM] * (2 + len(arrays) + len(more)),
        out_specs=VMEM,
        out_shape=jax.ShapeDtypeStruct((rank, tokens.shape[0]), dtype),
        compiler_params=params(24),
        cost_estimate=cost,
        name="low_rows",
    )(ids, tokens, *arrays, *more)


def join_kernel(first_ref, second_ref, out_ref):
    out_ref[: first_ref.shape[0]] = first_ref[...]
    out_ref[first_ref.shape[0] :] = second_ref[...]


def joined(first, second):
    return pl.pallas_call(
        join_kernel,
        in_specs=[VMEM] * 2,
        out_specs=VMEM,
        out_shape=jax.ShapeDtypeStruct((2 * first.shape[0], *first.shape[1:]), BF16),
        compiler_params=params(16),
        cost_estimate=COST,
        name="joined",
    )(first, second)


def ups_kernel(terms, here, share, rank, ids_ref, bits_ref, matrix_ref, *refs):
    up_ref, mask_ref = refs[-2:]
    width = up_ref.shape[1]
    signs = (1 - 2 * bits_ref[...]).astype(F32)
    ids = jnp.broadcast_to(ids_ref[...], (rank, ids_ref.shape[1])).T
    for n, (i, k, cut, name) in enumerate(terms):
        turned = rotate(refs[i][k, :, cut : cut + width].astype(F32), signs, matrix_ref[...])
        up_ref[n * rank : (n + 1) * rank, :] = jnp.concatenate(turned, axis=1).astype(BF16)
        mine = ids == adapter(here, share, name)
        mask_ref[:, n * rank : (n + 1) * rank] = jnp.where(mine, 1.0, 0.0).astype(BF16)


def rotated_ups(ids, bits, matrix, here, share, terms, arrays, width):
    rank, rows = arrays[0].shape[1], ids.shape[1]
    every = len(terms) * rank
    return pl.pallas_call(
        functools.partial(ups_kernel, terms, here, share, rank),
        in_specs=[VMEM] * (3 + len(arrays)),
        out_specs=[VMEM, VMEM],
        out_shape=[jax.ShapeDtypeStruct((every, width), BF16), jax.ShapeDtypeStruct((rows, every), BF16)],
        compiler_params=params(32),
        cost_estimate=COST,
        name="rotated_ups",
    )(ids, bits, matrix, *arrays)


def final_kernel(mine_ref, theirs_ref, base_ref, up_ref, mask_ref, out_ref):
    low = (mine_ref[...].astype(F32) + theirs_ref[...].astype(F32)).T.astype(BF16)
    every = mask_ref.shape[1]
    spread = jnp.concatenate([low] * (every // low.shape[1]), axis=1) * mask_ref[...]
    delta = jnp.dot(spread, up_ref[...], preferred_element_type=F32)
    out_ref[...] = (base_ref[...] + delta).astype(BF16)


def final(mine, theirs, base, up, mask):
    rows, width = base.shape
    return pl.pallas_call(
        final_kernel,
        in_specs=[VMEM] * 5,
        out_specs=VMEM,
        out_shape=jax.ShapeDtypeStruct((rows, width), BF16),
        compiler_params=params(32),
        cost_estimate=COST,
        name="final",
    )(mine, theirs, base, up, mask)


def local(tokens, adapter_ids, base_weight, channel_scale, adapter_down, adapter_up, sign_bits):
    planes, groups, parts = lax.axis_size("adp"), lax.axis_size("grp"), lax.axis_size("tp")
    features = tokens.shape[1]
    here, _, rank = adapter_down.shape
    width = adapter_up.shape[2]
    share = here // groups
    matrix = hadamard(sign_bits.shape[0])
    bits, scale, ids = sign_bits[None, :], channel_scale[None, :], adapter_ids.T
    down = jnp.swapaxes(adapter_down, 1, 2)

    own = lax.dynamic_slice_in_dim(down, lax.axis_index("grp") * share, share, 0)
    near = swap(own, "adp", 1)
    mine = [(0, own)]
    bit = planes // 2
    while bit > 1:
        mine += [(plane | bit, swap(piece, "adp", bit)) for plane, piece in mine]
        bit //= 2
    half = parts // 2
    offsets = (*range(1, parts, 2), *range(2, parts, 2))
    passed, *blocks = partials(tokens, base_weight, parts, offsets, scale, lasting(4))
    near, passed = together(near, passed)
    scale, block = partials(tokens, base_weight, parts, (0,), passed, COST)
    blocks = blocks[:half] + [block] + blocks[half:]
    close, scale, *far = together(near, scale, *(piece for _, piece in mine[1:]))
    mine = mine[:1] + [(plane, piece) for (plane, _), piece in zip(mine[1:], far)]
    odd = [(1, near)] + [(plane | 1, swap(piece, "adp", 1)) for plane, piece in mine[1:]]

    def others(pieces):
        return [(plane, off, swap(piece, "grp", off)) for plane, piece in pieces for off in range(1, groups)]

    swapped = others(odd[:1]) + others(mine[1:]) + others(odd[1:])
    held = [(plane, 0, piece) for plane, piece in [(1, close)] + mine[1:] + odd[1:]]

    def terms(pieces, start):
        return [(start + i, k, 0, (plane, off, k)) for i, (plane, off, _) in enumerate(pieces) for k in range(share)]

    def more(low, pieces, dtype, cost=COST):
        arrays, every = [p for *_, p in pieces], terms(pieces, 0)
        if low is None:
            every += [(len(arrays), k, 0, ("plane", 0, k)) for k in range(here)]
            arrays = arrays + [down]
        return low_rows(ids, tokens, here, share, [((0, features), every)], arrays, low, dtype, cost)

    low = more(None, held[: len(mine)] + swapped[:1], F32, lasting(2))
    low, ups, *came = together(low, adapter_up, *(swap(block, "tp", 1) for block in blocks[:half]))

    order = [0]
    bit = planes // 2
    rest = held[len(mine) :]
    while bit > 1:
        (plane, off, piece), other = rest[0], swap(ups, "adp", bit)
        piece, other = together(piece, other)
        rest[0], ups = (plane, off, piece), joined(ups, other)
        order += [plane | bit for plane in order]
        bit //= 2
    low = more(low, swapped[1:-1] + rest, F32, lasting(5))

    sums = [[block, pair] for block, pair in zip(blocks[half:], came)]
    bit = 2
    while bit < parts:
        came = [swap(add(*terms), "tp", bit) for terms in sums[1::2]]
        sums = [terms + [pair] for terms, pair in zip(sums[0::2], came)]
        bit *= 2
    base = rotated_base(sums[0], scale, bits, matrix)

    every = [(side, here * i + k, 0, ("plane", plane | side, k)) for side in (0, 1) for i, plane in enumerate(order) for k in range(here)]
    up, mask = rotated_ups(ids, bits, matrix, here, share, every, [ups, swap(ups, "adp", 1)], width)

    low, up, mask = together(low, up, mask)
    low = more(low, swapped[-1:], BF16)
    bit = 1
    while bit < parts // 2:
        low = add(low, swap(low, "tp", bit))
        bit *= 2
    other = swap(low, "tp", bit)

    return final(low, other, base, up, mask)


def solution(mesh):
    return jax.shard_map(
        local,
        mesh=mesh,
        in_specs=(
            P(("grp", "adp"), "tp"),
            P(("grp", "adp"), None),
            P("tp", None),
            P("tp"),
            P("adp", "tp", None),
            P("adp", None, "tp"),
            P(),
        ),
        out_specs=P(("grp", "adp"), "tp"),
        check_vma=False,
    )
```

```python
import functools

import jax
import jax.numpy as jnp
import numpy as np
from jax import lax
from jax.experimental import pallas as pl
from jax.experimental.pallas import tpu as pltpu
from jax.sharding import PartitionSpec as P

VMEM = pl.BlockSpec(memory_space=pltpu.VMEM)
SMEM = pl.BlockSpec(memory_space=pltpu.SMEM)
F32, BF16 = jnp.float32, jnp.bfloat16
LAST = (((1,), (1,)), ((), ()))


def params(mib):
    return pltpu.CompilerParams(vmem_limit_bytes=mib << 20)


COST = pl.CostEstimate(flops=1, bytes_accessed=1, transcendentals=0)


def lasting(microseconds):
    return pl.CostEstimate(flops=int(microseconds * 1e9), bytes_accessed=1, transcendentals=0)


def hadamard(size):
    index = np.arange(size)
    shared = index[:, None] & index[None, :]
    parity = np.zeros_like(shared)
    while shared.any():
        parity, shared = parity ^ (shared & 1), shared >> 1
    return jnp.asarray(1 - 2 * parity, BF16)


def swap(x, axis, bit):
    return lax.ppermute(x, axis, [(i, i ^ bit) for i in range(lax.axis_size(axis))])


def together(*values):
    return lax.optimization_barrier(values)


def rotate(value, signs, matrix):
    head = matrix.shape[0]
    scale = signs * (1.0 / np.sqrt(head))
    turned = []
    for at in range(0, value.shape[1], head):
        signed = value[:, at : at + head] * scale
        high = signed.astype(BF16)
        rest = (signed - high.astype(F32)).astype(BF16)
        turned.append(
            jnp.dot(high, matrix, preferred_element_type=F32) + jnp.dot(rest, matrix, preferred_element_type=F32)
        )
    return turned


def partial_kernel(offsets, parts, tokens_ref, weight_ref, before_ref, after_ref, *outs):
    me, width = lax.axis_index("tp"), weight_ref.shape[1] // parts
    for offset, out_ref in zip(offsets, outs):
        at = pl.multiple_of(jnp.bitwise_xor(me, offset) * width, width)
        product = jnp.dot(tokens_ref[...], weight_ref[:, pl.ds(at, width)], preferred_element_type=F32)
        out_ref[...] = product.astype(BF16)
    after_ref[...] = before_ref[...]


def partials(tokens, weight, parts, offsets, before, cost):
    block = jax.ShapeDtypeStruct((tokens.shape[0], weight.shape[1] // parts), BF16)
    return pl.pallas_call(
        functools.partial(partial_kernel, offsets, parts),
        in_specs=[VMEM] * 3,
        out_specs=[VMEM] * (1 + len(offsets)),
        out_shape=[jax.ShapeDtypeStruct(before.shape, before.dtype)] + [block] * len(offsets),
        compiler_params=params(24),
        cost_estimate=cost,
        name="partials",
    )(tokens, weight, before)


def add_kernel(*refs):
    total = refs[0][...].astype(F32)
    for ref in refs[1:-1]:
        total = total + ref[...].astype(F32)
    refs[-1][...] = total.astype(BF16)


def add(*terms):
    return pl.pallas_call(
        add_kernel,
        in_specs=[VMEM] * len(terms),
        out_specs=VMEM,
        out_shape=jax.ShapeDtypeStruct(terms[0].shape, BF16),
        compiler_params=params(16),
        cost_estimate=COST,
        name="add",
    )(*terms)


def base_kernel(scale_ref, bits_ref, matrix_ref, *refs):
    total = refs[0][...].astype(F32)
    for ref in refs[1:-1]:
        total = total + ref[...].astype(F32)
    signs = (1 - 2 * bits_ref[...]).astype(F32)
    refs[-1][...] = jnp.concatenate(rotate(total * scale_ref[...], signs, matrix_ref[...]), axis=1)


def rotated_base(terms, scale, bits, matrix):
    return pl.pallas_call(
        base_kernel,
        in_specs=[VMEM] * (3 + len(terms)),
        out_specs=VMEM,
        out_shape=jax.ShapeDtypeStruct(terms[0].shape, F32),
        compiler_params=params(16),
        cost_estimate=COST,
        name="rotated_base",
    )(scale, bits, matrix, *terms)


def adapter(here, share, name):
    z = lax.axis_index("adp")
    if name[0] == "plane":
        return jnp.bitwise_xor(z, name[1]) * here + name[2]
    plane, off, k = name
    return jnp.bitwise_xor(z, plane) * here + jnp.bitwise_xor(lax.axis_index("grp"), off) * share + k


def low_kernel(groups, here, share, rank, more, ids_ref, tokens_ref, *refs):
    out_ref = refs[-1]
    total = refs[-2][...] if more else None
    for (start, stop), terms in groups:
        rows = [refs[i][k, :, cut : cut + stop - start] for i, k, cut, _ in terms]
        joined = rows[0] if len(rows) == 1 else jnp.concatenate(rows, axis=0)
        product = lax.dot_general(joined, tokens_ref[:, start:stop], LAST, preferred_element_type=F32)
        for n, (_, _, _, name) in enumerate(terms):
            mine = ids_ref[...] == adapter(here, share, name)
            term = jnp.where(mine, product[n * rank : (n + 1) * rank], 0.0)
            total = term if total is None else total + term
    out_ref[...] = total.astype(out_ref.dtype)


def low_rows(ids, tokens, here, share, groups, arrays, before, dtype, cost=COST):
    rank = arrays[0].shape[1]
    more = [] if before is None else [before]
    return pl.pallas_call(
        functools.partial(low_kernel, groups, here, share, rank, bool(more)),
        in_specs=[VMEM] * (2 + len(arrays) + len(more)),
        out_specs=VMEM,
        out_shape=jax.ShapeDtypeStruct((rank, tokens.shape[0]), dtype),
        compiler_params=params(24),
        cost_estimate=cost,
        name="low_rows",
    )(ids, tokens, *arrays, *more)


def ups_kernel(terms, here, share, rank, ids_ref, bits_ref, matrix_ref, *refs):
    up_ref, mask_ref = refs[-2:]
    width = up_ref.shape[1]
    signs = (1 - 2 * bits_ref[...]).astype(F32)
    ids = jnp.broadcast_to(ids_ref[...], (rank, ids_ref.shape[1])).T
    for n, (i, k, cut, name) in enumerate(terms):
        turned = rotate(refs[i][k, :, cut : cut + width].astype(F32), signs, matrix_ref[...])
        up_ref[n * rank : (n + 1) * rank, :] = jnp.concatenate(turned, axis=1).astype(BF16)
        mine = ids == adapter(here, share, name)
        mask_ref[:, n * rank : (n + 1) * rank] = jnp.where(mine, 1.0, 0.0).astype(BF16)


def rotated_ups(ids, bits, matrix, here, share, terms, arrays, width):
    rank, rows = arrays[0].shape[1], ids.shape[1]
    every = len(terms) * rank
    return pl.pallas_call(
        functools.partial(ups_kernel, terms, here, share, rank),
        in_specs=[VMEM] * (3 + len(arrays)),
        out_specs=[VMEM, VMEM],
        out_shape=[jax.ShapeDtypeStruct((every, width), BF16), jax.ShapeDtypeStruct((rows, every), BF16)],
        compiler_params=params(32),
        cost_estimate=COST,
        name="rotated_ups",
    )(ids, bits, matrix, *arrays)


def final_kernel(mine_ref, theirs_ref, base_ref, up_ref, mask_ref, out_ref):
    low = (mine_ref[...].astype(F32) + theirs_ref[...].astype(F32)).T.astype(BF16)
    every = mask_ref.shape[1]
    spread = jnp.concatenate([low] * (every // low.shape[1]), axis=1) * mask_ref[...]
    delta = jnp.dot(spread, up_ref[...], preferred_element_type=F32)
    out_ref[...] = (base_ref[...] + delta).astype(BF16)


def final(mine, theirs, base, up, mask):
    rows, width = base.shape
    return pl.pallas_call(
        final_kernel,
        in_specs=[VMEM] * 5,
        out_specs=VMEM,
        out_shape=jax.ShapeDtypeStruct((rows, width), BF16),
        compiler_params=params(32),
        cost_estimate=COST,
        name="final",
    )(mine, theirs, base, up, mask)


def local(tokens, adapter_ids, base_weight, channel_scale, adapter_down, adapter_up, sign_bits):
    planes, groups, parts = lax.axis_size("adp"), lax.axis_size("grp"), lax.axis_size("tp")
    features = tokens.shape[1]
    here, _, rank = adapter_down.shape
    width = adapter_up.shape[2]
    share = here // groups
    matrix = hadamard(sign_bits.shape[0])
    bits, scale, ids = sign_bits[None, :], channel_scale[None, :], adapter_ids.T
    down = jnp.swapaxes(adapter_down, 1, 2)

    start = lax.axis_index("grp") * share
    own = lax.dynamic_slice_in_dim(down, start, share, 0)
    near = swap(own, "adp", 1)
    mine = [(0, jnp.concatenate([own, lax.dynamic_slice_in_dim(adapter_up, start, share, 0)], axis=2))]
    bit = planes // 2
    while bit > 1:
        mine += [(plane | bit, swap(piece, "adp", bit)) for plane, piece in mine]
        bit //= 2
    half = parts // 2
    offsets = (*range(1, parts, 2), *range(2, parts, 2))
    passed, *blocks = partials(tokens, base_weight, parts, offsets, scale, lasting(4))
    near, passed = together(near, passed)
    scale, block = partials(tokens, base_weight, parts, (0,), passed, COST)
    blocks = blocks[:half] + [block] + blocks[half:]
    close, scale, *far = together(near, scale, *(piece for _, piece in mine[1:]))
    mine = mine[:1] + [(plane, piece) for (plane, _), piece in zip(mine[1:], far)]
    odd = [(1, near)] + [(plane | 1, swap(piece, "adp", 1)) for plane, piece in mine[1:]]

    def others(pieces):
        return [(plane, off, swap(piece, "grp", off)) for plane, piece in pieces for off in range(1, groups)]

    swapped = others(odd[:1]) + others(mine[1:]) + others(odd[1:])
    held = [(plane, 0, piece) for plane, piece in [(1, close)] + mine[1:] + odd[1:]]

    def terms(pieces, start):
        return [(start + i, k, 0, (plane, off, k)) for i, (plane, off, _) in enumerate(pieces) for k in range(share)]

    def more(low, pieces, dtype, cost=COST):
        arrays, every = [p for *_, p in pieces], terms(pieces, 0)
        if low is None:
            every += [(len(arrays), k, 0, ("plane", 0, k)) for k in range(here)]
            arrays = arrays + [down]
        return low_rows(ids, tokens, here, share, [((0, features), every)], arrays, low, dtype, cost)

    low = more(None, held[: len(mine)] + swapped[:1], F32, lasting(2))
    low, *came = together(low, *(swap(block, "tp", 1) for block in blocks[:half]))

    rest = held[len(mine) :]
    plane, off, piece = swapped[-2]
    piece, up = together(piece, adapter_up)
    swapped[-2] = plane, off, piece
    ups = [adapter_up, swap(up, "adp", 1)]
    low = more(low, swapped[1:-1] + rest, F32, lasting(5))

    sums = [[block, pair] for block, pair in zip(blocks[half:], came)]
    bit = 2
    while bit < parts:
        came = [swap(add(*terms), "tp", bit) for terms in sums[1::2]]
        sums = [terms + [pair] for terms, pair in zip(sums[0::2], came)]
        bit *= 2
    base = rotated_base(sums[0], scale, bits, matrix)

    low, ups[1] = together(low, ups[1])
    low = more(low, swapped[-1:], BF16)
    bit = 1
    while bit < parts // 2:
        low = add(low, swap(low, "tp", bit))
        bit *= 2
    theirs = swap(low, "tp", bit)


    far = [one for one in held + swapped if one[0] > 1]
    every = [(plane, k, 0, ("plane", plane, k)) for plane in (0, 1) for k in range(here)]
    every += [(2 + i, k, features, (plane, off, k)) for i, (plane, off, _) in enumerate(far) for k in range(share)]
    up, mask = rotated_ups(ids, bits, matrix, here, share, every, ups + [piece for *_, piece in far], width)
    return final(low, theirs, base, up, mask)


def solution(mesh):
    return jax.shard_map(
        local,
        mesh=mesh,
        in_specs=(
            P(("grp", "adp"), "tp"),
            P(("grp", "adp"), None),
            P("tp", None),
            P("tp"),
            P("adp", "tp", None),
            P("adp", None, "tp"),
            P(),
        ),
        out_specs=P(("grp", "adp"), "tp"),
        check_vma=False,
    )
```

```python
import functools

import jax
import jax.numpy as jnp
import numpy as np
from jax import lax
from jax.experimental import pallas as pl
from jax.experimental.pallas import tpu as pltpu
from jax.sharding import PartitionSpec as P

VMEM = pl.BlockSpec(memory_space=pltpu.VMEM)
SMEM = pl.BlockSpec(memory_space=pltpu.SMEM)
F32, BF16 = jnp.float32, jnp.bfloat16
LAST = (((1,), (1,)), ((), ()))


def params(mib):
    return pltpu.CompilerParams(vmem_limit_bytes=mib << 20)


COST = pl.CostEstimate(flops=1, bytes_accessed=1, transcendentals=0)


def lasting(microseconds):
    return pl.CostEstimate(flops=int(microseconds * 1e9), bytes_accessed=1, transcendentals=0)


def hadamard(size):
    index = np.arange(size)
    shared = index[:, None] & index[None, :]
    parity = np.zeros_like(shared)
    while shared.any():
        parity, shared = parity ^ (shared & 1), shared >> 1
    return jnp.asarray(1 - 2 * parity, BF16)


def swap(x, axis, bit):
    return lax.ppermute(x, axis, [(i, i ^ bit) for i in range(lax.axis_size(axis))])


def together(*values):
    return lax.optimization_barrier(values)


def rotate(value, signs, matrix):
    head = matrix.shape[0]
    scale = signs * (1.0 / np.sqrt(head))
    turned = []
    for at in range(0, value.shape[1], head):
        signed = value[:, at : at + head] * scale
        high = signed.astype(BF16)
        rest = (signed - high.astype(F32)).astype(BF16)
        turned.append(
            jnp.dot(high, matrix, preferred_element_type=F32) + jnp.dot(rest, matrix, preferred_element_type=F32)
        )
    return turned


def partial_kernel(offsets, parts, tokens_ref, weight_ref, *refs):
    me, width = lax.axis_index("tp"), weight_ref.shape[1] // parts
    for offset, out_ref in zip(offsets, refs[-len(offsets) :]):
        at = pl.multiple_of(jnp.bitwise_xor(me, offset) * width, width)
        product = jnp.dot(tokens_ref[...], weight_ref[:, pl.ds(at, width)], preferred_element_type=F32)
        out_ref[...] = product.astype(BF16)


def partials(tokens, weight, parts, offsets, cost, *before):
    block = jax.ShapeDtypeStruct((tokens.shape[0], weight.shape[1] // parts), BF16)
    return pl.pallas_call(
        functools.partial(partial_kernel, offsets, parts),
        in_specs=[VMEM] * (2 + len(before)),
        out_specs=[VMEM] * len(offsets),
        out_shape=[block] * len(offsets),
        compiler_params=params(24),
        cost_estimate=cost,
        name="partials",
    )(tokens, weight, *before)


def add_kernel(*refs):
    total = refs[0][...].astype(F32)
    for ref in refs[1:-1]:
        total = total + ref[...].astype(F32)
    refs[-1][...] = total.astype(BF16)


def add(*terms):
    return pl.pallas_call(
        add_kernel,
        in_specs=[VMEM] * len(terms),
        out_specs=VMEM,
        out_shape=jax.ShapeDtypeStruct(terms[0].shape, BF16),
        compiler_params=params(16),
        cost_estimate=COST,
        name="add",
    )(*terms)


def base_kernel(scale_ref, bits_ref, matrix_ref, *refs):
    total = refs[0][...].astype(F32)
    for ref in refs[1:-1]:
        total = total + ref[...].astype(F32)
    signs = (1 - 2 * bits_ref[...]).astype(F32)
    refs[-1][...] = jnp.concatenate(rotate(total * scale_ref[...], signs, matrix_ref[...]), axis=1)


def rotated_base(terms, scale, bits, matrix):
    return pl.pallas_call(
        base_kernel,
        in_specs=[VMEM] * (3 + len(terms)),
        out_specs=VMEM,
        out_shape=jax.ShapeDtypeStruct(terms[0].shape, F32),
        compiler_params=params(16),
        cost_estimate=COST,
        name="rotated_base",
    )(scale, bits, matrix, *terms)


def adapter(here, share, name):
    z = lax.axis_index("adp")
    if name[0] == "plane":
        return jnp.bitwise_xor(z, name[1]) * here + name[2]
    plane, off, k = name
    return jnp.bitwise_xor(z, plane) * here + jnp.bitwise_xor(lax.axis_index("grp"), off) * share + k


def low_kernel(groups, here, share, rank, more, ids_ref, tokens_ref, *refs):
    out_ref = refs[-1]
    total = refs[-2][...] if more else None
    for (start, stop), terms in groups:
        rows = [refs[i][k, :, cut : cut + stop - start] for i, k, cut, _ in terms]
        joined = rows[0] if len(rows) == 1 else jnp.concatenate(rows, axis=0)
        product = lax.dot_general(joined, tokens_ref[:, start:stop], LAST, preferred_element_type=F32)
        for n, (_, _, _, name) in enumerate(terms):
            mine = ids_ref[...] == adapter(here, share, name)
            term = jnp.where(mine, product[n * rank : (n + 1) * rank], 0.0)
            total = term if total is None else total + term
    out_ref[...] = total.astype(out_ref.dtype)


def low_rows(ids, tokens, here, share, groups, arrays, before, dtype, cost=COST):
    rank = arrays[0].shape[1]
    more = [] if before is None else [before]
    return pl.pallas_call(
        functools.partial(low_kernel, groups, here, share, rank, bool(more)),
        in_specs=[VMEM] * (2 + len(arrays) + len(more)),
        out_specs=VMEM,
        out_shape=jax.ShapeDtypeStruct((rank, tokens.shape[0]), dtype),
        compiler_params=params(24),
        cost_estimate=cost,
        name="low_rows",
    )(ids, tokens, *arrays, *more)


def ups_kernel(terms, here, share, rank, ids_ref, bits_ref, matrix_ref, *refs):
    up_ref, mask_ref = refs[-2:]
    width = up_ref.shape[1]
    signs = (1 - 2 * bits_ref[...]).astype(F32)
    ids = jnp.broadcast_to(ids_ref[...], (rank, ids_ref.shape[1])).T
    for n, (i, k, cut, name) in enumerate(terms):
        turned = rotate(refs[i][k, :, cut : cut + width].astype(F32), signs, matrix_ref[...])
        up_ref[n * rank : (n + 1) * rank, :] = jnp.concatenate(turned, axis=1).astype(BF16)
        mine = ids == adapter(here, share, name)
        mask_ref[:, n * rank : (n + 1) * rank] = jnp.where(mine, 1.0, 0.0).astype(BF16)


def rotated_ups(ids, bits, matrix, here, share, terms, arrays, width):
    rank, rows = arrays[0].shape[1], ids.shape[1]
    every = len(terms) * rank
    return pl.pallas_call(
        functools.partial(ups_kernel, terms, here, share, rank),
        in_specs=[VMEM] * (3 + len(arrays)),
        out_specs=[VMEM, VMEM],
        out_shape=[jax.ShapeDtypeStruct((every, width), BF16), jax.ShapeDtypeStruct((rows, every), BF16)],
        compiler_params=params(32),
        cost_estimate=COST,
        name="rotated_ups",
    )(ids, bits, matrix, *arrays)


def final_kernel(mine_ref, theirs_ref, base_ref, up_ref, mask_ref, out_ref):
    low = (mine_ref[...].astype(F32) + theirs_ref[...].astype(F32)).T.astype(BF16)
    every = mask_ref.shape[1]
    spread = jnp.concatenate([low] * (every // low.shape[1]), axis=1) * mask_ref[...]
    delta = jnp.dot(spread, up_ref[...], preferred_element_type=F32)
    out_ref[...] = (base_ref[...] + delta).astype(BF16)


def final(mine, theirs, base, up, mask):
    rows, width = base.shape
    return pl.pallas_call(
        final_kernel,
        in_specs=[VMEM] * 5,
        out_specs=VMEM,
        out_shape=jax.ShapeDtypeStruct((rows, width), BF16),
        compiler_params=params(32),
        cost_estimate=COST,
        name="final",
    )(mine, theirs, base, up, mask)


def local(tokens, adapter_ids, base_weight, channel_scale, adapter_down, adapter_up, sign_bits):
    planes, groups, parts = lax.axis_size("adp"), lax.axis_size("grp"), lax.axis_size("tp")
    features = tokens.shape[1]
    here, _, rank = adapter_down.shape
    width = adapter_up.shape[2]
    share = here // groups
    matrix = hadamard(sign_bits.shape[0])
    bits, scale, ids = sign_bits[None, :], channel_scale[None, :], adapter_ids.T
    down = jnp.swapaxes(adapter_down, 1, 2)

    start = lax.axis_index("grp") * share
    own = lax.dynamic_slice_in_dim(down, start, share, 0)
    near = swap(own, "adp", 1)
    mine = [(0, jnp.concatenate([own, lax.dynamic_slice_in_dim(adapter_up, start, share, 0)], axis=2))]
    bit = planes // 2
    while bit > 1:
        mine += [(plane | bit, swap(piece, "adp", bit)) for plane, piece in mine]
        bit //= 2
    half = parts // 2
    offsets = (*range(1, parts, 2), *range(2, parts, 2))
    blocks = list(partials(tokens, base_weight, parts, offsets, lasting(4)))
    near, blocks[-1] = together(near, blocks[-1])
    (block,) = partials(tokens, base_weight, parts, (0,), COST, blocks[-1])
    close, block, *far = together(near, block, *(piece for _, piece in mine[1:]))
    blocks = blocks[:half] + [block] + blocks[half:]
    mine = mine[:1] + [(plane, piece) for (plane, _), piece in zip(mine[1:], far)]
    odd = [(1, near)] + [(plane | 1, swap(piece, "adp", 1)) for plane, piece in mine[1:]]

    def others(pieces):
        return [(plane, off, swap(piece, "grp", off)) for plane, piece in pieces for off in range(1, groups)]

    swapped = others(odd[:1]) + others(mine[1:]) + others(odd[1:])
    held = [(plane, 0, piece) for plane, piece in [(1, close)] + mine[1:] + odd[1:]]

    def terms(pieces, start):
        return [(start + i, k, 0, (plane, off, k)) for i, (plane, off, _) in enumerate(pieces) for k in range(share)]

    def more(low, pieces, dtype, cost=COST):
        arrays, every = [p for *_, p in pieces], terms(pieces, 0)
        if low is None:
            every += [(len(arrays), k, 0, ("plane", 0, k)) for k in range(here)]
            arrays = arrays + [down]
        return low_rows(ids, tokens, here, share, [((0, features), every)], arrays, low, dtype, cost)

    low = more(None, held[: len(mine)] + swapped[:1], F32, lasting(2))
    low, *came = together(low, *(swap(block, "tp", 1) for block in blocks[:half]))

    rest = held[len(mine) :]
    low = more(low, swapped[1:-1] + rest, F32, lasting(5))
    low, up = together(low, adapter_up)
    ups = [adapter_up, swap(up, "adp", 1)]

    sums = [[block, pair] for block, pair in zip(blocks[half:], came)]
    bit = 2
    while bit < parts:
        came = [swap(add(*terms), "tp", bit) for terms in sums[1::2]]
        sums = [terms + [pair] for terms, pair in zip(sums[0::2], came)]
        bit *= 2
    base = rotated_base(sums[0], scale, bits, matrix)

    low, ups[1] = together(low, ups[1])
    low = more(low, swapped[-1:], BF16)
    bit = 1
    while bit < parts // 2:
        low = add(low, swap(low, "tp", bit))
        bit *= 2
    theirs = swap(low, "tp", bit)


    far = [one for one in held + swapped if one[0] > 1]
    every = [(plane, k, 0, ("plane", plane, k)) for plane in (0, 1) for k in range(here)]
    every += [(2 + i, k, features, (plane, off, k)) for i, (plane, off, _) in enumerate(far) for k in range(share)]
    up, mask = rotated_ups(ids, bits, matrix, here, share, every, ups + [piece for *_, piece in far], width)
    return final(low, theirs, base, up, mask)


def solution(mesh):
    return jax.shard_map(
        local,
        mesh=mesh,
        in_specs=(
            P(("grp", "adp"), "tp"),
            P(("grp", "adp"), None),
            P("tp", None),
            P("tp"),
            P("adp", "tp", None),
            P("adp", None, "tp"),
            P(),
        ),
        out_specs=P(("grp", "adp"), "tp"),
        check_vma=False,
    )
```

```python
import functools

import jax
import jax.numpy as jnp
import numpy as np
from jax import lax
from jax.experimental import pallas as pl
from jax.experimental.pallas import tpu as pltpu
from jax.sharding import PartitionSpec as P

VMEM = pl.BlockSpec(memory_space=pltpu.VMEM)
SMEM = pl.BlockSpec(memory_space=pltpu.SMEM)
F32, BF16 = jnp.float32, jnp.bfloat16
LAST = (((1,), (1,)), ((), ()))


def params(mib):
    return pltpu.CompilerParams(vmem_limit_bytes=mib << 20)


COST = pl.CostEstimate(flops=1, bytes_accessed=1, transcendentals=0)


def lasting(microseconds):
    return pl.CostEstimate(flops=int(microseconds * 1e9), bytes_accessed=1, transcendentals=0)


def hadamard(size):
    index = np.arange(size)
    shared = index[:, None] & index[None, :]
    parity = np.zeros_like(shared)
    while shared.any():
        parity, shared = parity ^ (shared & 1), shared >> 1
    return jnp.asarray(1 - 2 * parity, BF16)


def swap(x, axis, bit):
    return lax.ppermute(x, axis, [(i, i ^ bit) for i in range(lax.axis_size(axis))])


def together(*values):
    return lax.optimization_barrier(values)


def rotate(value, signs, matrix):
    head = matrix.shape[0]
    scale = signs * (1.0 / np.sqrt(head))
    turned = []
    for at in range(0, value.shape[1], head):
        signed = value[:, at : at + head] * scale
        high = signed.astype(BF16)
        rest = (signed - high.astype(F32)).astype(BF16)
        turned.append(
            jnp.dot(high, matrix, preferred_element_type=F32) + jnp.dot(rest, matrix, preferred_element_type=F32)
        )
    return turned


def partial_kernel(offsets, parts, tokens_ref, weight_ref, *refs):
    me, width = lax.axis_index("tp"), weight_ref.shape[1] // parts
    for offset, out_ref in zip(offsets, refs[-len(offsets) :]):
        at = pl.multiple_of(jnp.bitwise_xor(me, offset) * width, width)
        product = jnp.dot(tokens_ref[...], weight_ref[:, pl.ds(at, width)], preferred_element_type=F32)
        out_ref[...] = product.astype(BF16)


def partials(tokens, weight, parts, offsets, cost, *before):
    block = jax.ShapeDtypeStruct((tokens.shape[0], weight.shape[1] // parts), BF16)
    return pl.pallas_call(
        functools.partial(partial_kernel, offsets, parts),
        in_specs=[VMEM] * (2 + len(before)),
        out_specs=[VMEM] * len(offsets),
        out_shape=[block] * len(offsets),
        compiler_params=params(24),
        cost_estimate=cost,
        name="partials",
    )(tokens, weight, *before)


def add_kernel(*refs):
    total = refs[0][...].astype(F32)
    for ref in refs[1:-1]:
        total = total + ref[...].astype(F32)
    refs[-1][...] = total.astype(BF16)


def add(*terms):
    return pl.pallas_call(
        add_kernel,
        in_specs=[VMEM] * len(terms),
        out_specs=VMEM,
        out_shape=jax.ShapeDtypeStruct(terms[0].shape, BF16),
        compiler_params=params(16),
        cost_estimate=COST,
        name="add",
    )(*terms)


def adapter(here, share, name):
    z = lax.axis_index("adp")
    if name[0] == "plane":
        return jnp.bitwise_xor(z, name[1]) * here + name[2]
    plane, off, k = name
    return jnp.bitwise_xor(z, plane) * here + jnp.bitwise_xor(lax.axis_index("grp"), off) * share + k


def low_kernel(groups, here, share, rank, more, ids_ref, tokens_ref, *refs):
    out_ref = refs[-1]
    total = refs[-2][...] if more else None
    for (start, stop), terms in groups:
        rows = [refs[i][k, :, cut : cut + stop - start] for i, k, cut, _ in terms]
        joined = rows[0] if len(rows) == 1 else jnp.concatenate(rows, axis=0)
        product = lax.dot_general(joined, tokens_ref[:, start:stop], LAST, preferred_element_type=F32)
        for n, (_, _, _, name) in enumerate(terms):
            mine = ids_ref[...] == adapter(here, share, name)
            term = jnp.where(mine, product[n * rank : (n + 1) * rank], 0.0)
            total = term if total is None else total + term
    out_ref[...] = total.astype(out_ref.dtype)


def low_rows(ids, tokens, here, share, groups, arrays, before, dtype, cost=COST):
    rank = arrays[0].shape[1]
    more = [] if before is None else [before]
    return pl.pallas_call(
        functools.partial(low_kernel, groups, here, share, rank, bool(more)),
        in_specs=[VMEM] * (2 + len(arrays) + len(more)),
        out_specs=VMEM,
        out_shape=jax.ShapeDtypeStruct((rank, tokens.shape[0]), dtype),
        compiler_params=params(24),
        cost_estimate=cost,
        name="low_rows",
    )(ids, tokens, *arrays, *more)


def ups_kernel(named, terms, here, share, rank, ids_ref, bits_ref, matrix_ref, *refs):
    up_ref, mask_ref = refs[-2:]
    width = up_ref.shape[1]
    signs = (1 - 2 * bits_ref[...]).astype(F32)
    for n, (i, k, cut) in enumerate(terms):
        turned = rotate(refs[i][k, :, cut : cut + width].astype(F32), signs, matrix_ref[...])
        up_ref[n * rank : (n + 1) * rank, :] = jnp.concatenate(turned, axis=1).astype(BF16)
    ids = jnp.broadcast_to(ids_ref[...], (rank, ids_ref.shape[1])).T
    mask_ref[...] = jnp.zeros_like(mask_ref)
    for n, name in enumerate(named):
        mine = ids == adapter(here, share, name)
        mask_ref[:, n * rank : (n + 1) * rank] = jnp.where(mine, 1.0, 0.0).astype(BF16)


def rotated_ups(ids, bits, matrix, here, share, named, terms, arrays, width):
    rank, rows = arrays[0].shape[1], ids.shape[1]
    columns = -(-len(named) * rank // 128) * 128
    return pl.pallas_call(
        functools.partial(ups_kernel, named, terms, here, share, rank),
        in_specs=[VMEM] * (3 + len(arrays)),
        out_specs=[VMEM, VMEM],
        out_shape=[jax.ShapeDtypeStruct((len(terms) * rank, width), BF16), jax.ShapeDtypeStruct((rows, columns), BF16)],
        compiler_params=params(32),
        cost_estimate=COST,
        name="rotated_ups",
    )(ids, bits, matrix, *arrays)


def pick_kernel(named, here, share, ids_ref, pick_ref):
    rows, slots = pick_ref.shape[0], pick_ref.shape[1] // len(named)
    earlier = lax.broadcasted_iota(jnp.int32, (rows, rows), 0) < lax.broadcasted_iota(jnp.int32, (rows, rows), 1)
    earlier = jnp.where(earlier, 1.0, 0.0).astype(BF16)
    ids = jnp.broadcast_to(ids_ref[...], (8, rows))
    for k, name in enumerate(named):
        mine = ids == adapter(here, share, name)
        rank = jnp.dot(jnp.where(mine, 1.0, 0.0).astype(BF16), earlier, preferred_element_type=F32)
        rank = jnp.where(mine, rank, -1.0)
        rank = jnp.broadcast_to(rank[:1], (128, rows)).T
        for at in range(0, slots, 128):
            slot = (lax.broadcasted_iota(jnp.int32, (rows, 128), 1) + at).astype(F32)
            pick_ref[:, k * slots + at : k * slots + at + 128] = jnp.where(rank == slot, 1.0, 0.0).astype(BF16)


def picked(ids, here, share, named, slots):
    return pl.pallas_call(
        functools.partial(pick_kernel, named, here, share),
        in_specs=[VMEM],
        out_specs=VMEM,
        out_shape=jax.ShapeDtypeStruct((ids.shape[1], len(named) * slots), BF16),
        compiler_params=params(24),
        cost_estimate=COST,
        name="picked",
    )(ids)


def compact_kernel(tokens_ref, piece_ref, pick_ref, out_ref):
    share, features = piece_ref.shape[0], tokens_ref.shape[1]
    slots = pick_ref.shape[1] // share
    for k in range(share):
        product = lax.dot_general(piece_ref[k, :, :features], tokens_ref[...], LAST, preferred_element_type=F32)
        columns = slice(k * slots, (k + 1) * slots)
        kept = jnp.dot(product.astype(BF16), pick_ref[:, columns], preferred_element_type=F32)
        out_ref[:, columns] = kept.astype(BF16)


def compact(tokens, piece, pick):
    return pl.pallas_call(
        compact_kernel,
        in_specs=[VMEM] * 3,
        out_specs=VMEM,
        out_shape=jax.ShapeDtypeStruct((piece.shape[1], pick.shape[1]), BF16),
        compiler_params=params(24),
        cost_estimate=COST,
        name="compact",
    )(tokens, piece, pick)


def most_kernel(mine_ref, theirs_ref, up_ref, mask_ref, near_ref, scale_ref, bits_ref, matrix_ref, *refs):
    low = (mine_ref[...].astype(F32) + theirs_ref[...].astype(F32)).astype(BF16).T
    rank, columns = low.shape[1], mask_ref.shape[1]
    signs = (1 - 2 * bits_ref[...]).astype(F32)
    ups = [up_ref[...]]
    for k in range(near_ref.shape[0]):
        turned = rotate(near_ref[k].astype(F32), signs, matrix_ref[...])
        ups.append(jnp.concatenate(turned, axis=1).astype(BF16))
    missing = columns - sum(up.shape[0] for up in ups)
    if missing:
        ups.append(jnp.zeros((missing, up_ref.shape[1]), BF16))
    spread = jnp.concatenate([low] * (columns // rank), axis=1) * mask_ref[...]
    delta = jnp.dot(spread, jnp.concatenate(ups, axis=0), preferred_element_type=F32)
    value = functools.reduce(jnp.add, [ref[...].astype(F32) for ref in refs[:-1]]) * scale_ref[...]
    refs[-1][...] = jnp.concatenate(rotate(value, signs, matrix_ref[...]), axis=1) + delta


def most(mine, theirs, up, mask, near, scale, bits, matrix, terms):
    return pl.pallas_call(
        most_kernel,
        in_specs=[VMEM] * (8 + len(terms)),
        out_specs=VMEM,
        out_shape=jax.ShapeDtypeStruct(terms[0].shape, F32),
        compiler_params=params(32),
        cost_estimate=COST,
        name="most",
    )(mine, theirs, up, mask, near, scale, bits, matrix, *terms)


def final_kernel(mine_ref, theirs_ref, pick_ref, piece_ref, bits_ref, matrix_ref, most_ref, out_ref):
    share, width = piece_ref.shape[0], out_ref.shape[1]
    features, slots = piece_ref.shape[2] - width, pick_ref.shape[1] // share
    signs = (1 - 2 * bits_ref[...]).astype(F32)
    low = (mine_ref[...].astype(F32) + theirs_ref[...].astype(F32)).astype(BF16).T
    deltas = []
    for k in range(share):
        turned = rotate(piece_ref[k, :, features:].astype(F32), signs, matrix_ref[...])
        up = jnp.concatenate(turned, axis=1).astype(BF16)
        deltas.append(jnp.dot(low[k * slots : (k + 1) * slots], up, preferred_element_type=F32).astype(BF16))
    delta = deltas[0] if share == 1 else jnp.concatenate(deltas, axis=0)
    result = most_ref[...] + jnp.dot(pick_ref[...], delta, preferred_element_type=F32)
    out_ref[...] = result.astype(BF16)


def final(mine, theirs, pick, piece, bits, matrix, rest):
    return pl.pallas_call(
        final_kernel,
        in_specs=[VMEM] * 7,
        out_specs=VMEM,
        out_shape=jax.ShapeDtypeStruct(rest.shape, BF16),
        compiler_params=params(32),
        cost_estimate=COST,
        name="final",
    )(mine, theirs, pick, piece, bits, matrix, rest)


def local(tokens, adapter_ids, base_weight, channel_scale, adapter_down, adapter_up, sign_bits):
    planes, groups, parts = lax.axis_size("adp"), lax.axis_size("grp"), lax.axis_size("tp")
    features = tokens.shape[1]
    here, _, rank = adapter_down.shape
    width = adapter_up.shape[2]
    share = here // groups
    matrix = hadamard(sign_bits.shape[0])
    bits, scale, ids = sign_bits[None, :], channel_scale[None, :], adapter_ids.T
    down = jnp.swapaxes(adapter_down, 1, 2)

    start = lax.axis_index("grp") * share
    own = lax.dynamic_slice_in_dim(down, start, share, 0)
    near = swap(own, "adp", 1)
    mine = [(0, jnp.concatenate([own, lax.dynamic_slice_in_dim(adapter_up, start, share, 0)], axis=2))]
    bit = planes // 2
    while bit > 1:
        mine += [(plane | bit, swap(piece, "adp", bit)) for plane, piece in mine]
        bit //= 2
    half = parts // 2
    offsets = (*range(1, parts, 2), *range(2, parts, 2))
    blocks = list(partials(tokens, base_weight, parts, offsets, lasting(4)))
    near, blocks[-1] = together(near, blocks[-1])
    (block,) = partials(tokens, base_weight, parts, (0,), COST, blocks[-1])
    close, block, *far = together(near, block, *(piece for _, piece in mine[1:]))
    blocks = blocks[:half] + [block] + blocks[half:]
    mine = mine[:1] + [(plane, piece) for (plane, _), piece in zip(mine[1:], far)]
    odd = [(1, near)] + [(plane | 1, swap(piece, "adp", 1)) for plane, piece in mine[1:]]

    def others(pieces):
        return [(plane, off, swap(piece, "grp", off)) for plane, piece in pieces for off in range(1, groups)]

    swapped = others(odd[:1]) + others(mine[1:]) + others(odd[1:])
    held = [(plane, 0, piece) for plane, piece in [(1, close)] + mine[1:] + odd[1:]]

    def terms(pieces, start):
        return [(start + i, k, 0, (plane, off, k)) for i, (plane, off, _) in enumerate(pieces) for k in range(share)]

    def more(low, pieces, dtype, cost=COST):
        arrays, every = [p for *_, p in pieces], terms(pieces, 0)
        if low is None:
            every += [(len(arrays), k, 0, ("plane", 0, k)) for k in range(here)]
            arrays = arrays + [down]
        return low_rows(ids, tokens, here, share, [((0, features), every)], arrays, low, dtype, cost)

    low = more(None, held[: len(mine)] + swapped[:1], F32, lasting(2))
    slots = -(-2 * tokens.shape[0] // (here * planes) // 128) * 128
    last = swapped[-1]
    pick = picked(ids, here, share, [(last[0], last[1], k) for k in range(share)], slots)
    low, pick, *came = together(low, pick, *(swap(block, "tp", 1) for block in blocks[:half]))

    def both(low):
        bit = 1
        while bit < parts // 2:
            low = add(low, swap(low, "tp", bit))
            bit *= 2
        return low, swap(low, "tp", bit)

    rest = held[len(mine) :]
    low = more(low, swapped[1:-1] + rest, BF16, lasting(5))
    low, up = together(low, adapter_up)
    near_up = swap(up, "adp", 1)
    low, other = both(low)

    sums = [[block, pair] for block, pair in zip(blocks[half:], came)]
    bit = 2
    while bit < parts:
        came = [swap(add(*terms), "tp", bit) for terms in sums[1::2]]
        sums = [terms + [pair] for terms, pair in zip(sums[0::2], came)]
        bit *= 2

    far = [one for one in held + swapped[:-1] if one[0] > 1]
    named = [("plane", 0, k) for k in range(here)]
    named += [(plane, off, k) for plane, off, _ in far for k in range(share)]
    ups = [(0, k, 0) for k in range(here)] + [(1 + i, k, features) for i in range(len(far)) for k in range(share)]
    named += [("plane", 1, k) for k in range(here)]
    arrays = [adapter_up] + [piece for *_, piece in far]
    up, mask = rotated_ups(ids, bits, matrix, here, share, named, ups, arrays, width)

    piece, up, mask, near_up = together(last[2], up, mask, near_up)
    kept, more_kept = both(compact(tokens, piece, pick))
    rest = most(low, other, up, mask, near_up, scale, bits, matrix, sums[0])
    return final(kept, more_kept, pick, piece, bits, matrix, rest)


def solution(mesh):
    return jax.shard_map(
        local,
        mesh=mesh,
        in_specs=(
            P(("grp", "adp"), "tp"),
            P(("grp", "adp"), None),
            P("tp", None),
            P("tp"),
            P("adp", "tp", None),
            P("adp", None, "tp"),
            P(),
        ),
        out_specs=P(("grp", "adp"), "tp"),
        check_vma=False,
    )
```

```python
import functools

import jax
import jax.numpy as jnp
import numpy as np
from jax import lax
from jax.experimental import pallas as pl
from jax.experimental.pallas import tpu as pltpu
from jax.sharding import PartitionSpec as P

VMEM = pl.BlockSpec(memory_space=pltpu.VMEM)
SMEM = pl.BlockSpec(memory_space=pltpu.SMEM)
F32, BF16 = jnp.float32, jnp.bfloat16
LAST = (((1,), (1,)), ((), ()))


def params(mib):
    return pltpu.CompilerParams(vmem_limit_bytes=mib << 20)


COST = pl.CostEstimate(flops=1, bytes_accessed=1, transcendentals=0)


def lasting(microseconds):
    return pl.CostEstimate(flops=int(microseconds * 1e9), bytes_accessed=1, transcendentals=0)


def hadamard(size):
    index = np.arange(size)
    shared = index[:, None] & index[None, :]
    parity = np.zeros_like(shared)
    while shared.any():
        parity, shared = parity ^ (shared & 1), shared >> 1
    return jnp.asarray(1 - 2 * parity, BF16)


def swap(x, axis, bit):
    return lax.ppermute(x, axis, [(i, i ^ bit) for i in range(lax.axis_size(axis))])


def together(*values):
    return lax.optimization_barrier(values)


def rotate(value, signs, matrix):
    head = matrix.shape[0]
    scale = signs * (1.0 / np.sqrt(head))
    turned = []
    for at in range(0, value.shape[1], head):
        signed = value[:, at : at + head] * scale
        high = signed.astype(BF16)
        rest = (signed - high.astype(F32)).astype(BF16)
        turned.append(
            jnp.dot(high, matrix, preferred_element_type=F32) + jnp.dot(rest, matrix, preferred_element_type=F32)
        )
    return turned


def partial_kernel(offsets, parts, tokens_ref, weight_ref, *refs):
    me, width = lax.axis_index("tp"), weight_ref.shape[1] // parts
    for offset, out_ref in zip(offsets, refs[-len(offsets) :]):
        at = pl.multiple_of(jnp.bitwise_xor(me, offset) * width, width)
        product = jnp.dot(tokens_ref[...], weight_ref[:, pl.ds(at, width)], preferred_element_type=F32)
        out_ref[...] = product.astype(BF16)


def partials(tokens, weight, parts, offsets, cost, *before):
    block = jax.ShapeDtypeStruct((tokens.shape[0], weight.shape[1] // parts), BF16)
    return pl.pallas_call(
        functools.partial(partial_kernel, offsets, parts),
        in_specs=[VMEM] * (2 + len(before)),
        out_specs=[VMEM] * len(offsets),
        out_shape=[block] * len(offsets),
        compiler_params=params(24),
        cost_estimate=cost,
        name="partials",
    )(tokens, weight, *before)


def add_kernel(*refs):
    total = refs[0][...].astype(F32)
    for ref in refs[1:-1]:
        total = total + ref[...].astype(F32)
    refs[-1][...] = total.astype(BF16)


def add(*terms):
    return pl.pallas_call(
        add_kernel,
        in_specs=[VMEM] * len(terms),
        out_specs=VMEM,
        out_shape=jax.ShapeDtypeStruct(terms[0].shape, BF16),
        compiler_params=params(16),
        cost_estimate=COST,
        name="add",
    )(*terms)


def adapter(here, share, name):
    z = lax.axis_index("adp")
    if name[0] == "plane":
        return jnp.bitwise_xor(z, name[1]) * here + name[2]
    plane, off, k = name
    return jnp.bitwise_xor(z, plane) * here + jnp.bitwise_xor(lax.axis_index("grp"), off) * share + k


def low_kernel(groups, here, share, rank, more, ids_ref, tokens_ref, *refs):
    out_ref = refs[-1]
    total = refs[-2][...] if more else None
    for (start, stop), terms in groups:
        rows = [refs[i][k, :, cut : cut + stop - start] for i, k, cut, _ in terms]
        joined = rows[0] if len(rows) == 1 else jnp.concatenate(rows, axis=0)
        product = lax.dot_general(joined, tokens_ref[:, start:stop], LAST, preferred_element_type=F32)
        for n, (_, _, _, name) in enumerate(terms):
            mine = ids_ref[...] == adapter(here, share, name)
            term = jnp.where(mine, product[n * rank : (n + 1) * rank], 0.0)
            total = term if total is None else total + term
    out_ref[...] = total.astype(out_ref.dtype)


def low_rows(ids, tokens, here, share, groups, arrays, before, dtype, cost=COST):
    rank = arrays[0].shape[1]
    more = [] if before is None else [before]
    return pl.pallas_call(
        functools.partial(low_kernel, groups, here, share, rank, bool(more)),
        in_specs=[VMEM] * (2 + len(arrays) + len(more)),
        out_specs=VMEM,
        out_shape=jax.ShapeDtypeStruct((rank, tokens.shape[0]), dtype),
        compiler_params=params(24),
        cost_estimate=cost,
        name="low_rows",
    )(ids, tokens, *arrays, *more)


def ups_kernel(named, terms, here, share, rank, ids_ref, bits_ref, matrix_ref, *refs):
    up_ref, mask_ref = refs[-2:]
    width = up_ref.shape[1]
    up_ref[...] = jnp.zeros_like(up_ref)
    signs = (1 - 2 * bits_ref[...]).astype(F32)
    for n, (i, k, cut) in enumerate(terms):
        turned = rotate(refs[i][k, :, cut : cut + width].astype(F32), signs, matrix_ref[...])
        up_ref[n * rank : (n + 1) * rank, :] = jnp.concatenate(turned, axis=1).astype(BF16)
    ids = jnp.broadcast_to(ids_ref[...], (rank, ids_ref.shape[1])).T
    mask_ref[...] = jnp.zeros_like(mask_ref)
    for n, name in enumerate(named):
        mine = ids == adapter(here, share, name)
        mask_ref[:, n * rank : (n + 1) * rank] = jnp.where(mine, 1.0, 0.0).astype(BF16)


def rotated_ups(ids, bits, matrix, here, share, named, terms, arrays, width):
    rank, rows = arrays[0].shape[1], ids.shape[1]
    columns = -(-len(named) * rank // 128) * 128
    return pl.pallas_call(
        functools.partial(ups_kernel, named, terms, here, share, rank),
        in_specs=[VMEM] * (3 + len(arrays)),
        out_specs=[VMEM, VMEM],
        out_shape=[jax.ShapeDtypeStruct((columns, width), BF16), jax.ShapeDtypeStruct((rows, columns), BF16)],
        compiler_params=params(32),
        cost_estimate=COST,
        name="rotated_ups",
    )(ids, bits, matrix, *arrays)


def pick_kernel(named, here, share, ids_ref, pick_ref):
    rows, slots = pick_ref.shape[0], pick_ref.shape[1] // len(named)
    earlier = lax.broadcasted_iota(jnp.int32, (rows, rows), 0) < lax.broadcasted_iota(jnp.int32, (rows, rows), 1)
    earlier = jnp.where(earlier, 1.0, 0.0).astype(BF16)
    ids = jnp.broadcast_to(ids_ref[...], (8, rows))
    for k, name in enumerate(named):
        mine = ids == adapter(here, share, name)
        rank = jnp.dot(jnp.where(mine, 1.0, 0.0).astype(BF16), earlier, preferred_element_type=F32)
        rank = jnp.where(mine, rank, -1.0)
        rank = jnp.broadcast_to(rank[:1], (128, rows)).T
        for at in range(0, slots, 128):
            slot = (lax.broadcasted_iota(jnp.int32, (rows, 128), 1) + at).astype(F32)
            pick_ref[:, k * slots + at : k * slots + at + 128] = jnp.where(rank == slot, 1.0, 0.0).astype(BF16)


def picked(ids, here, share, named, slots):
    return pl.pallas_call(
        functools.partial(pick_kernel, named, here, share),
        in_specs=[VMEM],
        out_specs=VMEM,
        out_shape=jax.ShapeDtypeStruct((ids.shape[1], len(named) * slots), BF16),
        compiler_params=params(24),
        cost_estimate=COST,
        name="picked",
    )(ids)


def compact_kernel(tokens_ref, piece_ref, pick_ref, out_ref):
    share, features = piece_ref.shape[0], tokens_ref.shape[1]
    slots = pick_ref.shape[1] // share
    for k in range(share):
        product = lax.dot_general(piece_ref[k, :, :features], tokens_ref[...], LAST, preferred_element_type=F32)
        columns = slice(k * slots, (k + 1) * slots)
        kept = jnp.dot(product.astype(BF16), pick_ref[:, columns], preferred_element_type=F32)
        out_ref[:, columns] = kept.astype(BF16)


def compact(tokens, piece, pick):
    return pl.pallas_call(
        compact_kernel,
        in_specs=[VMEM] * 3,
        out_specs=VMEM,
        out_shape=jax.ShapeDtypeStruct((piece.shape[1], pick.shape[1]), BF16),
        compiler_params=params(24),
        cost_estimate=COST,
        name="compact",
    )(tokens, piece, pick)


def most_kernel(mine_ref, theirs_ref, up_ref, mask_ref, scale_ref, bits_ref, matrix_ref, *refs):
    low = (mine_ref[...].astype(F32) + theirs_ref[...].astype(F32)).astype(BF16).T
    rank, columns = low.shape[1], mask_ref.shape[1]
    signs = (1 - 2 * bits_ref[...]).astype(F32)
    spread = jnp.concatenate([low] * (columns // rank), axis=1) * mask_ref[...]
    delta = jnp.dot(spread, up_ref[...], preferred_element_type=F32)
    value = functools.reduce(jnp.add, [ref[...].astype(F32) for ref in refs[:-1]]) * scale_ref[...]
    refs[-1][...] = jnp.concatenate(rotate(value, signs, matrix_ref[...]), axis=1) + delta


def most(mine, theirs, up, mask, scale, bits, matrix, terms):
    return pl.pallas_call(
        most_kernel,
        in_specs=[VMEM] * (7 + len(terms)),
        out_specs=VMEM,
        out_shape=jax.ShapeDtypeStruct(terms[0].shape, F32),
        compiler_params=params(32),
        cost_estimate=COST,
        name="most",
    )(mine, theirs, up, mask, scale, bits, matrix, *terms)


def final_kernel(pick_ref, piece_ref, bits_ref, matrix_ref, most_ref, *refs):
    kept_refs, out_ref = refs[:-1], refs[-1]
    share, width = piece_ref.shape[0], out_ref.shape[1]
    features, slots = piece_ref.shape[2] - width, pick_ref.shape[1] // share
    signs = (1 - 2 * bits_ref[...]).astype(F32)
    low = functools.reduce(jnp.add, [ref[...].astype(F32) for ref in kept_refs]).astype(BF16).T
    deltas = []
    for k in range(share):
        turned = rotate(piece_ref[k, :, features:].astype(F32), signs, matrix_ref[...])
        up = jnp.concatenate(turned, axis=1).astype(BF16)
        deltas.append(jnp.dot(low[k * slots : (k + 1) * slots], up, preferred_element_type=F32).astype(BF16))
    delta = deltas[0] if share == 1 else jnp.concatenate(deltas, axis=0)
    result = most_ref[...] + jnp.dot(pick_ref[...], delta, preferred_element_type=F32)
    out_ref[...] = result.astype(BF16)


def final(kept, pick, piece, bits, matrix, rest):
    return pl.pallas_call(
        final_kernel,
        in_specs=[VMEM] * (5 + len(kept)),
        out_specs=VMEM,
        out_shape=jax.ShapeDtypeStruct(rest.shape, BF16),
        compiler_params=params(32),
        cost_estimate=COST,
        name="final",
    )(pick, piece, bits, matrix, rest, *kept)


def local(tokens, adapter_ids, base_weight, channel_scale, adapter_down, adapter_up, sign_bits):
    planes, groups, parts = lax.axis_size("adp"), lax.axis_size("grp"), lax.axis_size("tp")
    features = tokens.shape[1]
    here, _, rank = adapter_down.shape
    width = adapter_up.shape[2]
    share = here // groups
    matrix = hadamard(sign_bits.shape[0])
    bits, scale, ids = sign_bits[None, :], channel_scale[None, :], adapter_ids.T
    down = jnp.swapaxes(adapter_down, 1, 2)

    start = lax.axis_index("grp") * share
    own = jnp.concatenate([lax.dynamic_slice_in_dim(a, start, share, 0) for a in (down, adapter_up)], axis=2)
    near = swap(own, "adp", 1)
    mine = [(0, own)]
    bit = planes // 2
    while bit > 1:
        mine += [(plane | bit, swap(piece, "adp", bit)) for plane, piece in mine]
        bit //= 2
    half = parts // 2
    offsets = (*range(1, parts, 2), *range(2, parts, 2))
    blocks = list(partials(tokens, base_weight, parts, offsets, lasting(4)))
    near, blocks[-1] = together(near, blocks[-1])
    (block,) = partials(tokens, base_weight, parts, (0,), COST, blocks[-1])
    close, block, *far = together(near, block, *(piece for _, piece in mine[1:]))
    blocks = blocks[:half] + [block] + blocks[half:]
    mine = mine[:1] + [(plane, piece) for (plane, _), piece in zip(mine[1:], far)]
    odd = [(1, near)] + [(plane | 1, swap(piece, "adp", 1)) for plane, piece in mine[1:]]

    def others(pieces):
        return [(plane, off, swap(piece, "grp", off)) for plane, piece in pieces for off in range(1, groups)]

    swapped = others(odd[:1]) + others(mine[1:]) + others(odd[1:])
    held = [(plane, 0, piece) for plane, piece in [(1, close)] + mine[1:] + odd[1:]]

    def terms(pieces, start):
        return [(start + i, k, 0, (plane, off, k)) for i, (plane, off, _) in enumerate(pieces) for k in range(share)]

    def more(low, pieces, dtype, cost=COST):
        arrays, every = [p for *_, p in pieces], terms(pieces, 0)
        if low is None:
            every += [(len(arrays), k, 0, ("plane", 0, k)) for k in range(here)]
            arrays = arrays + [down]
        return low_rows(ids, tokens, here, share, [((0, features), every)], arrays, low, dtype, cost)

    low = more(None, held[: len(mine)] + swapped[:1], F32, lasting(2))
    slots = -(-2 * tokens.shape[0] // (here * planes) // 128) * 128
    last = swapped[-1]
    pick = picked(ids, here, share, [(last[0], last[1], k) for k in range(share)], slots)
    low, pick, *came = together(low, pick, *(swap(block, "tp", 1) for block in blocks[:half]))

    def both(low):
        bit = 1
        while bit < parts // 2:
            low = add(low, swap(low, "tp", bit))
            bit *= 2
        return low, swap(low, "tp", bit)

    rest = held[len(mine) :]
    low = more(low, swapped[1:-1] + rest, BF16, lasting(5))
    low, other = both(low)

    sums = [[block, pair] for block, pair in zip(blocks[half:], came)]
    bit = 2
    while bit < parts:
        came = [swap(add(*terms), "tp", bit) for terms in sums[1::2]]
        sums = [terms + [pair] for terms, pair in zip(sums[0::2], came)]
        bit *= 2

    far = held + swapped[:-1]
    named = [("plane", 0, k) for k in range(here)]
    named += [(plane, off, k) for plane, off, _ in far for k in range(share)]
    ups = [(0, k, 0) for k in range(here)] + [(1 + i, k, features) for i in range(len(far)) for k in range(share)]
    arrays = [adapter_up] + [piece for *_, piece in far]
    up, mask = rotated_ups(ids, bits, matrix, here, share, named, ups, arrays, width)

    piece, up, mask = together(last[2], up, mask)
    kept = compact(tokens, piece, pick)
    kept = [kept] + [swap(kept, "tp", offset) for offset in range(1, parts)]
    rest = most(low, other, up, mask, scale, bits, matrix, sums[0])
    return final(kept, pick, piece, bits, matrix, rest)


def solution(mesh):
    return jax.shard_map(
        local,
        mesh=mesh,
        in_specs=(
            P(("grp", "adp"), "tp"),
            P(("grp", "adp"), None),
            P("tp", None),
            P("tp"),
            P("adp", "tp", None),
            P("adp", None, "tp"),
            P(),
        ),
        out_specs=P(("grp", "adp"), "tp"),
        check_vma=False,
    )
```

```python
import functools

import jax
import jax.numpy as jnp
import numpy as np
from jax import lax
from jax.experimental import pallas as pl
from jax.experimental.pallas import tpu as pltpu
from jax.sharding import PartitionSpec as P

VMEM = pl.BlockSpec(memory_space=pltpu.VMEM)
SMEM = pl.BlockSpec(memory_space=pltpu.SMEM)
F32, BF16 = jnp.float32, jnp.bfloat16
LAST = (((1,), (1,)), ((), ()))


def params(mib):
    return pltpu.CompilerParams(vmem_limit_bytes=mib << 20)


COST = pl.CostEstimate(flops=1, bytes_accessed=1, transcendentals=0)


def lasting(microseconds):
    return pl.CostEstimate(flops=int(microseconds * 1e9), bytes_accessed=1, transcendentals=0)


def hadamard(size):
    index = np.arange(size)
    shared = index[:, None] & index[None, :]
    parity = np.zeros_like(shared)
    while shared.any():
        parity, shared = parity ^ (shared & 1), shared >> 1
    return jnp.asarray(1 - 2 * parity, BF16)


def swap(x, axis, bit):
    return lax.ppermute(x, axis, [(i, i ^ bit) for i in range(lax.axis_size(axis))])


def together(*values):
    return lax.optimization_barrier(values)


def rotate(value, signs, matrix):
    head = matrix.shape[0]
    scale = signs * (1.0 / np.sqrt(head))
    turned = []
    for at in range(0, value.shape[1], head):
        signed = value[:, at : at + head] * scale
        high = signed.astype(BF16)
        rest = (signed - high.astype(F32)).astype(BF16)
        turned.append(
            jnp.dot(high, matrix, preferred_element_type=F32) + jnp.dot(rest, matrix, preferred_element_type=F32)
        )
    return turned


def partial_kernel(offsets, parts, tokens_ref, weight_ref, *refs):
    me, width = lax.axis_index("tp"), weight_ref.shape[1] // parts
    for offset, out_ref in zip(offsets, refs[-len(offsets) :]):
        at = pl.multiple_of(jnp.bitwise_xor(me, offset) * width, width)
        product = jnp.dot(tokens_ref[...], weight_ref[:, pl.ds(at, width)], preferred_element_type=F32)
        out_ref[...] = product.astype(BF16)


def partials(tokens, weight, parts, offsets, cost, *before):
    block = jax.ShapeDtypeStruct((tokens.shape[0], weight.shape[1] // parts), BF16)
    return pl.pallas_call(
        functools.partial(partial_kernel, offsets, parts),
        in_specs=[VMEM] * (2 + len(before)),
        out_specs=[VMEM] * len(offsets),
        out_shape=[block] * len(offsets),
        compiler_params=params(24),
        cost_estimate=cost,
        name="partials",
    )(tokens, weight, *before)


def add_kernel(*refs):
    total = refs[0][...].astype(F32)
    for ref in refs[1:-1]:
        total = total + ref[...].astype(F32)
    refs[-1][...] = total.astype(BF16)


def add(*terms):
    return pl.pallas_call(
        add_kernel,
        in_specs=[VMEM] * len(terms),
        out_specs=VMEM,
        out_shape=jax.ShapeDtypeStruct(terms[0].shape, BF16),
        compiler_params=params(16),
        cost_estimate=COST,
        name="add",
    )(*terms)


def adapter(here, share, name):
    z = lax.axis_index("adp")
    if name[0] == "plane":
        return jnp.bitwise_xor(z, name[1]) * here + name[2]
    plane, off, k = name
    return jnp.bitwise_xor(z, plane) * here + jnp.bitwise_xor(lax.axis_index("grp"), off) * share + k


def low_kernel(groups, here, share, rank, more, ids_ref, tokens_ref, *refs):
    out_ref = refs[-1]
    total = refs[-2][...] if more else None
    for (start, stop), terms in groups:
        rows = [refs[i][k, :, cut : cut + stop - start] for i, k, cut, _ in terms]
        joined = rows[0] if len(rows) == 1 else jnp.concatenate(rows, axis=0)
        product = lax.dot_general(joined, tokens_ref[:, start:stop], LAST, preferred_element_type=F32)
        for n, (_, _, _, name) in enumerate(terms):
            mine = ids_ref[...] == adapter(here, share, name)
            term = jnp.where(mine, product[n * rank : (n + 1) * rank], 0.0)
            total = term if total is None else total + term
    out_ref[...] = total.astype(out_ref.dtype)


def low_rows(ids, tokens, here, share, groups, arrays, before, dtype, cost=COST):
    rank = arrays[0].shape[1]
    more = [] if before is None else [before]
    return pl.pallas_call(
        functools.partial(low_kernel, groups, here, share, rank, bool(more)),
        in_specs=[VMEM] * (2 + len(arrays) + len(more)),
        out_specs=VMEM,
        out_shape=jax.ShapeDtypeStruct((rank, tokens.shape[0]), dtype),
        compiler_params=params(24),
        cost_estimate=cost,
        name="low_rows",
    )(ids, tokens, *arrays, *more)


def ups_kernel(named, terms, here, share, rank, ids_ref, bits_ref, matrix_ref, *refs):
    up_ref, mask_ref = refs[-2:]
    width = up_ref.shape[1]
    up_ref[...] = jnp.zeros_like(up_ref)
    signs = (1 - 2 * bits_ref[...]).astype(F32)
    for n, (i, k, cut) in enumerate(terms):
        turned = rotate(refs[i][k, :, cut : cut + width].astype(F32), signs, matrix_ref[...])
        up_ref[n * rank : (n + 1) * rank, :] = jnp.concatenate(turned, axis=1).astype(BF16)
    ids = jnp.broadcast_to(ids_ref[...], (rank, ids_ref.shape[1])).T
    mask_ref[...] = jnp.zeros_like(mask_ref)
    for n, name in enumerate(named):
        mine = ids == adapter(here, share, name)
        mask_ref[:, n * rank : (n + 1) * rank] = jnp.where(mine, 1.0, 0.0).astype(BF16)


def rotated_ups(ids, bits, matrix, here, share, named, terms, arrays, width):
    rank, rows = arrays[0].shape[1], ids.shape[1]
    columns = -(-len(named) * rank // 128) * 128
    return pl.pallas_call(
        functools.partial(ups_kernel, named, terms, here, share, rank),
        in_specs=[VMEM] * (3 + len(arrays)),
        out_specs=[VMEM, VMEM],
        out_shape=[jax.ShapeDtypeStruct((columns, width), BF16), jax.ShapeDtypeStruct((rows, columns), BF16)],
        compiler_params=params(32),
        cost_estimate=COST,
        name="rotated_ups",
    )(ids, bits, matrix, *arrays)


def pick_kernel(named, here, share, ids_ref, pick_ref):
    rows, slots = pick_ref.shape[0], pick_ref.shape[1] // len(named)
    earlier = lax.broadcasted_iota(jnp.int32, (rows, rows), 0) < lax.broadcasted_iota(jnp.int32, (rows, rows), 1)
    earlier = jnp.where(earlier, 1.0, 0.0).astype(BF16)
    ids = jnp.broadcast_to(ids_ref[...], (8, rows))
    for k, name in enumerate(named):
        mine = ids == adapter(here, share, name)
        rank = jnp.dot(jnp.where(mine, 1.0, 0.0).astype(BF16), earlier, preferred_element_type=F32)
        rank = jnp.where(mine, rank, -1.0)
        rank = jnp.broadcast_to(rank[:1], (128, rows)).T
        for at in range(0, slots, 128):
            slot = (lax.broadcasted_iota(jnp.int32, (rows, 128), 1) + at).astype(F32)
            pick_ref[:, k * slots + at : k * slots + at + 128] = jnp.where(rank == slot, 1.0, 0.0).astype(BF16)


def picked(ids, here, share, named, slots):
    return pl.pallas_call(
        functools.partial(pick_kernel, named, here, share),
        in_specs=[VMEM],
        out_specs=VMEM,
        out_shape=jax.ShapeDtypeStruct((ids.shape[1], len(named) * slots), BF16),
        compiler_params=params(24),
        cost_estimate=COST,
        name="picked",
    )(ids)


def compact_kernel(tokens_ref, piece_ref, pick_ref, out_ref):
    share, features = piece_ref.shape[0], tokens_ref.shape[1]
    slots = pick_ref.shape[1] // share
    for k in range(share):
        product = lax.dot_general(piece_ref[k, :, :features], tokens_ref[...], LAST, preferred_element_type=F32)
        columns = slice(k * slots, (k + 1) * slots)
        kept = jnp.dot(product.astype(BF16), pick_ref[:, columns], preferred_element_type=F32)
        out_ref[:, columns] = kept.astype(BF16)


def compact(tokens, piece, pick):
    return pl.pallas_call(
        compact_kernel,
        in_specs=[VMEM] * 3,
        out_specs=VMEM,
        out_shape=jax.ShapeDtypeStruct((piece.shape[1], pick.shape[1]), BF16),
        compiler_params=params(24),
        cost_estimate=COST,
        name="compact",
    )(tokens, piece, pick)


def most_kernel(mine_ref, theirs_ref, up_ref, mask_ref, scale_ref, bits_ref, matrix_ref, *refs):
    low = (mine_ref[...].astype(F32) + theirs_ref[...].astype(F32)).astype(BF16).T
    rank, columns = low.shape[1], mask_ref.shape[1]
    signs = (1 - 2 * bits_ref[...]).astype(F32)
    spread = jnp.concatenate([low] * (columns // rank), axis=1) * mask_ref[...]
    delta = jnp.dot(spread, up_ref[...], preferred_element_type=F32)
    value = functools.reduce(jnp.add, [ref[...].astype(F32) for ref in refs[:-1]]) * scale_ref[...]
    refs[-1][...] = jnp.concatenate(rotate(value, signs, matrix_ref[...]), axis=1) + delta


def most(mine, theirs, up, mask, scale, bits, matrix, terms):
    return pl.pallas_call(
        most_kernel,
        in_specs=[VMEM] * (7 + len(terms)),
        out_specs=VMEM,
        out_shape=jax.ShapeDtypeStruct(terms[0].shape, F32),
        compiler_params=params(32),
        cost_estimate=COST,
        name="most",
    )(mine, theirs, up, mask, scale, bits, matrix, *terms)


def final_kernel(pick_ref, piece_ref, bits_ref, matrix_ref, most_ref, *refs):
    kept_refs, out_ref = refs[:-1], refs[-1]
    share, width = piece_ref.shape[0], out_ref.shape[1]
    features, slots = piece_ref.shape[2] - width, pick_ref.shape[1] // share
    signs = (1 - 2 * bits_ref[...]).astype(F32)
    low = functools.reduce(jnp.add, [ref[...].astype(F32) for ref in kept_refs]).astype(BF16).T
    deltas = []
    for k in range(share):
        turned = rotate(piece_ref[k, :, features:].astype(F32), signs, matrix_ref[...])
        up = jnp.concatenate(turned, axis=1).astype(BF16)
        deltas.append(jnp.dot(low[k * slots : (k + 1) * slots], up, preferred_element_type=F32).astype(BF16))
    delta = deltas[0] if share == 1 else jnp.concatenate(deltas, axis=0)
    result = most_ref[...] + jnp.dot(pick_ref[...], delta, preferred_element_type=F32)
    out_ref[...] = result.astype(BF16)


def final(kept, pick, piece, bits, matrix, rest):
    return pl.pallas_call(
        final_kernel,
        in_specs=[VMEM] * (5 + len(kept)),
        out_specs=VMEM,
        out_shape=jax.ShapeDtypeStruct(rest.shape, BF16),
        compiler_params=params(32),
        cost_estimate=COST,
        name="final",
    )(pick, piece, bits, matrix, rest, *kept)


def local(tokens, adapter_ids, base_weight, channel_scale, adapter_down, adapter_up, sign_bits):
    planes, groups, parts = lax.axis_size("adp"), lax.axis_size("grp"), lax.axis_size("tp")
    features = tokens.shape[1]
    here, _, rank = adapter_down.shape
    width = adapter_up.shape[2]
    share = here // groups
    matrix = hadamard(sign_bits.shape[0])
    bits, scale, ids = sign_bits[None, :], channel_scale[None, :], adapter_ids.T
    down = jnp.swapaxes(adapter_down, 1, 2)

    start = lax.axis_index("grp") * share
    own = lax.dynamic_slice_in_dim(down, start, share, 0)
    near = swap(own, "adp", 1)
    mine = [(0, jnp.concatenate([own, lax.dynamic_slice_in_dim(adapter_up, start, share, 0)], axis=2))]
    bit = planes // 2
    while bit > 1:
        mine += [(plane | bit, swap(piece, "adp", bit)) for plane, piece in mine]
        bit //= 2
    half = parts // 2
    offsets = (*range(1, parts, 2), *range(2, parts, 2))
    blocks = list(partials(tokens, base_weight, parts, offsets, lasting(4)))
    near, blocks[-1], up = together(near, blocks[-1], adapter_up)
    (block,) = partials(tokens, base_weight, parts, (0,), COST, blocks[-1])
    close, block, near_up, *far = together(near, block, swap(up, "adp", 1), *(piece for _, piece in mine[1:]))
    blocks = blocks[:half] + [block] + blocks[half:]
    mine = mine[:1] + [(plane, piece) for (plane, _), piece in zip(mine[1:], far)]
    odd = [(1, near)] + [(plane | 1, swap(piece, "adp", 1)) for plane, piece in mine[1:]]

    def others(pieces):
        return [(plane, off, swap(piece, "grp", off)) for plane, piece in pieces for off in range(1, groups)]

    swapped = others(odd[:1]) + others(mine[1:]) + others(odd[1:])
    held = [(plane, 0, piece) for plane, piece in [(1, close)] + mine[1:] + odd[1:]]

    def terms(pieces, start):
        return [(start + i, k, 0, (plane, off, k)) for i, (plane, off, _) in enumerate(pieces) for k in range(share)]

    def more(low, pieces, dtype, cost=COST):
        arrays, every = [p for *_, p in pieces], terms(pieces, 0)
        if low is None:
            every += [(len(arrays), k, 0, ("plane", 0, k)) for k in range(here)]
            arrays = arrays + [down]
        return low_rows(ids, tokens, here, share, [((0, features), every)], arrays, low, dtype, cost)

    low = more(None, held[: len(mine)] + swapped[:1], F32, lasting(2))
    slots = -(-2 * tokens.shape[0] // (here * planes) // 128) * 128
    last = swapped[-1]
    pick = picked(ids, here, share, [(last[0], last[1], k) for k in range(share)], slots)
    low, pick, *came = together(low, pick, *(swap(block, "tp", 1) for block in blocks[:half]))

    def both(low):
        bit = 1
        while bit < parts // 2:
            low = add(low, swap(low, "tp", bit))
            bit *= 2
        return low, swap(low, "tp", bit)

    rest = held[len(mine) :]
    low = more(low, swapped[1:-1] + rest, BF16, lasting(5))
    low, other = both(low)

    sums = [[block, pair] for block, pair in zip(blocks[half:], came)]
    bit = 2
    while bit < parts:
        came = [swap(add(*terms), "tp", bit) for terms in sums[1::2]]
        sums = [terms + [pair] for terms, pair in zip(sums[0::2], came)]
        bit *= 2

    far = [one for one in held + swapped[:-1] if one[0] > 1]
    named = [("plane", 0, k) for k in range(here)]
    named += [(plane, off, k) for plane, off, _ in far for k in range(share)]
    ups = [(0, k, 0) for k in range(here)] + [(1 + i, k, features) for i in range(len(far)) for k in range(share)]
    named += [("plane", 1, k) for k in range(here)]
    ups += [(1 + len(far), k, 0) for k in range(here)]
    arrays = [adapter_up] + [piece for *_, piece in far] + [near_up]
    up, mask = rotated_ups(ids, bits, matrix, here, share, named, ups, arrays, width)

    piece, up, mask = together(last[2], up, mask)
    kept = compact(tokens, piece, pick)
    kept = [kept] + [swap(kept, "tp", offset) for offset in range(1, parts)]
    rest = most(low, other, up, mask, scale, bits, matrix, sums[0])
    return final(kept, pick, piece, bits, matrix, rest)


def solution(mesh):
    return jax.shard_map(
        local,
        mesh=mesh,
        in_specs=(
            P(("grp", "adp"), "tp"),
            P(("grp", "adp"), None),
            P("tp", None),
            P("tp"),
            P("adp", "tp", None),
            P("adp", None, "tp"),
            P(),
        ),
        out_specs=P(("grp", "adp"), "tp"),
        check_vma=False,
    )
```

```python
import functools

import jax
import jax.numpy as jnp
import numpy as np
from jax import lax
from jax.experimental import pallas as pl
from jax.experimental.pallas import tpu as pltpu
from jax.sharding import PartitionSpec as P

VMEM = pl.BlockSpec(memory_space=pltpu.VMEM)
SMEM = pl.BlockSpec(memory_space=pltpu.SMEM)
F32, BF16 = jnp.float32, jnp.bfloat16
LAST = (((1,), (1,)), ((), ()))


def params(mib):
    return pltpu.CompilerParams(vmem_limit_bytes=mib << 20)


COST = pl.CostEstimate(flops=1, bytes_accessed=1, transcendentals=0)


def lasting(microseconds):
    return pl.CostEstimate(flops=int(microseconds * 1e9), bytes_accessed=1, transcendentals=0)


def hadamard(size):
    index = np.arange(size)
    shared = index[:, None] & index[None, :]
    parity = np.zeros_like(shared)
    while shared.any():
        parity, shared = parity ^ (shared & 1), shared >> 1
    return jnp.asarray(1 - 2 * parity, BF16)


def swap(x, axis, bit):
    return lax.ppermute(x, axis, [(i, i ^ bit) for i in range(lax.axis_size(axis))])


def together(*values):
    return lax.optimization_barrier(values)


def rotate(value, signs, matrix):
    head = matrix.shape[0]
    scale = signs * (1.0 / np.sqrt(head))
    turned = []
    for at in range(0, value.shape[1], head):
        signed = value[:, at : at + head] * scale
        high = signed.astype(BF16)
        rest = (signed - high.astype(F32)).astype(BF16)
        turned.append(
            jnp.dot(high, matrix, preferred_element_type=F32) + jnp.dot(rest, matrix, preferred_element_type=F32)
        )
    return turned


def partial_kernel(offsets, parts, tokens_ref, weight_ref, *refs):
    me, width = lax.axis_index("tp"), weight_ref.shape[1] // parts
    for offset, out_ref in zip(offsets, refs[-len(offsets) :]):
        at = pl.multiple_of(jnp.bitwise_xor(me, offset) * width, width)
        product = jnp.dot(tokens_ref[...], weight_ref[:, pl.ds(at, width)], preferred_element_type=F32)
        out_ref[...] = product.astype(BF16)


def partials(tokens, weight, parts, offsets, cost, *before):
    block = jax.ShapeDtypeStruct((tokens.shape[0], weight.shape[1] // parts), BF16)
    return pl.pallas_call(
        functools.partial(partial_kernel, offsets, parts),
        in_specs=[VMEM] * (2 + len(before)),
        out_specs=[VMEM] * len(offsets),
        out_shape=[block] * len(offsets),
        compiler_params=params(24),
        cost_estimate=cost,
        name="partials",
    )(tokens, weight, *before)


def add_kernel(*refs):
    total = refs[0][...].astype(F32)
    for ref in refs[1:-1]:
        total = total + ref[...].astype(F32)
    refs[-1][...] = total.astype(BF16)


def add(*terms):
    return pl.pallas_call(
        add_kernel,
        in_specs=[VMEM] * len(terms),
        out_specs=VMEM,
        out_shape=jax.ShapeDtypeStruct(terms[0].shape, BF16),
        compiler_params=params(16),
        cost_estimate=COST,
        name="add",
    )(*terms)


def adapter(here, share, name):
    z = lax.axis_index("adp")
    if name[0] == "plane":
        return jnp.bitwise_xor(z, name[1]) * here + name[2]
    plane, off, k = name
    return jnp.bitwise_xor(z, plane) * here + jnp.bitwise_xor(lax.axis_index("grp"), off) * share + k


def low_kernel(groups, here, share, rank, more, ids_ref, tokens_ref, *refs):
    out_ref = refs[-1]
    total = refs[-2][...] if more else None
    for (start, stop), terms in groups:
        rows = [refs[i][k, :, cut : cut + stop - start] for i, k, cut, _ in terms]
        joined = rows[0] if len(rows) == 1 else jnp.concatenate(rows, axis=0)
        product = lax.dot_general(joined, tokens_ref[:, start:stop], LAST, preferred_element_type=F32)
        for n, (_, _, _, name) in enumerate(terms):
            mine = ids_ref[...] == adapter(here, share, name)
            term = jnp.where(mine, product[n * rank : (n + 1) * rank], 0.0)
            total = term if total is None else total + term
    out_ref[...] = total.astype(out_ref.dtype)


def low_rows(ids, tokens, here, share, groups, arrays, before, dtype, cost=COST):
    rank = arrays[0].shape[1]
    more = [] if before is None else [before]
    return pl.pallas_call(
        functools.partial(low_kernel, groups, here, share, rank, bool(more)),
        in_specs=[VMEM] * (2 + len(arrays) + len(more)),
        out_specs=VMEM,
        out_shape=jax.ShapeDtypeStruct((rank, tokens.shape[0]), dtype),
        compiler_params=params(24),
        cost_estimate=cost,
        name="low_rows",
    )(ids, tokens, *arrays, *more)


def ups_kernel(named, terms, here, share, rank, ids_ref, bits_ref, matrix_ref, *refs):
    up_ref, mask_ref = refs[-2:]
    width = up_ref.shape[1]
    signs = (1 - 2 * bits_ref[...]).astype(F32)
    for n, (i, k, cut) in enumerate(terms):
        turned = rotate(refs[i][k, :, cut : cut + width].astype(F32), signs, matrix_ref[...])
        up_ref[n * rank : (n + 1) * rank, :] = jnp.concatenate(turned, axis=1).astype(BF16)
    ids = jnp.broadcast_to(ids_ref[...], (rank, ids_ref.shape[1])).T
    mask_ref[...] = jnp.zeros_like(mask_ref)
    for n, name in enumerate(named):
        mine = ids == adapter(here, share, name)
        mask_ref[:, n * rank : (n + 1) * rank] = jnp.where(mine, 1.0, 0.0).astype(BF16)


def rotated_ups(ids, bits, matrix, here, share, named, terms, arrays, width):
    rank, rows = arrays[0].shape[1], ids.shape[1]
    columns = -(-len(named) * rank // 128) * 128
    return pl.pallas_call(
        functools.partial(ups_kernel, named, terms, here, share, rank),
        in_specs=[VMEM] * (3 + len(arrays)),
        out_specs=[VMEM, VMEM],
        out_shape=[jax.ShapeDtypeStruct((len(terms) * rank, width), BF16), jax.ShapeDtypeStruct((rows, columns), BF16)],
        compiler_params=params(32),
        cost_estimate=COST,
        name="rotated_ups",
    )(ids, bits, matrix, *arrays)


def pick_kernel(named, here, share, ids_ref, pick_ref):
    rows, slots = pick_ref.shape[0], pick_ref.shape[1] // len(named)
    earlier = lax.broadcasted_iota(jnp.int32, (rows, rows), 0) < lax.broadcasted_iota(jnp.int32, (rows, rows), 1)
    earlier = jnp.where(earlier, 1.0, 0.0).astype(BF16)
    ids = jnp.broadcast_to(ids_ref[...], (8, rows))
    for k, name in enumerate(named):
        mine = ids == adapter(here, share, name)
        rank = jnp.dot(jnp.where(mine, 1.0, 0.0).astype(BF16), earlier, preferred_element_type=F32)
        rank = jnp.where(mine, rank, -1.0)
        rank = jnp.broadcast_to(rank[:1], (128, rows)).T
        for at in range(0, slots, 128):
            slot = (lax.broadcasted_iota(jnp.int32, (rows, 128), 1) + at).astype(F32)
            pick_ref[:, k * slots + at : k * slots + at + 128] = jnp.where(rank == slot, 1.0, 0.0).astype(BF16)


def picked(ids, here, share, named, slots):
    return pl.pallas_call(
        functools.partial(pick_kernel, named, here, share),
        in_specs=[VMEM],
        out_specs=VMEM,
        out_shape=jax.ShapeDtypeStruct((ids.shape[1], len(named) * slots), BF16),
        compiler_params=params(24),
        cost_estimate=COST,
        name="picked",
    )(ids)


def compact_kernel(tokens_ref, piece_ref, pick_ref, out_ref):
    share, features = piece_ref.shape[0], tokens_ref.shape[1]
    slots = pick_ref.shape[1] // share
    for k in range(share):
        product = lax.dot_general(piece_ref[k, :, :features], tokens_ref[...], LAST, preferred_element_type=F32)
        columns = slice(k * slots, (k + 1) * slots)
        kept = jnp.dot(product.astype(BF16), pick_ref[:, columns], preferred_element_type=F32)
        out_ref[:, columns] = kept.astype(BF16)


def compact(tokens, piece, pick):
    return pl.pallas_call(
        compact_kernel,
        in_specs=[VMEM] * 3,
        out_specs=VMEM,
        out_shape=jax.ShapeDtypeStruct((piece.shape[1], pick.shape[1]), BF16),
        compiler_params=params(24),
        cost_estimate=lasting(2),
        name="compact",
    )(tokens, piece, pick)


def most_kernel(mine_ref, theirs_ref, up_ref, mask_ref, near_ref, scale_ref, bits_ref, matrix_ref, *refs):
    low = (mine_ref[...].astype(F32) + theirs_ref[...].astype(F32)).astype(BF16).T
    rank, columns = low.shape[1], mask_ref.shape[1]
    signs = (1 - 2 * bits_ref[...]).astype(F32)
    ups = [up_ref[...]]
    for k in range(near_ref.shape[0]):
        turned = rotate(near_ref[k].astype(F32), signs, matrix_ref[...])
        ups.append(jnp.concatenate(turned, axis=1).astype(BF16))
    missing = columns - sum(up.shape[0] for up in ups)
    if missing:
        ups.append(jnp.zeros((missing, up_ref.shape[1]), BF16))
    spread = jnp.concatenate([low] * (columns // rank), axis=1) * mask_ref[...]
    delta = jnp.dot(spread, jnp.concatenate(ups, axis=0), preferred_element_type=F32)
    value = functools.reduce(jnp.add, [ref[...].astype(F32) for ref in refs[:-1]]) * scale_ref[...]
    refs[-1][...] = jnp.concatenate(rotate(value, signs, matrix_ref[...]), axis=1) + delta


def most(mine, theirs, up, mask, near, scale, bits, matrix, terms):
    return pl.pallas_call(
        most_kernel,
        in_specs=[VMEM] * (8 + len(terms)),
        out_specs=VMEM,
        out_shape=jax.ShapeDtypeStruct(terms[0].shape, F32),
        compiler_params=params(32),
        cost_estimate=COST,
        name="most",
    )(mine, theirs, up, mask, near, scale, bits, matrix, *terms)


def final_kernel(pick_ref, piece_ref, bits_ref, matrix_ref, most_ref, *refs):
    kept_refs, out_ref = refs[:-1], refs[-1]
    share, width = piece_ref.shape[0], out_ref.shape[1]
    features, slots = piece_ref.shape[2] - width, pick_ref.shape[1] // share
    signs = (1 - 2 * bits_ref[...]).astype(F32)
    low = functools.reduce(jnp.add, [ref[...].astype(F32) for ref in kept_refs]).astype(BF16).T
    deltas = []
    for k in range(share):
        turned = rotate(piece_ref[k, :, features:].astype(F32), signs, matrix_ref[...])
        up = jnp.concatenate(turned, axis=1).astype(BF16)
        deltas.append(jnp.dot(low[k * slots : (k + 1) * slots], up, preferred_element_type=F32).astype(BF16))
    delta = deltas[0] if share == 1 else jnp.concatenate(deltas, axis=0)
    result = most_ref[...] + jnp.dot(pick_ref[...], delta, preferred_element_type=F32)
    out_ref[...] = result.astype(BF16)


def final(kept, pick, piece, bits, matrix, rest):
    return pl.pallas_call(
        final_kernel,
        in_specs=[VMEM] * (5 + len(kept)),
        out_specs=VMEM,
        out_shape=jax.ShapeDtypeStruct(rest.shape, BF16),
        compiler_params=params(32),
        cost_estimate=COST,
        name="final",
    )(pick, piece, bits, matrix, rest, *kept)


def local(tokens, adapter_ids, base_weight, channel_scale, adapter_down, adapter_up, sign_bits):
    planes, groups, parts = lax.axis_size("adp"), lax.axis_size("grp"), lax.axis_size("tp")
    features = tokens.shape[1]
    here, _, rank = adapter_down.shape
    width = adapter_up.shape[2]
    share = here // groups
    matrix = hadamard(sign_bits.shape[0])
    bits, scale, ids = sign_bits[None, :], channel_scale[None, :], adapter_ids.T
    down = jnp.swapaxes(adapter_down, 1, 2)

    start = lax.axis_index("grp") * share
    own = lax.dynamic_slice_in_dim(down, start, share, 0)
    near = swap(own, "adp", 1)
    mine = [(0, jnp.concatenate([own, lax.dynamic_slice_in_dim(adapter_up, start, share, 0)], axis=2))]
    bit = planes // 2
    while bit > 1:
        mine += [(plane | bit, swap(piece, "adp", bit)) for plane, piece in mine]
        bit //= 2
    half = parts // 2
    offsets = (*range(1, parts, 2), *range(2, parts, 2))
    blocks = list(partials(tokens, base_weight, parts, offsets, lasting(4)))
    near, blocks[-1] = together(near, blocks[-1])
    (block,) = partials(tokens, base_weight, parts, (0,), COST, blocks[-1])
    close, block, *far = together(near, block, *(piece for _, piece in mine[1:]))
    blocks = blocks[:half] + [block] + blocks[half:]
    mine = mine[:1] + [(plane, piece) for (plane, _), piece in zip(mine[1:], far)]
    odd = [(1, near)] + [(plane | 1, swap(piece, "adp", 1)) for plane, piece in mine[1:]]

    def others(pieces):
        return [(plane, off, swap(piece, "grp", off)) for plane, piece in pieces for off in range(1, groups)]

    swapped = others(odd[:1]) + others(mine[1:]) + others(odd[1:])
    held = [(plane, 0, piece) for plane, piece in [(1, close)] + mine[1:] + odd[1:]]

    def terms(pieces, start):
        return [(start + i, k, 0, (plane, off, k)) for i, (plane, off, _) in enumerate(pieces) for k in range(share)]

    def more(low, pieces, dtype, cost=COST):
        arrays, every = [p for *_, p in pieces], terms(pieces, 0)
        if low is None:
            every += [(len(arrays), k, 0, ("plane", 0, k)) for k in range(here)]
            arrays = arrays + [down]
        return low_rows(ids, tokens, here, share, [((0, features), every)], arrays, low, dtype, cost)

    low = more(None, held[: len(mine)] + swapped[:1], F32, lasting(2))
    slots = -(-2 * tokens.shape[0] // (here * planes) // 128) * 128
    last = swapped[-1]
    pick = picked(ids, here, share, [(last[0], last[1], k) for k in range(share)], slots)
    low, pick, *came = together(low, pick, *(swap(block, "tp", 1) for block in blocks[:half]))

    def both(low):
        bit = 1
        while bit < parts // 2:
            low = add(low, swap(low, "tp", bit))
            bit *= 2
        return low, swap(low, "tp", bit)

    rest = held[len(mine) :]
    low = more(low, swapped[1:-1] + rest, BF16, lasting(5))
    low, up = together(low, adapter_up)
    near_up = swap(up, "adp", 1)
    low, other = both(low)

    sums = [[block, pair] for block, pair in zip(blocks[half:], came)]
    bit = 2
    while bit < parts:
        came = [swap(add(*terms), "tp", bit) for terms in sums[1::2]]
        sums = [terms + [pair] for terms, pair in zip(sums[0::2], came)]
        bit *= 2

    far = [one for one in held + swapped[:-1] if one[0] > 1]
    named = [("plane", 0, k) for k in range(here)]
    named += [(plane, off, k) for plane, off, _ in far for k in range(share)]
    ups = [(0, k, 0) for k in range(here)] + [(1 + i, k, features) for i in range(len(far)) for k in range(share)]
    named += [("plane", 1, k) for k in range(here)]
    arrays = [adapter_up] + [piece for *_, piece in far]
    up, mask = rotated_ups(ids, bits, matrix, here, share, named, ups, arrays, width)

    piece, up, mask, near_up = together(last[2], up, mask, near_up)
    kept = compact(tokens, piece, pick)
    kept = [kept] + [swap(kept, "tp", offset) for offset in range(1, parts)]
    rest = most(low, other, up, mask, near_up, scale, bits, matrix, sums[0])
    return final(kept, pick, piece, bits, matrix, rest)


def solution(mesh):
    return jax.shard_map(
        local,
        mesh=mesh,
        in_specs=(
            P(("grp", "adp"), "tp"),
            P(("grp", "adp"), None),
            P("tp", None),
            P("tp"),
            P("adp", "tp", None),
            P("adp", None, "tp"),
            P(),
        ),
        out_specs=P(("grp", "adp"), "tp"),
        check_vma=False,
    )
```

```python
import functools

import jax
import jax.numpy as jnp
import numpy as np
from jax import lax
from jax.experimental import pallas as pl
from jax.experimental.pallas import tpu as pltpu
from jax.sharding import PartitionSpec as P

VMEM = pl.BlockSpec(memory_space=pltpu.VMEM)
SMEM = pl.BlockSpec(memory_space=pltpu.SMEM)
F32, BF16 = jnp.float32, jnp.bfloat16
LAST = (((1,), (1,)), ((), ()))


def params(mib):
    return pltpu.CompilerParams(vmem_limit_bytes=mib << 20)


COST = pl.CostEstimate(flops=1, bytes_accessed=1, transcendentals=0)


def lasting(microseconds):
    return pl.CostEstimate(flops=int(microseconds * 1e9), bytes_accessed=1, transcendentals=0)


def hadamard(size):
    index = np.arange(size)
    shared = index[:, None] & index[None, :]
    parity = np.zeros_like(shared)
    while shared.any():
        parity, shared = parity ^ (shared & 1), shared >> 1
    return jnp.asarray(1 - 2 * parity, BF16)


def swap(x, axis, bit):
    return lax.ppermute(x, axis, [(i, i ^ bit) for i in range(lax.axis_size(axis))])


def together(*values):
    return lax.optimization_barrier(values)


def rotate(value, signs, matrix):
    head = matrix.shape[0]
    scale = signs * (1.0 / np.sqrt(head))
    turned = []
    for at in range(0, value.shape[1], head):
        signed = value[:, at : at + head] * scale
        high = signed.astype(BF16)
        rest = (signed - high.astype(F32)).astype(BF16)
        turned.append(
            jnp.dot(high, matrix, preferred_element_type=F32) + jnp.dot(rest, matrix, preferred_element_type=F32)
        )
    return turned


def partial_kernel(offsets, parts, tokens_ref, weight_ref, *refs):
    me, width = lax.axis_index("tp"), weight_ref.shape[1] // parts
    for offset, out_ref in zip(offsets, refs[-len(offsets) :]):
        at = pl.multiple_of(jnp.bitwise_xor(me, offset) * width, width)
        product = jnp.dot(tokens_ref[...], weight_ref[:, pl.ds(at, width)], preferred_element_type=F32)
        out_ref[...] = product.astype(BF16)


def partials(tokens, weight, parts, offsets, cost, *before):
    block = jax.ShapeDtypeStruct((tokens.shape[0], weight.shape[1] // parts), BF16)
    return pl.pallas_call(
        functools.partial(partial_kernel, offsets, parts),
        in_specs=[VMEM] * (2 + len(before)),
        out_specs=[VMEM] * len(offsets),
        out_shape=[block] * len(offsets),
        compiler_params=params(24),
        cost_estimate=cost,
        name="partials",
    )(tokens, weight, *before)


def add_kernel(*refs):
    total = refs[0][...].astype(F32)
    for ref in refs[1:-1]:
        total = total + ref[...].astype(F32)
    refs[-1][...] = total.astype(BF16)


def add(*terms):
    return pl.pallas_call(
        add_kernel,
        in_specs=[VMEM] * len(terms),
        out_specs=VMEM,
        out_shape=jax.ShapeDtypeStruct(terms[0].shape, BF16),
        compiler_params=params(16),
        cost_estimate=COST,
        name="add",
    )(*terms)


def adapter(here, share, name):
    z = lax.axis_index("adp")
    if name[0] == "plane":
        return jnp.bitwise_xor(z, name[1]) * here + name[2]
    plane, off, k = name
    return jnp.bitwise_xor(z, plane) * here + jnp.bitwise_xor(lax.axis_index("grp"), off) * share + k


def low_kernel(groups, here, share, rank, more, ids_ref, tokens_ref, *refs):
    out_ref = refs[-1]
    total = refs[-2][...] if more else None
    for (start, stop), terms in groups:
        rows = [refs[i][k, :, cut : cut + stop - start] for i, k, cut, _ in terms]
        joined = rows[0] if len(rows) == 1 else jnp.concatenate(rows, axis=0)
        product = lax.dot_general(joined, tokens_ref[:, start:stop], LAST, preferred_element_type=F32)
        for n, (_, _, _, name) in enumerate(terms):
            mine = ids_ref[...] == adapter(here, share, name)
            term = jnp.where(mine, product[n * rank : (n + 1) * rank], 0.0)
            total = term if total is None else total + term
    out_ref[...] = total.astype(out_ref.dtype)


def low_rows(ids, tokens, here, share, groups, arrays, before, dtype, cost=COST):
    rank = arrays[0].shape[1]
    more = [] if before is None else [before]
    return pl.pallas_call(
        functools.partial(low_kernel, groups, here, share, rank, bool(more)),
        in_specs=[VMEM] * (2 + len(arrays) + len(more)),
        out_specs=VMEM,
        out_shape=jax.ShapeDtypeStruct((rank, tokens.shape[0]), dtype),
        compiler_params=params(24),
        cost_estimate=cost,
        name="low_rows",
    )(ids, tokens, *arrays, *more)


def ups_kernel(named, terms, here, share, rank, ids_ref, bits_ref, matrix_ref, *refs):
    up_ref, mask_ref = refs[-2:]
    width = up_ref.shape[1]
    signs = (1 - 2 * bits_ref[...]).astype(F32)
    for n, (i, k, cut) in enumerate(terms):
        turned = rotate(refs[i][k, :, cut : cut + width].astype(F32), signs, matrix_ref[...])
        up_ref[n * rank : (n + 1) * rank, :] = jnp.concatenate(turned, axis=1).astype(BF16)
    ids = jnp.broadcast_to(ids_ref[...], (rank, ids_ref.shape[1])).T
    mask_ref[...] = jnp.zeros_like(mask_ref)
    for n, name in enumerate(named):
        mine = ids == adapter(here, share, name)
        mask_ref[:, n * rank : (n + 1) * rank] = jnp.where(mine, 1.0, 0.0).astype(BF16)


def rotated_ups(ids, bits, matrix, here, share, named, terms, arrays, width):
    rank, rows = arrays[0].shape[1], ids.shape[1]
    columns = -(-len(named) * rank // 128) * 128
    return pl.pallas_call(
        functools.partial(ups_kernel, named, terms, here, share, rank),
        in_specs=[VMEM] * (3 + len(arrays)),
        out_specs=[VMEM, VMEM],
        out_shape=[jax.ShapeDtypeStruct((len(terms) * rank, width), BF16), jax.ShapeDtypeStruct((rows, columns), BF16)],
        compiler_params=params(32),
        cost_estimate=COST,
        name="rotated_ups",
    )(ids, bits, matrix, *arrays)


def pick_kernel(named, here, share, ids_ref, pick_ref):
    rows, slots = pick_ref.shape[0], pick_ref.shape[1] // len(named)
    earlier = lax.broadcasted_iota(jnp.int32, (rows, rows), 0) < lax.broadcasted_iota(jnp.int32, (rows, rows), 1)
    earlier = jnp.where(earlier, 1.0, 0.0).astype(BF16)
    ids = jnp.broadcast_to(ids_ref[...], (8, rows))
    for k, name in enumerate(named):
        mine = ids == adapter(here, share, name)
        rank = jnp.dot(jnp.where(mine, 1.0, 0.0).astype(BF16), earlier, preferred_element_type=F32)
        rank = jnp.where(mine, rank, -1.0)
        rank = jnp.broadcast_to(rank[:1], (128, rows)).T
        for at in range(0, slots, 128):
            slot = (lax.broadcasted_iota(jnp.int32, (rows, 128), 1) + at).astype(F32)
            pick_ref[:, k * slots + at : k * slots + at + 128] = jnp.where(rank == slot, 1.0, 0.0).astype(BF16)


def picked(ids, here, share, named, slots):
    return pl.pallas_call(
        functools.partial(pick_kernel, named, here, share),
        in_specs=[VMEM],
        out_specs=VMEM,
        out_shape=jax.ShapeDtypeStruct((ids.shape[1], len(named) * slots), BF16),
        compiler_params=params(24),
        cost_estimate=COST,
        name="picked",
    )(ids)


def compact_kernel(tokens_ref, piece_ref, pick_ref, out_ref):
    share, features = piece_ref.shape[0], tokens_ref.shape[1]
    slots = pick_ref.shape[1] // share
    for k in range(share):
        product = lax.dot_general(piece_ref[k, :, :features], tokens_ref[...], LAST, preferred_element_type=F32)
        columns = slice(k * slots, (k + 1) * slots)
        kept = jnp.dot(product.astype(BF16), pick_ref[:, columns], preferred_element_type=F32)
        out_ref[:, columns] = kept.astype(BF16)


def compact(tokens, piece, pick):
    return pl.pallas_call(
        compact_kernel,
        in_specs=[VMEM] * 3,
        out_specs=VMEM,
        out_shape=jax.ShapeDtypeStruct((piece.shape[1], pick.shape[1]), BF16),
        compiler_params=params(24),
        cost_estimate=lasting(2),
        name="compact",
    )(tokens, piece, pick)


def most_kernel(mine_ref, theirs_ref, up_ref, mask_ref, near_ref, scale_ref, bits_ref, matrix_ref, *refs):
    low = (mine_ref[...].astype(F32) + theirs_ref[...].astype(F32)).astype(BF16).T
    rank, columns = low.shape[1], mask_ref.shape[1]
    signs = (1 - 2 * bits_ref[...]).astype(F32)
    ups = [up_ref[...]]
    for k in range(near_ref.shape[0]):
        turned = rotate(near_ref[k].astype(F32), signs, matrix_ref[...])
        ups.append(jnp.concatenate(turned, axis=1).astype(BF16))
    missing = columns - sum(up.shape[0] for up in ups)
    if missing:
        ups.append(jnp.zeros((missing, up_ref.shape[1]), BF16))
    spread = jnp.concatenate([low] * (columns // rank), axis=1) * mask_ref[...]
    delta = jnp.dot(spread, jnp.concatenate(ups, axis=0), preferred_element_type=F32)
    value = functools.reduce(jnp.add, [ref[...].astype(F32) for ref in refs[:-1]]) * scale_ref[...]
    refs[-1][...] = jnp.concatenate(rotate(value, signs, matrix_ref[...]), axis=1) + delta


def most(mine, theirs, up, mask, near, scale, bits, matrix, terms):
    return pl.pallas_call(
        most_kernel,
        in_specs=[VMEM] * (8 + len(terms)),
        out_specs=VMEM,
        out_shape=jax.ShapeDtypeStruct(terms[0].shape, F32),
        compiler_params=params(32),
        cost_estimate=COST,
        name="most",
    )(mine, theirs, up, mask, near, scale, bits, matrix, *terms)


def final_kernel(pick_ref, piece_ref, bits_ref, matrix_ref, most_ref, *refs):
    kept_refs, out_ref = refs[:-1], refs[-1]
    share, width = piece_ref.shape[0], out_ref.shape[1]
    features, slots = piece_ref.shape[2] - width, pick_ref.shape[1] // share
    signs = (1 - 2 * bits_ref[...]).astype(F32)
    low = functools.reduce(jnp.add, [ref[...].astype(F32) for ref in kept_refs]).astype(BF16).T
    deltas = []
    for k in range(share):
        turned = rotate(piece_ref[k, :, features:].astype(F32), signs, matrix_ref[...])
        up = jnp.concatenate(turned, axis=1).astype(BF16)
        deltas.append(jnp.dot(low[k * slots : (k + 1) * slots], up, preferred_element_type=F32).astype(BF16))
    delta = deltas[0] if share == 1 else jnp.concatenate(deltas, axis=0)
    result = most_ref[...] + jnp.dot(pick_ref[...], delta, preferred_element_type=F32)
    out_ref[...] = result.astype(BF16)


def final(kept, pick, piece, bits, matrix, rest):
    return pl.pallas_call(
        final_kernel,
        in_specs=[VMEM] * (5 + len(kept)),
        out_specs=VMEM,
        out_shape=jax.ShapeDtypeStruct(rest.shape, BF16),
        compiler_params=params(32),
        cost_estimate=COST,
        name="final",
    )(pick, piece, bits, matrix, rest, *kept)


def local(tokens, adapter_ids, base_weight, channel_scale, adapter_down, adapter_up, sign_bits):
    planes, groups, parts = lax.axis_size("adp"), lax.axis_size("grp"), lax.axis_size("tp")
    features = tokens.shape[1]
    here, _, rank = adapter_down.shape
    width = adapter_up.shape[2]
    share = here // groups
    matrix = hadamard(sign_bits.shape[0])
    bits, scale, ids = sign_bits[None, :], channel_scale[None, :], adapter_ids.T
    down = jnp.swapaxes(adapter_down, 1, 2)

    start = lax.axis_index("grp") * share
    own = lax.dynamic_slice_in_dim(down, start, share, 0)
    near = swap(own, "adp", 1)
    mine = [(0, jnp.concatenate([own, lax.dynamic_slice_in_dim(adapter_up, start, share, 0)], axis=2))]
    bit = planes // 2
    while bit > 1:
        mine += [(plane | bit, swap(piece, "adp", bit)) for plane, piece in mine]
        bit //= 2
    half = parts // 2
    offsets = (*range(1, parts, 2), *range(2, parts, 2))
    blocks = list(partials(tokens, base_weight, parts, offsets, lasting(4)))
    near, blocks[-1] = together(near, blocks[-1])
    (block,) = partials(tokens, base_weight, parts, (0,), COST, blocks[-1])
    close, block, *far = together(near, block, *(piece for _, piece in mine[1:]))
    blocks = blocks[:half] + [block] + blocks[half:]
    mine = mine[:1] + [(plane, piece) for (plane, _), piece in zip(mine[1:], far)]
    odd = [(1, near)] + [(plane | 1, swap(piece, "adp", 1)) for plane, piece in mine[1:]]

    def others(pieces):
        return [(plane, off, swap(piece, "grp", off)) for plane, piece in pieces for off in range(1, groups)]

    swapped = others(odd[:1]) + others(mine[1:]) + others(odd[1:])
    held = [(plane, 0, piece) for plane, piece in [(1, close)] + mine[1:] + odd[1:]]

    def terms(pieces, start):
        return [(start + i, k, 0, (plane, off, k)) for i, (plane, off, _) in enumerate(pieces) for k in range(share)]

    def more(low, pieces, dtype, cost=COST):
        arrays, every = [p for *_, p in pieces], terms(pieces, 0)
        if low is None:
            every += [(len(arrays), k, 0, ("plane", 0, k)) for k in range(here)]
            arrays = arrays + [down]
        return low_rows(ids, tokens, here, share, [((0, features), every)], arrays, low, dtype, cost)

    low = more(None, held[: len(mine)] + swapped[:1], F32, lasting(2))
    slots = -(-2 * tokens.shape[0] // (here * planes) // 128) * 128
    last = swapped[-1]
    pick = picked(ids, here, share, [(last[0], last[1], k) for k in range(share)], slots)
    low, pick = together(low, pick)
    blocks[half], *came = together(blocks[half], *(swap(block, "tp", 1) for block in blocks[:half]))

    def both(low):
        bit = 1
        while bit < parts // 2:
            low = add(low, swap(low, "tp", bit))
            bit *= 2
        return low, swap(low, "tp", bit)

    rest = held[len(mine) :]
    low = more(low, swapped[1:-1] + rest, BF16, lasting(5))
    low, up = together(low, adapter_up)
    near_up = swap(up, "adp", 1)
    low, other = both(low)

    sums = [[block, pair] for block, pair in zip(blocks[half:], came)]
    bit = 2
    while bit < parts:
        came = [swap(add(*terms), "tp", bit) for terms in sums[1::2]]
        sums = [terms + [pair] for terms, pair in zip(sums[0::2], came)]
        bit *= 2

    far = [one for one in held + swapped[:-1] if one[0] > 1]
    named = [("plane", 0, k) for k in range(here)]
    named += [(plane, off, k) for plane, off, _ in far for k in range(share)]
    ups = [(0, k, 0) for k in range(here)] + [(1 + i, k, features) for i in range(len(far)) for k in range(share)]
    named += [("plane", 1, k) for k in range(here)]
    arrays = [adapter_up] + [piece for *_, piece in far]
    up, mask = rotated_ups(ids, bits, matrix, here, share, named, ups, arrays, width)

    piece, up, mask, near_up = together(last[2], up, mask, near_up)
    kept = compact(tokens, piece, pick)
    kept = [kept] + [swap(kept, "tp", offset) for offset in range(1, parts)]
    rest = most(low, other, up, mask, near_up, scale, bits, matrix, sums[0])
    return final(kept, pick, piece, bits, matrix, rest)


def solution(mesh):
    return jax.shard_map(
        local,
        mesh=mesh,
        in_specs=(
            P(("grp", "adp"), "tp"),
            P(("grp", "adp"), None),
            P("tp", None),
            P("tp"),
            P("adp", "tp", None),
            P("adp", None, "tp"),
            P(),
        ),
        out_specs=P(("grp", "adp"), "tp"),
        check_vma=False,
    )
```

```python
import functools

import jax
import jax.numpy as jnp
import numpy as np
from jax import lax
from jax.experimental import pallas as pl
from jax.experimental.pallas import tpu as pltpu
from jax.sharding import PartitionSpec as P

VMEM = pl.BlockSpec(memory_space=pltpu.VMEM)
SMEM = pl.BlockSpec(memory_space=pltpu.SMEM)
F32, BF16 = jnp.float32, jnp.bfloat16
LAST = (((1,), (1,)), ((), ()))


def params(mib):
    return pltpu.CompilerParams(vmem_limit_bytes=mib << 20)


COST = pl.CostEstimate(flops=1, bytes_accessed=1, transcendentals=0)


def lasting(microseconds):
    return pl.CostEstimate(flops=int(microseconds * 1e9), bytes_accessed=1, transcendentals=0)


def hadamard(size):
    index = np.arange(size)
    shared = index[:, None] & index[None, :]
    parity = np.zeros_like(shared)
    while shared.any():
        parity, shared = parity ^ (shared & 1), shared >> 1
    return jnp.asarray(1 - 2 * parity, BF16)


def swap(x, axis, bit):
    return lax.ppermute(x, axis, [(i, i ^ bit) for i in range(lax.axis_size(axis))])


def together(*values):
    return lax.optimization_barrier(values)


def rotate(value, signs, matrix):
    head = matrix.shape[0]
    scale = signs * (1.0 / np.sqrt(head))
    turned = []
    for at in range(0, value.shape[1], head):
        signed = value[:, at : at + head] * scale
        high = signed.astype(BF16)
        rest = (signed - high.astype(F32)).astype(BF16)
        turned.append(
            jnp.dot(high, matrix, preferred_element_type=F32) + jnp.dot(rest, matrix, preferred_element_type=F32)
        )
    return turned


def partial_kernel(offsets, parts, tokens_ref, weight_ref, *refs):
    me, width = lax.axis_index("tp"), weight_ref.shape[1] // parts
    for offset, out_ref in zip(offsets, refs[-len(offsets) :]):
        at = pl.multiple_of(jnp.bitwise_xor(me, offset) * width, width)
        product = jnp.dot(tokens_ref[...], weight_ref[:, pl.ds(at, width)], preferred_element_type=F32)
        out_ref[...] = product.astype(BF16)


def partials(tokens, weight, parts, offsets, cost, *before):
    block = jax.ShapeDtypeStruct((tokens.shape[0], weight.shape[1] // parts), BF16)
    return pl.pallas_call(
        functools.partial(partial_kernel, offsets, parts),
        in_specs=[VMEM] * (2 + len(before)),
        out_specs=[VMEM] * len(offsets),
        out_shape=[block] * len(offsets),
        compiler_params=params(24),
        cost_estimate=cost,
        name="partials",
    )(tokens, weight, *before)


def add_kernel(*refs):
    total = refs[0][...].astype(F32)
    for ref in refs[1:-1]:
        total = total + ref[...].astype(F32)
    refs[-1][...] = total.astype(BF16)


def add(*terms):
    return pl.pallas_call(
        add_kernel,
        in_specs=[VMEM] * len(terms),
        out_specs=VMEM,
        out_shape=jax.ShapeDtypeStruct(terms[0].shape, BF16),
        compiler_params=params(16),
        cost_estimate=COST,
        name="add",
    )(*terms)


def adapter(here, share, name):
    z = lax.axis_index("adp")
    if name[0] == "plane":
        return jnp.bitwise_xor(z, name[1]) * here + name[2]
    plane, off, k = name
    return jnp.bitwise_xor(z, plane) * here + jnp.bitwise_xor(lax.axis_index("grp"), off) * share + k


def low_kernel(groups, here, share, rank, more, ids_ref, tokens_ref, *refs):
    out_ref = refs[-1]
    total = refs[-2][...] if more else None
    for (start, stop), terms in groups:
        rows = [refs[i][k, :, cut : cut + stop - start] for i, k, cut, _ in terms]
        joined = rows[0] if len(rows) == 1 else jnp.concatenate(rows, axis=0)
        product = lax.dot_general(joined, tokens_ref[:, start:stop], LAST, preferred_element_type=F32)
        for n, (_, _, _, name) in enumerate(terms):
            mine = ids_ref[...] == adapter(here, share, name)
            term = jnp.where(mine, product[n * rank : (n + 1) * rank], 0.0)
            total = term if total is None else total + term
    out_ref[...] = total.astype(out_ref.dtype)


def low_rows(ids, tokens, here, share, groups, arrays, before, dtype, cost=COST):
    rank = arrays[0].shape[1]
    more = [] if before is None else [before]
    return pl.pallas_call(
        functools.partial(low_kernel, groups, here, share, rank, bool(more)),
        in_specs=[VMEM] * (2 + len(arrays) + len(more)),
        out_specs=VMEM,
        out_shape=jax.ShapeDtypeStruct((rank, tokens.shape[0]), dtype),
        compiler_params=params(24),
        cost_estimate=cost,
        name="low_rows",
    )(ids, tokens, *arrays, *more)


def ups_kernel(named, terms, here, share, rank, ids_ref, bits_ref, matrix_ref, *refs):
    up_ref, mask_ref = refs[-2:]
    width = up_ref.shape[1]
    signs = (1 - 2 * bits_ref[...]).astype(F32)
    for n, (i, k, cut) in enumerate(terms):
        turned = rotate(refs[i][k, :, cut : cut + width].astype(F32), signs, matrix_ref[...])
        up_ref[n * rank : (n + 1) * rank, :] = jnp.concatenate(turned, axis=1).astype(BF16)
    ids = jnp.broadcast_to(ids_ref[...], (rank, ids_ref.shape[1])).T
    mask_ref[...] = jnp.zeros_like(mask_ref)
    for n, name in enumerate(named):
        mine = ids == adapter(here, share, name)
        mask_ref[:, n * rank : (n + 1) * rank] = jnp.where(mine, 1.0, 0.0).astype(BF16)


def rotated_ups(ids, bits, matrix, here, share, named, terms, arrays, width):
    rank, rows = arrays[0].shape[1], ids.shape[1]
    columns = -(-len(named) * rank // 128) * 128
    return pl.pallas_call(
        functools.partial(ups_kernel, named, terms, here, share, rank),
        in_specs=[VMEM] * (3 + len(arrays)),
        out_specs=[VMEM, VMEM],
        out_shape=[jax.ShapeDtypeStruct((len(terms) * rank, width), BF16), jax.ShapeDtypeStruct((rows, columns), BF16)],
        compiler_params=params(32),
        cost_estimate=COST,
        name="rotated_ups",
    )(ids, bits, matrix, *arrays)


def pick_kernel(named, here, share, ids_ref, pick_ref):
    rows, slots = pick_ref.shape[0], pick_ref.shape[1] // len(named)
    earlier = lax.broadcasted_iota(jnp.int32, (rows, rows), 0) < lax.broadcasted_iota(jnp.int32, (rows, rows), 1)
    earlier = jnp.where(earlier, 1.0, 0.0).astype(BF16)
    ids = jnp.broadcast_to(ids_ref[...], (8, rows))
    for k, name in enumerate(named):
        mine = ids == adapter(here, share, name)
        rank = jnp.dot(jnp.where(mine, 1.0, 0.0).astype(BF16), earlier, preferred_element_type=F32)
        rank = jnp.where(mine, rank, -1.0)
        rank = jnp.broadcast_to(rank[:1], (128, rows)).T
        for at in range(0, slots, 128):
            slot = (lax.broadcasted_iota(jnp.int32, (rows, 128), 1) + at).astype(F32)
            pick_ref[:, k * slots + at : k * slots + at + 128] = jnp.where(rank == slot, 1.0, 0.0).astype(BF16)


def picked(ids, here, share, named, slots):
    return pl.pallas_call(
        functools.partial(pick_kernel, named, here, share),
        in_specs=[VMEM],
        out_specs=VMEM,
        out_shape=jax.ShapeDtypeStruct((ids.shape[1], len(named) * slots), BF16),
        compiler_params=params(24),
        cost_estimate=COST,
        name="picked",
    )(ids)


def compact_kernel(tokens_ref, piece_ref, pick_ref, out_ref):
    share, features = piece_ref.shape[0], tokens_ref.shape[1]
    slots = pick_ref.shape[1] // share
    for k in range(share):
        product = lax.dot_general(piece_ref[k, :, :features], tokens_ref[...], LAST, preferred_element_type=F32)
        columns = slice(k * slots, (k + 1) * slots)
        kept = jnp.dot(product.astype(BF16), pick_ref[:, columns], preferred_element_type=F32)
        out_ref[:, columns] = kept.astype(BF16)


def compact(tokens, piece, pick):
    return pl.pallas_call(
        compact_kernel,
        in_specs=[VMEM] * 3,
        out_specs=VMEM,
        out_shape=jax.ShapeDtypeStruct((piece.shape[1], pick.shape[1]), BF16),
        compiler_params=params(24),
        cost_estimate=lasting(2),
        name="compact",
    )(tokens, piece, pick)


def most_kernel(mine_ref, theirs_ref, up_ref, mask_ref, near_ref, scale_ref, bits_ref, matrix_ref, *refs):
    low = (mine_ref[...].astype(F32) + theirs_ref[...].astype(F32)).astype(BF16).T
    rank, columns = low.shape[1], mask_ref.shape[1]
    signs = (1 - 2 * bits_ref[...]).astype(F32)
    ups = [up_ref[...]]
    for k in range(near_ref.shape[0]):
        turned = rotate(near_ref[k].astype(F32), signs, matrix_ref[...])
        ups.append(jnp.concatenate(turned, axis=1).astype(BF16))
    missing = columns - sum(up.shape[0] for up in ups)
    if missing:
        ups.append(jnp.zeros((missing, up_ref.shape[1]), BF16))
    spread = jnp.concatenate([low] * (columns // rank), axis=1) * mask_ref[...]
    delta = jnp.dot(spread, jnp.concatenate(ups, axis=0), preferred_element_type=F32)
    value = functools.reduce(jnp.add, [ref[...].astype(F32) for ref in refs[:-1]]) * scale_ref[...]
    refs[-1][...] = jnp.concatenate(rotate(value, signs, matrix_ref[...]), axis=1) + delta


def most(mine, theirs, up, mask, near, scale, bits, matrix, terms):
    return pl.pallas_call(
        most_kernel,
        in_specs=[VMEM] * (8 + len(terms)),
        out_specs=VMEM,
        out_shape=jax.ShapeDtypeStruct(terms[0].shape, F32),
        compiler_params=params(32),
        cost_estimate=COST,
        name="most",
    )(mine, theirs, up, mask, near, scale, bits, matrix, *terms)


def final_kernel(pick_ref, piece_ref, bits_ref, matrix_ref, most_ref, *refs):
    kept_refs, out_ref = refs[:-1], refs[-1]
    share, width = piece_ref.shape[0], out_ref.shape[1]
    features, slots = piece_ref.shape[2] - width, pick_ref.shape[1] // share
    signs = (1 - 2 * bits_ref[...]).astype(F32)
    low = functools.reduce(jnp.add, [ref[...].astype(F32) for ref in kept_refs]).astype(BF16).T
    deltas = []
    for k in range(share):
        turned = rotate(piece_ref[k, :, features:].astype(F32), signs, matrix_ref[...])
        up = jnp.concatenate(turned, axis=1).astype(BF16)
        deltas.append(jnp.dot(low[k * slots : (k + 1) * slots], up, preferred_element_type=F32).astype(BF16))
    delta = deltas[0] if share == 1 else jnp.concatenate(deltas, axis=0)
    result = most_ref[...] + jnp.dot(pick_ref[...], delta, preferred_element_type=F32)
    out_ref[...] = result.astype(BF16)


def final(kept, pick, piece, bits, matrix, rest):
    return pl.pallas_call(
        final_kernel,
        in_specs=[VMEM] * (5 + len(kept)),
        out_specs=VMEM,
        out_shape=jax.ShapeDtypeStruct(rest.shape, BF16),
        compiler_params=params(32),
        cost_estimate=COST,
        name="final",
    )(pick, piece, bits, matrix, rest, *kept)


def local(tokens, adapter_ids, base_weight, channel_scale, adapter_down, adapter_up, sign_bits):
    planes, groups, parts = lax.axis_size("adp"), lax.axis_size("grp"), lax.axis_size("tp")
    features = tokens.shape[1]
    here, _, rank = adapter_down.shape
    width = adapter_up.shape[2]
    share = here // groups
    matrix = hadamard(sign_bits.shape[0])
    bits, scale, ids = sign_bits[None, :], channel_scale[None, :], adapter_ids.T
    down = jnp.swapaxes(adapter_down, 1, 2)

    start = lax.axis_index("grp") * share
    own = lax.dynamic_slice_in_dim(down, start, share, 0)
    near = swap(own, "adp", 1)
    mine = [(0, jnp.concatenate([own, lax.dynamic_slice_in_dim(adapter_up, start, share, 0)], axis=2))]
    bit = planes // 2
    while bit > 1:
        mine += [(plane | bit, swap(piece, "adp", bit)) for plane, piece in mine]
        bit //= 2
    half = parts // 2
    offsets = (*range(1, parts, 2), *range(2, parts, 2))
    blocks = list(partials(tokens, base_weight, parts, offsets, lasting(4)))
    near, blocks[-1] = together(near, blocks[-1])
    (block,) = partials(tokens, base_weight, parts, (0,), COST, blocks[-1])
    close, block, *far = together(near, block, *(piece for _, piece in mine[1:]))
    blocks = blocks[:half] + [block] + blocks[half:]
    mine = mine[:1] + [(plane, piece) for (plane, _), piece in zip(mine[1:], far)]
    odd = [(1, near)] + [(plane | 1, swap(piece, "adp", 1)) for plane, piece in mine[1:]]

    def others(pieces):
        return [(plane, off, swap(piece, "grp", off)) for plane, piece in pieces for off in range(1, groups)]

    swapped = others(odd[:1]) + others(mine[1:]) + others(odd[1:])
    held = [(plane, 0, piece) for plane, piece in [(1, close)] + mine[1:] + odd[1:]]

    def terms(pieces, start):
        return [(start + i, k, 0, (plane, off, k)) for i, (plane, off, _) in enumerate(pieces) for k in range(share)]

    def more(low, pieces, dtype, cost=COST):
        arrays, every = [p for *_, p in pieces], terms(pieces, 0)
        if low is None:
            every += [(len(arrays), k, 0, ("plane", 0, k)) for k in range(here)]
            arrays = arrays + [down]
        return low_rows(ids, tokens, here, share, [((0, features), every)], arrays, low, dtype, cost)

    low = more(None, held[: len(mine)] + swapped[:1], F32, lasting(2))
    slots = -(-2 * tokens.shape[0] // (here * planes) // 128) * 128
    last = swapped[-1]
    pick = picked(ids, here, share, [(last[0], last[1], k) for k in range(share)], slots)
    low, pick, *came = together(low, pick, *(swap(block, "tp", 1) for block in blocks[:half]))

    def both(low):
        bit = 1
        while bit < parts // 2:
            low = add(low, swap(low, "tp", bit))
            bit *= 2
        return low, swap(low, "tp", bit)

    rest = held[len(mine) :]
    low = more(low, swapped[1:-1] + rest, BF16, lasting(5))
    low, up = together(low, adapter_up)
    near_up = swap(up, "adp", 1)
    low, other = both(low)

    sums = [[block, pair] for block, pair in zip(blocks[half:], came)]
    bit = 2
    while bit < parts:
        came = [swap(add(*terms), "tp", bit) for terms in sums[1::2]]
        sums = [terms + [pair] for terms, pair in zip(sums[0::2], came)]
        bit *= 2

    far = [one for one in held + swapped[:-1] if one[0] > 1]
    named = [("plane", 0, k) for k in range(here)]
    named += [(plane, off, k) for plane, off, _ in far for k in range(share)]
    ups = [(0, k, 0) for k in range(here)] + [(1 + i, k, features) for i in range(len(far)) for k in range(share)]
    named += [("plane", 1, k) for k in range(here)]
    arrays = [adapter_up] + [piece for *_, piece in far]
    up, mask = rotated_ups(ids, bits, matrix, here, share, named, ups, arrays, width)

    piece, up, mask = together(last[2], up, mask)
    kept = compact(tokens, piece, pick)
    kept = [kept] + [swap(kept, "tp", offset) for offset in range(1, parts)]
    rest = most(low, other, up, mask, near_up, scale, bits, matrix, sums[0])
    return final(kept, pick, piece, bits, matrix, rest)


def solution(mesh):
    return jax.shard_map(
        local,
        mesh=mesh,
        in_specs=(
            P(("grp", "adp"), "tp"),
            P(("grp", "adp"), None),
            P("tp", None),
            P("tp"),
            P("adp", "tp", None),
            P("adp", None, "tp"),
            P(),
        ),
        out_specs=P(("grp", "adp"), "tp"),
        check_vma=False,
    )
```

```python
import functools

import jax
import jax.numpy as jnp
import numpy as np
from jax import lax
from jax.experimental import pallas as pl
from jax.experimental.pallas import tpu as pltpu
from jax.sharding import PartitionSpec as P

VMEM = pl.BlockSpec(memory_space=pltpu.VMEM)
SMEM = pl.BlockSpec(memory_space=pltpu.SMEM)
F32, BF16 = jnp.float32, jnp.bfloat16
LAST = (((1,), (1,)), ((), ()))
FIRST = (((0,), (0,)), ((), ()))


def params(mib):
    return pltpu.CompilerParams(vmem_limit_bytes=mib << 20)


COST = pl.CostEstimate(flops=1, bytes_accessed=1, transcendentals=0)


def lasting(microseconds):
    return pl.CostEstimate(flops=int(microseconds * 1e9), bytes_accessed=1, transcendentals=0)


def hadamard(size):
    index = np.arange(size)
    shared = index[:, None] & index[None, :]
    parity = np.zeros_like(shared)
    while shared.any():
        parity, shared = parity ^ (shared & 1), shared >> 1
    return jnp.asarray(1 - 2 * parity, BF16)


def swap(x, axis, bit):
    return lax.ppermute(x, axis, [(i, i ^ bit) for i in range(lax.axis_size(axis))])


def together(*values):
    return lax.optimization_barrier(values)


def rotate(value, signs, matrix):
    head = matrix.shape[0]
    scale = signs * (1.0 / np.sqrt(head))
    turned = []
    for at in range(0, value.shape[1], head):
        signed = value[:, at : at + head] * scale
        high = signed.astype(BF16)
        rest = (signed - high.astype(F32)).astype(BF16)
        turned.append(
            jnp.dot(high, matrix, preferred_element_type=F32) + jnp.dot(rest, matrix, preferred_element_type=F32)
        )
    return turned


def partial_kernel(offsets, parts, tokens_ref, weight_ref, *refs):
    me, width = lax.axis_index("tp"), weight_ref.shape[1] // parts
    for offset, out_ref in zip(offsets, refs[-len(offsets) :]):
        at = pl.multiple_of(jnp.bitwise_xor(me, offset) * width, width)
        product = jnp.dot(tokens_ref[...], weight_ref[:, pl.ds(at, width)], preferred_element_type=F32)
        out_ref[...] = product.astype(BF16)


def partials(tokens, weight, parts, offsets, cost, *before):
    block = jax.ShapeDtypeStruct((tokens.shape[0], weight.shape[1] // parts), BF16)
    return pl.pallas_call(
        functools.partial(partial_kernel, offsets, parts),
        in_specs=[VMEM] * (2 + len(before)),
        out_specs=[VMEM] * len(offsets),
        out_shape=[block] * len(offsets),
        compiler_params=params(24),
        cost_estimate=cost,
        name="partials",
    )(tokens, weight, *before)


def add_kernel(*refs):
    total = refs[0][...].astype(F32)
    for ref in refs[1:-1]:
        total = total + ref[...].astype(F32)
    refs[-1][...] = total.astype(BF16)


def add(*terms):
    return pl.pallas_call(
        add_kernel,
        in_specs=[VMEM] * len(terms),
        out_specs=VMEM,
        out_shape=jax.ShapeDtypeStruct(terms[0].shape, BF16),
        compiler_params=params(16),
        cost_estimate=COST,
        name="add",
    )(*terms)


def adapter(here, share, name):
    z = lax.axis_index("adp")
    if name[0] == "plane":
        return jnp.bitwise_xor(z, name[1]) * here + name[2]
    plane, off, k = name
    return jnp.bitwise_xor(z, plane) * here + jnp.bitwise_xor(lax.axis_index("grp"), off) * share + k


def low_kernel(groups, here, share, rank, more, ids_ref, tokens_ref, *refs):
    out_ref = refs[-1]
    total = refs[-2][...] if more else None
    for (start, stop), terms in groups:
        rows = [refs[i][k, :, cut : cut + stop - start] for i, k, cut, _ in terms]
        joined = rows[0] if len(rows) == 1 else jnp.concatenate(rows, axis=0)
        product = lax.dot_general(joined, tokens_ref[:, start:stop], LAST, preferred_element_type=F32)
        for n, (_, _, _, name) in enumerate(terms):
            mine = ids_ref[...] == adapter(here, share, name)
            term = jnp.where(mine, product[n * rank : (n + 1) * rank], 0.0)
            total = term if total is None else total + term
    out_ref[...] = total.astype(out_ref.dtype)


def low_rows(ids, tokens, here, share, groups, arrays, before, dtype, cost=COST):
    rank = arrays[0].shape[1]
    more = [] if before is None else [before]
    return pl.pallas_call(
        functools.partial(low_kernel, groups, here, share, rank, bool(more)),
        in_specs=[VMEM] * (2 + len(arrays) + len(more)),
        out_specs=VMEM,
        out_shape=jax.ShapeDtypeStruct((rank, tokens.shape[0]), dtype),
        compiler_params=params(24),
        cost_estimate=cost,
        name="low_rows",
    )(ids, tokens, *arrays, *more)


def ups_kernel(named, terms, here, share, rank, ids_ref, bits_ref, matrix_ref, *refs):
    up_ref, mask_ref = refs[-2:]
    width = up_ref.shape[1]
    signs = (1 - 2 * bits_ref[...]).astype(F32)
    for n, (i, k, cut) in enumerate(terms):
        turned = rotate(refs[i][k, :, cut : cut + width].astype(F32), signs, matrix_ref[...])
        up_ref[n * rank : (n + 1) * rank, :] = jnp.concatenate(turned, axis=1).astype(BF16)
    ids = jnp.broadcast_to(ids_ref[...], (rank, ids_ref.shape[1])).T
    mask_ref[...] = jnp.zeros_like(mask_ref)
    for n, name in enumerate(named):
        mine = ids == adapter(here, share, name)
        mask_ref[:, n * rank : (n + 1) * rank] = jnp.where(mine, 1.0, 0.0).astype(BF16)


def rotated_ups(ids, bits, matrix, here, share, named, terms, arrays, width):
    rank, rows = arrays[0].shape[1], ids.shape[1]
    columns = -(-len(named) * rank // 128) * 128
    return pl.pallas_call(
        functools.partial(ups_kernel, named, terms, here, share, rank),
        in_specs=[VMEM] * (3 + len(arrays)),
        out_specs=[VMEM, VMEM],
        out_shape=[jax.ShapeDtypeStruct((len(terms) * rank, width), BF16), jax.ShapeDtypeStruct((rows, columns), BF16)],
        compiler_params=params(32),
        cost_estimate=COST,
        name="rotated_ups",
    )(ids, bits, matrix, *arrays)


def pick_kernel(named, here, share, ids_ref, tokens_ref, pick_ref, chosen_ref):
    rows, slots = pick_ref.shape[0], pick_ref.shape[1] // len(named)
    earlier = lax.broadcasted_iota(jnp.int32, (rows, rows), 0) < lax.broadcasted_iota(jnp.int32, (rows, rows), 1)
    earlier = jnp.where(earlier, 1.0, 0.0).astype(BF16)
    ids = jnp.broadcast_to(ids_ref[...], (8, rows))
    for k, name in enumerate(named):
        mine = ids == adapter(here, share, name)
        rank = jnp.dot(jnp.where(mine, 1.0, 0.0).astype(BF16), earlier, preferred_element_type=F32)
        rank = jnp.where(mine, rank, -1.0)
        rank = jnp.broadcast_to(rank[:1], (128, rows)).T
        for at in range(0, slots, 128):
            slot = (lax.broadcasted_iota(jnp.int32, (rows, 128), 1) + at).astype(F32)
            pick_ref[:, k * slots + at : k * slots + at + 128] = jnp.where(rank == slot, 1.0, 0.0).astype(BF16)
    rows = lax.dot_general(pick_ref[...], tokens_ref[...], FIRST, preferred_element_type=F32)
    chosen_ref[...] = rows.astype(BF16)


def picked(ids, tokens, here, share, named, slots):
    rows, features = tokens.shape
    columns = len(named) * slots
    return pl.pallas_call(
        functools.partial(pick_kernel, named, here, share),
        in_specs=[VMEM] * 2,
        out_specs=[VMEM] * 2,
        out_shape=[jax.ShapeDtypeStruct((rows, columns), BF16), jax.ShapeDtypeStruct((columns, features), BF16)],
        compiler_params=params(24),
        cost_estimate=COST,
        name="picked",
    )(ids, tokens)


def compact_kernel(chosen_ref, piece_ref, out_ref):
    share, features = piece_ref.shape[0], chosen_ref.shape[1]
    slots = chosen_ref.shape[0] // share
    for k in range(share):
        mine = slice(k * slots, (k + 1) * slots)
        product = lax.dot_general(
            piece_ref[k, :, :features], chosen_ref[mine], LAST, preferred_element_type=F32
        )
        out_ref[:, mine] = product.astype(BF16)


def compact(chosen, piece):
    return pl.pallas_call(
        compact_kernel,
        in_specs=[VMEM] * 2,
        out_specs=VMEM,
        out_shape=jax.ShapeDtypeStruct((piece.shape[1], chosen.shape[0]), BF16),
        compiler_params=params(24),
        cost_estimate=lasting(2),
        name="compact",
    )(chosen, piece)


def most_kernel(mine_ref, theirs_ref, up_ref, mask_ref, near_ref, scale_ref, bits_ref, matrix_ref, *refs):
    low = (mine_ref[...].astype(F32) + theirs_ref[...].astype(F32)).astype(BF16).T
    rank, columns = low.shape[1], mask_ref.shape[1]
    signs = (1 - 2 * bits_ref[...]).astype(F32)
    ups = [up_ref[...]]
    for k in range(near_ref.shape[0]):
        turned = rotate(near_ref[k].astype(F32), signs, matrix_ref[...])
        ups.append(jnp.concatenate(turned, axis=1).astype(BF16))
    missing = columns - sum(up.shape[0] for up in ups)
    if missing:
        ups.append(jnp.zeros((missing, up_ref.shape[1]), BF16))
    spread = jnp.concatenate([low] * (columns // rank), axis=1) * mask_ref[...]
    delta = jnp.dot(spread, jnp.concatenate(ups, axis=0), preferred_element_type=F32)
    value = functools.reduce(jnp.add, [ref[...].astype(F32) for ref in refs[:-1]]) * scale_ref[...]
    refs[-1][...] = jnp.concatenate(rotate(value, signs, matrix_ref[...]), axis=1) + delta


def most(mine, theirs, up, mask, near, scale, bits, matrix, terms):
    return pl.pallas_call(
        most_kernel,
        in_specs=[VMEM] * (8 + len(terms)),
        out_specs=VMEM,
        out_shape=jax.ShapeDtypeStruct(terms[0].shape, F32),
        compiler_params=params(32),
        cost_estimate=COST,
        name="most",
    )(mine, theirs, up, mask, near, scale, bits, matrix, *terms)


def final_kernel(pick_ref, piece_ref, bits_ref, matrix_ref, most_ref, *refs):
    kept_refs, (out_ref, half_ref, sems) = refs[:-3], refs[-3:]
    share, width = piece_ref.shape[0], out_ref.shape[1]
    features, slots = piece_ref.shape[2] - width, pick_ref.shape[1] // share
    signs = (1 - 2 * bits_ref[...]).astype(F32)
    low = functools.reduce(jnp.add, [ref[...].astype(F32) for ref in kept_refs]).astype(BF16).T
    deltas = []
    for k in range(share):
        turned = rotate(piece_ref[k, :, features:].astype(F32), signs, matrix_ref[...])
        up = jnp.concatenate(turned, axis=1).astype(BF16)
        deltas.append(jnp.dot(low[k * slots : (k + 1) * slots], up, preferred_element_type=F32).astype(BF16))
    delta = deltas[0] if share == 1 else jnp.concatenate(deltas, axis=0)
    count, rows, _ = half_ref.shape
    copies = []
    for n in range(count):
        part = slice(n * rows, (n + 1) * rows)
        result = most_ref[part] + jnp.dot(pick_ref[part], delta, preferred_element_type=F32)
        half_ref[n] = result.astype(BF16)
        copies.append(pltpu.make_async_copy(half_ref.at[n], out_ref.at[pl.ds(n * rows, rows)], sems.at[n]))
        copies[-1].start()
    for copy in copies:
        copy.wait()


def final(kept, pick, piece, bits, matrix, rest):
    return pl.pallas_call(
        final_kernel,
        in_specs=[VMEM] * (5 + len(kept)),
        out_specs=pl.BlockSpec(memory_space=pl.ANY),
        out_shape=jax.ShapeDtypeStruct(rest.shape, BF16),
        scratch_shapes=[pltpu.VMEM((2, rest.shape[0] // 2, rest.shape[1]), BF16), pltpu.SemaphoreType.DMA((2,))],
        compiler_params=params(32),
        cost_estimate=COST,
        name="final",
    )(pick, piece, bits, matrix, rest, *kept)


def local(tokens, adapter_ids, base_weight, channel_scale, adapter_down, adapter_up, sign_bits):
    planes, groups, parts = lax.axis_size("adp"), lax.axis_size("grp"), lax.axis_size("tp")
    features = tokens.shape[1]
    here, _, rank = adapter_down.shape
    width = adapter_up.shape[2]
    share = here // groups
    matrix = hadamard(sign_bits.shape[0])
    bits, scale, ids = sign_bits[None, :], channel_scale[None, :], adapter_ids.T
    down = jnp.swapaxes(adapter_down, 1, 2)

    start = lax.axis_index("grp") * share
    own = lax.dynamic_slice_in_dim(down, start, share, 0)
    near = swap(own, "adp", 1)
    mine = [(0, jnp.concatenate([own, lax.dynamic_slice_in_dim(adapter_up, start, share, 0)], axis=2))]
    bit = planes // 2
    while bit > 1:
        mine += [(plane | bit, swap(piece, "adp", bit)) for plane, piece in mine]
        bit //= 2
    half = parts // 2
    offsets = (*range(1, parts, 2), *range(2, parts, 2))
    blocks = list(partials(tokens, base_weight, parts, offsets, lasting(4)))
    near, blocks[-1] = together(near, blocks[-1])
    (block,) = partials(tokens, base_weight, parts, (0,), COST, blocks[-1])
    slots = -(-2 * tokens.shape[0] // (here * planes) // 128) * 128
    lasts = [(planes - 1, groups - 1, k) for k in range(share)]
    pick, chosen = picked(ids, tokens, here, share, lasts, slots)
    close, block, pick, chosen, *far = together(near, block, pick, chosen, *(piece for _, piece in mine[1:]))
    blocks = blocks[:half] + [block] + blocks[half:]
    mine = mine[:1] + [(plane, piece) for (plane, _), piece in zip(mine[1:], far)]
    odd = [(1, near)] + [(plane | 1, swap(piece, "adp", 1)) for plane, piece in mine[1:]]

    def others(pieces):
        return [(plane, off, swap(piece, "grp", off)) for plane, piece in pieces for off in range(1, groups)]

    swapped = others(odd[:1]) + others(mine[1:]) + others(odd[1:])
    held = [(plane, 0, piece) for plane, piece in [(1, close)] + mine[1:] + odd[1:]]

    def terms(pieces, start):
        return [(start + i, k, 0, (plane, off, k)) for i, (plane, off, _) in enumerate(pieces) for k in range(share)]

    def more(low, pieces, dtype, cost=COST):
        arrays, every = [p for *_, p in pieces], terms(pieces, 0)
        if low is None:
            every += [(len(arrays), k, 0, ("plane", 0, k)) for k in range(here)]
            arrays = arrays + [down]
        return low_rows(ids, tokens, here, share, [((0, features), every)], arrays, low, dtype, cost)

    low = more(None, held[: len(mine)] + swapped[:1], F32, lasting(2))
    low, *came = together(low, *(swap(block, "tp", 1) for block in blocks[:half]))

    def both(low):
        bit = 1
        while bit < parts // 2:
            low = add(low, swap(low, "tp", bit))
            bit *= 2
        return low, swap(low, "tp", bit)

    rest = held[len(mine) :]
    low = more(low, swapped[1:-1] + rest, BF16, lasting(5))
    low, up = together(low, adapter_up)
    near_up = swap(up, "adp", 1)
    low, other = both(low)

    sums = [[block, pair] for block, pair in zip(blocks[half:], came)]
    bit = 2
    while bit < parts:
        came = [swap(add(*terms), "tp", bit) for terms in sums[1::2]]
        sums = [terms + [pair] for terms, pair in zip(sums[0::2], came)]
        bit *= 2

    far = [one for one in held + swapped[:-1] if one[0] > 1]
    named = [("plane", 0, k) for k in range(here)]
    named += [(plane, off, k) for plane, off, _ in far for k in range(share)]
    ups = [(0, k, 0) for k in range(here)] + [(1 + i, k, features) for i in range(len(far)) for k in range(share)]
    named += [("plane", 1, k) for k in range(here)]
    arrays = [adapter_up] + [piece for *_, piece in far]
    up, mask = rotated_ups(ids, bits, matrix, here, share, named, ups, arrays, width)

    piece, up, mask = together(swapped[-1][2], up, mask)
    kept = compact(chosen, piece)
    kept = [kept] + [swap(kept, "tp", offset) for offset in range(1, parts)]
    rest = most(low, other, up, mask, near_up, scale, bits, matrix, sums[0])
    return final(kept, pick, piece, bits, matrix, rest)


def solution(mesh):
    return jax.shard_map(
        local,
        mesh=mesh,
        in_specs=(
            P(("grp", "adp"), "tp"),
            P(("grp", "adp"), None),
            P("tp", None),
            P("tp"),
            P("adp", "tp", None),
            P("adp", None, "tp"),
            P(),
        ),
        out_specs=P(("grp", "adp"), "tp"),
        check_vma=False,
    )
```

```python
import functools

import jax
import jax.numpy as jnp
import numpy as np
from jax import lax
from jax.experimental import pallas as pl
from jax.experimental.pallas import tpu as pltpu
from jax.sharding import PartitionSpec as P

VMEM = pl.BlockSpec(memory_space=pltpu.VMEM)
SMEM = pl.BlockSpec(memory_space=pltpu.SMEM)
F32, BF16 = jnp.float32, jnp.bfloat16
LAST = (((1,), (1,)), ((), ()))
FIRST = (((0,), (0,)), ((), ()))


def params(mib):
    return pltpu.CompilerParams(vmem_limit_bytes=mib << 20)


COST = pl.CostEstimate(flops=1, bytes_accessed=1, transcendentals=0)


def lasting(microseconds):
    return pl.CostEstimate(flops=int(microseconds * 1e9), bytes_accessed=1, transcendentals=0)


def hadamard(size):
    index = np.arange(size)
    shared = index[:, None] & index[None, :]
    parity = np.zeros_like(shared)
    while shared.any():
        parity, shared = parity ^ (shared & 1), shared >> 1
    return jnp.asarray(1 - 2 * parity, BF16)


def swap(x, axis, bit):
    return lax.ppermute(x, axis, [(i, i ^ bit) for i in range(lax.axis_size(axis))])


def together(*values):
    return lax.optimization_barrier(values)


def rotate(value, signs, matrix):
    head = matrix.shape[0]
    scale = signs * (1.0 / np.sqrt(head))
    turned = []
    for at in range(0, value.shape[1], head):
        signed = value[:, at : at + head] * scale
        high = signed.astype(BF16)
        rest = (signed - high.astype(F32)).astype(BF16)
        turned.append(
            jnp.dot(high, matrix, preferred_element_type=F32) + jnp.dot(rest, matrix, preferred_element_type=F32)
        )
    return turned


def partial_kernel(offsets, parts, tokens_ref, weight_ref, *refs):
    me, width = lax.axis_index("tp"), weight_ref.shape[1] // parts
    for offset, out_ref in zip(offsets, refs[-len(offsets) :]):
        at = pl.multiple_of(jnp.bitwise_xor(me, offset) * width, width)
        product = jnp.dot(tokens_ref[...], weight_ref[:, pl.ds(at, width)], preferred_element_type=F32)
        out_ref[...] = product.astype(BF16)


def partials(tokens, weight, parts, offsets, cost, *before):
    block = jax.ShapeDtypeStruct((tokens.shape[0], weight.shape[1] // parts), BF16)
    return pl.pallas_call(
        functools.partial(partial_kernel, offsets, parts),
        in_specs=[VMEM] * (2 + len(before)),
        out_specs=[VMEM] * len(offsets),
        out_shape=[block] * len(offsets),
        compiler_params=params(24),
        cost_estimate=cost,
        name="partials",
    )(tokens, weight, *before)


def add_kernel(*refs):
    total = refs[0][...].astype(F32)
    for ref in refs[1:-1]:
        total = total + ref[...].astype(F32)
    refs[-1][...] = total.astype(BF16)


def add(*terms):
    return pl.pallas_call(
        add_kernel,
        in_specs=[VMEM] * len(terms),
        out_specs=VMEM,
        out_shape=jax.ShapeDtypeStruct(terms[0].shape, BF16),
        compiler_params=params(16),
        cost_estimate=COST,
        name="add",
    )(*terms)


def adapter(here, share, name):
    z = lax.axis_index("adp")
    if name[0] == "plane":
        return jnp.bitwise_xor(z, name[1]) * here + name[2]
    plane, off, k = name
    return jnp.bitwise_xor(z, plane) * here + jnp.bitwise_xor(lax.axis_index("grp"), off) * share + k


def low_kernel(groups, here, share, rank, more, ids_ref, tokens_ref, *refs):
    out_ref = refs[-1]
    total = refs[-2][...] if more else None
    for (start, stop), terms in groups:
        rows = [refs[i][k, :, cut : cut + stop - start] for i, k, cut, _ in terms]
        joined = rows[0] if len(rows) == 1 else jnp.concatenate(rows, axis=0)
        product = lax.dot_general(joined, tokens_ref[:, start:stop], LAST, preferred_element_type=F32)
        for n, (_, _, _, name) in enumerate(terms):
            mine = ids_ref[...] == adapter(here, share, name)
            term = jnp.where(mine, product[n * rank : (n + 1) * rank], 0.0)
            total = term if total is None else total + term
    out_ref[...] = total.astype(out_ref.dtype)


def low_rows(ids, tokens, here, share, groups, arrays, before, dtype, cost=COST):
    rank = arrays[0].shape[1]
    more = [] if before is None else [before]
    return pl.pallas_call(
        functools.partial(low_kernel, groups, here, share, rank, bool(more)),
        in_specs=[VMEM] * (2 + len(arrays) + len(more)),
        out_specs=VMEM,
        out_shape=jax.ShapeDtypeStruct((rank, tokens.shape[0]), dtype),
        compiler_params=params(24),
        cost_estimate=cost,
        name="low_rows",
    )(ids, tokens, *arrays, *more)


def ups_kernel(named, terms, here, share, rank, ids_ref, bits_ref, matrix_ref, *refs):
    up_ref, mask_ref = refs[-2:]
    width = up_ref.shape[1]
    signs = (1 - 2 * bits_ref[...]).astype(F32)
    for n, (i, k, cut) in enumerate(terms):
        turned = rotate(refs[i][k, :, cut : cut + width].astype(F32), signs, matrix_ref[...])
        up_ref[n * rank : (n + 1) * rank, :] = jnp.concatenate(turned, axis=1).astype(BF16)
    ids = jnp.broadcast_to(ids_ref[...], (rank, ids_ref.shape[1])).T
    mask_ref[...] = jnp.zeros_like(mask_ref)
    for n, name in enumerate(named):
        mine = ids == adapter(here, share, name)
        mask_ref[:, n * rank : (n + 1) * rank] = jnp.where(mine, 1.0, 0.0).astype(BF16)


def rotated_ups(ids, bits, matrix, here, share, named, terms, arrays, width):
    rank, rows = arrays[0].shape[1], ids.shape[1]
    columns = -(-len(named) * rank // 128) * 128
    return pl.pallas_call(
        functools.partial(ups_kernel, named, terms, here, share, rank),
        in_specs=[VMEM] * (3 + len(arrays)),
        out_specs=[VMEM, VMEM],
        out_shape=[jax.ShapeDtypeStruct((len(terms) * rank, width), BF16), jax.ShapeDtypeStruct((rows, columns), BF16)],
        compiler_params=params(32),
        cost_estimate=COST,
        name="rotated_ups",
    )(ids, bits, matrix, *arrays)


def pick_kernel(named, here, share, ids_ref, tokens_ref, pick_ref, chosen_ref):
    rows, slots = pick_ref.shape[0], pick_ref.shape[1] // len(named)
    earlier = lax.broadcasted_iota(jnp.int32, (rows, rows), 0) < lax.broadcasted_iota(jnp.int32, (rows, rows), 1)
    earlier = jnp.where(earlier, 1.0, 0.0).astype(BF16)
    ids = jnp.broadcast_to(ids_ref[...], (8, rows))
    for k, name in enumerate(named):
        mine = ids == adapter(here, share, name)
        rank = jnp.dot(jnp.where(mine, 1.0, 0.0).astype(BF16), earlier, preferred_element_type=F32)
        rank = jnp.where(mine, rank, -1.0)
        rank = jnp.broadcast_to(rank[:1], (128, rows)).T
        for at in range(0, slots, 128):
            slot = (lax.broadcasted_iota(jnp.int32, (rows, 128), 1) + at).astype(F32)
            pick_ref[:, k * slots + at : k * slots + at + 128] = jnp.where(rank == slot, 1.0, 0.0).astype(BF16)
    rows = lax.dot_general(pick_ref[...], tokens_ref[...], FIRST, preferred_element_type=F32)
    chosen_ref[...] = rows.astype(BF16)


def picked(ids, tokens, here, share, named, slots):
    rows, features = tokens.shape
    columns = len(named) * slots
    return pl.pallas_call(
        functools.partial(pick_kernel, named, here, share),
        in_specs=[VMEM] * 2,
        out_specs=[VMEM] * 2,
        out_shape=[jax.ShapeDtypeStruct((rows, columns), BF16), jax.ShapeDtypeStruct((columns, features), BF16)],
        compiler_params=params(24),
        cost_estimate=COST,
        name="picked",
    )(ids, tokens)


def compact_kernel(chosen_ref, piece_ref, out_ref):
    share, features = piece_ref.shape[0], chosen_ref.shape[1]
    slots = chosen_ref.shape[0] // share
    for k in range(share):
        mine = slice(k * slots, (k + 1) * slots)
        product = lax.dot_general(
            piece_ref[k, :, :features], chosen_ref[mine], LAST, preferred_element_type=F32
        )
        out_ref[:, mine] = product.astype(BF16)


def compact(chosen, piece):
    return pl.pallas_call(
        compact_kernel,
        in_specs=[VMEM] * 2,
        out_specs=VMEM,
        out_shape=jax.ShapeDtypeStruct((piece.shape[1], chosen.shape[0]), BF16),
        compiler_params=params(24),
        cost_estimate=lasting(2),
        name="compact",
    )(chosen, piece)


def most_kernel(mine_ref, theirs_ref, up_ref, mask_ref, near_ref, piece_ref, scale_ref, bits_ref, matrix_ref, *refs):
    terms, (last_ref, out_ref) = refs[:-2], refs[-2:]
    rank, width = piece_ref.shape[1], out_ref.shape[1]
    low = (mine_ref[...].astype(F32) + theirs_ref[...].astype(F32)).astype(BF16).T
    columns = mask_ref.shape[1]
    signs = (1 - 2 * bits_ref[...]).astype(F32)
    ups = [up_ref[...]]
    for k in range(near_ref.shape[0]):
        turned = rotate(near_ref[k].astype(F32), signs, matrix_ref[...])
        ups.append(jnp.concatenate(turned, axis=1).astype(BF16))
    missing = columns - sum(up.shape[0] for up in ups)
    if missing:
        ups.append(jnp.zeros((missing, up_ref.shape[1]), BF16))
    spread = jnp.concatenate([low] * (columns // rank), axis=1) * mask_ref[...]
    delta = jnp.dot(spread, jnp.concatenate(ups, axis=0), preferred_element_type=F32)
    value = functools.reduce(jnp.add, [ref[...].astype(F32) for ref in terms]) * scale_ref[...]
    out_ref[...] = jnp.concatenate(rotate(value, signs, matrix_ref[...]), axis=1) + delta
    for k in range(piece_ref.shape[0]):
        turned = rotate(piece_ref[k, :, piece_ref.shape[2] - width :].astype(F32), signs, matrix_ref[...])
        last_ref[k * rank : (k + 1) * rank] = jnp.concatenate(turned, axis=1).astype(BF16)


def most(mine, theirs, up, mask, near, piece, scale, bits, matrix, terms):
    return pl.pallas_call(
        most_kernel,
        in_specs=[VMEM] * (9 + len(terms)),
        out_specs=[VMEM] * 2,
        out_shape=[
            jax.ShapeDtypeStruct((piece.shape[0] * piece.shape[1], terms[0].shape[1]), BF16),
            jax.ShapeDtypeStruct(terms[0].shape, F32),
        ],
        compiler_params=params(32),
        cost_estimate=COST,
        name="most",
    )(mine, theirs, up, mask, near, piece, scale, bits, matrix, *terms)


def final_kernel(pick_ref, last_ref, most_ref, *refs):
    kept_refs, (out_ref, half_ref, sems) = refs[:-3], refs[-3:]
    rank, slots = kept_refs[0].shape
    share = last_ref.shape[0] // rank
    slots = slots // share
    low = functools.reduce(jnp.add, [ref[...].astype(F32) for ref in kept_refs]).astype(BF16).T
    deltas = []
    for k in range(share):
        up = last_ref[k * rank : (k + 1) * rank]
        deltas.append(jnp.dot(low[k * slots : (k + 1) * slots], up, preferred_element_type=F32).astype(BF16))
    delta = deltas[0] if share == 1 else jnp.concatenate(deltas, axis=0)
    count, rows, _ = half_ref.shape
    copies = []
    for n in range(count):
        part = slice(n * rows, (n + 1) * rows)
        result = most_ref[part] + jnp.dot(pick_ref[part], delta, preferred_element_type=F32)
        half_ref[n] = result.astype(BF16)
        copies.append(pltpu.make_async_copy(half_ref.at[n], out_ref.at[pl.ds(n * rows, rows)], sems.at[n]))
        copies[-1].start()
    for copy in copies:
        copy.wait()


def final(kept, pick, last, rest):
    return pl.pallas_call(
        final_kernel,
        in_specs=[VMEM] * (3 + len(kept)),
        out_specs=pl.BlockSpec(memory_space=pl.ANY),
        out_shape=jax.ShapeDtypeStruct(rest.shape, BF16),
        scratch_shapes=[pltpu.VMEM((2, rest.shape[0] // 2, rest.shape[1]), BF16), pltpu.SemaphoreType.DMA((2,))],
        compiler_params=params(32),
        cost_estimate=COST,
        name="final",
    )(pick, last, rest, *kept)


def local(tokens, adapter_ids, base_weight, channel_scale, adapter_down, adapter_up, sign_bits):
    planes, groups, parts = lax.axis_size("adp"), lax.axis_size("grp"), lax.axis_size("tp")
    features = tokens.shape[1]
    here, _, rank = adapter_down.shape
    width = adapter_up.shape[2]
    share = here // groups
    matrix = hadamard(sign_bits.shape[0])
    bits, scale, ids = sign_bits[None, :], channel_scale[None, :], adapter_ids.T
    down = jnp.swapaxes(adapter_down, 1, 2)

    start = lax.axis_index("grp") * share
    own = lax.dynamic_slice_in_dim(down, start, share, 0)
    near = swap(own, "adp", 1)
    mine = [(0, jnp.concatenate([own, lax.dynamic_slice_in_dim(adapter_up, start, share, 0)], axis=2))]
    bit = planes // 2
    while bit > 1:
        mine += [(plane | bit, swap(piece, "adp", bit)) for plane, piece in mine]
        bit //= 2
    half = parts // 2
    offsets = (*range(1, parts, 2), *range(2, parts, 2))
    blocks = list(partials(tokens, base_weight, parts, offsets, lasting(4)))
    near, blocks[-1] = together(near, blocks[-1])
    (block,) = partials(tokens, base_weight, parts, (0,), COST, blocks[-1])
    slots = -(-2 * tokens.shape[0] // (here * planes) // 128) * 128
    lasts = [(planes - 1, groups - 1, k) for k in range(share)]
    pick, chosen = picked(ids, tokens, here, share, lasts, slots)
    close, block, pick, chosen, *far = together(near, block, pick, chosen, *(piece for _, piece in mine[1:]))
    blocks = blocks[:half] + [block] + blocks[half:]
    mine = mine[:1] + [(plane, piece) for (plane, _), piece in zip(mine[1:], far)]
    odd = [(1, near)] + [(plane | 1, swap(piece, "adp", 1)) for plane, piece in mine[1:]]

    def others(pieces):
        return [(plane, off, swap(piece, "grp", off)) for plane, piece in pieces for off in range(1, groups)]

    swapped = others(odd[:1]) + others(mine[1:]) + others(odd[1:])
    held = [(plane, 0, piece) for plane, piece in [(1, close)] + mine[1:] + odd[1:]]

    def terms(pieces, start):
        return [(start + i, k, 0, (plane, off, k)) for i, (plane, off, _) in enumerate(pieces) for k in range(share)]

    def more(low, pieces, dtype, cost=COST):
        arrays, every = [p for *_, p in pieces], terms(pieces, 0)
        if low is None:
            every += [(len(arrays), k, 0, ("plane", 0, k)) for k in range(here)]
            arrays = arrays + [down]
        return low_rows(ids, tokens, here, share, [((0, features), every)], arrays, low, dtype, cost)

    low = more(None, held[: len(mine)] + swapped[:1], F32, lasting(2))
    low, *came = together(low, *(swap(block, "tp", 1) for block in blocks[:half]))

    def both(low):
        bit = 1
        while bit < parts // 2:
            low = add(low, swap(low, "tp", bit))
            bit *= 2
        return low, swap(low, "tp", bit)

    rest = held[len(mine) :]
    low = more(low, swapped[1:-1] + rest, BF16, lasting(5))
    low, up = together(low, adapter_up)
    near_up = swap(up, "adp", 1)
    low, other = both(low)

    sums = [[block, pair] for block, pair in zip(blocks[half:], came)]
    bit = 2
    while bit < parts:
        came = [swap(add(*terms), "tp", bit) for terms in sums[1::2]]
        sums = [terms + [pair] for terms, pair in zip(sums[0::2], came)]
        bit *= 2

    far = [one for one in held + swapped[:-1] if one[0] > 1]
    named = [("plane", 0, k) for k in range(here)]
    named += [(plane, off, k) for plane, off, _ in far for k in range(share)]
    ups = [(0, k, 0) for k in range(here)] + [(1 + i, k, features) for i in range(len(far)) for k in range(share)]
    named += [("plane", 1, k) for k in range(here)]
    arrays = [adapter_up] + [piece for *_, piece in far]
    up, mask = rotated_ups(ids, bits, matrix, here, share, named, ups, arrays, width)

    piece, up, mask = together(swapped[-1][2], up, mask)
    kept = compact(chosen, piece)
    kept = [kept] + [swap(kept, "tp", offset) for offset in range(1, parts)]
    last, rest = most(low, other, up, mask, near_up, piece, scale, bits, matrix, sums[0])
    return final(kept, pick, last, rest)


def solution(mesh):
    return jax.shard_map(
        local,
        mesh=mesh,
        in_specs=(
            P(("grp", "adp"), "tp"),
            P(("grp", "adp"), None),
            P("tp", None),
            P("tp"),
            P("adp", "tp", None),
            P("adp", None, "tp"),
            P(),
        ),
        out_specs=P(("grp", "adp"), "tp"),
        check_vma=False,
    )
```

```python
import functools

import jax
import jax.numpy as jnp
import numpy as np
from jax import lax
from jax.experimental import pallas as pl
from jax.experimental.pallas import tpu as pltpu
from jax.sharding import PartitionSpec as P

VMEM = pl.BlockSpec(memory_space=pltpu.VMEM)
SMEM = pl.BlockSpec(memory_space=pltpu.SMEM)
F32, BF16 = jnp.float32, jnp.bfloat16
LAST = (((1,), (1,)), ((), ()))
FIRST = (((0,), (0,)), ((), ()))


def params(mib):
    return pltpu.CompilerParams(vmem_limit_bytes=mib << 20)


COST = pl.CostEstimate(flops=1, bytes_accessed=1, transcendentals=0)


def lasting(microseconds):
    return pl.CostEstimate(flops=int(microseconds * 1e9), bytes_accessed=1, transcendentals=0)


def hadamard(size):
    index = np.arange(size)
    shared = index[:, None] & index[None, :]
    parity = np.zeros_like(shared)
    while shared.any():
        parity, shared = parity ^ (shared & 1), shared >> 1
    return jnp.asarray(1 - 2 * parity, BF16)


def swap(x, axis, bit):
    return lax.ppermute(x, axis, [(i, i ^ bit) for i in range(lax.axis_size(axis))])


def together(*values):
    return lax.optimization_barrier(values)


def rotate(value, signs, matrix):
    head = matrix.shape[0]
    scale = signs * (1.0 / np.sqrt(head))
    turned = []
    for at in range(0, value.shape[1], head):
        signed = value[:, at : at + head] * scale
        high = signed.astype(BF16)
        rest = (signed - high.astype(F32)).astype(BF16)
        turned.append(
            jnp.dot(high, matrix, preferred_element_type=F32) + jnp.dot(rest, matrix, preferred_element_type=F32)
        )
    return turned


def partial_kernel(offsets, parts, tokens_ref, weight_ref, *refs):
    me, width = lax.axis_index("tp"), weight_ref.shape[1] // parts
    for offset, out_ref in zip(offsets, refs[-len(offsets) :]):
        at = pl.multiple_of(jnp.bitwise_xor(me, offset) * width, width)
        product = jnp.dot(tokens_ref[...], weight_ref[:, pl.ds(at, width)], preferred_element_type=F32)
        out_ref[...] = product.astype(BF16)


def partials(tokens, weight, parts, offsets, cost, *before):
    block = jax.ShapeDtypeStruct((tokens.shape[0], weight.shape[1] // parts), BF16)
    return pl.pallas_call(
        functools.partial(partial_kernel, offsets, parts),
        in_specs=[VMEM] * (2 + len(before)),
        out_specs=[VMEM] * len(offsets),
        out_shape=[block] * len(offsets),
        compiler_params=params(24),
        cost_estimate=cost,
        name="partials",
    )(tokens, weight, *before)


def add_kernel(*refs):
    total = refs[0][...].astype(F32)
    for ref in refs[1:-1]:
        total = total + ref[...].astype(F32)
    refs[-1][...] = total.astype(BF16)


def add(*terms):
    return pl.pallas_call(
        add_kernel,
        in_specs=[VMEM] * len(terms),
        out_specs=VMEM,
        out_shape=jax.ShapeDtypeStruct(terms[0].shape, BF16),
        compiler_params=params(16),
        cost_estimate=COST,
        name="add",
    )(*terms)


def adapter(here, share, name):
    z = lax.axis_index("adp")
    if name[0] == "plane":
        return jnp.bitwise_xor(z, name[1]) * here + name[2]
    plane, off, k = name
    return jnp.bitwise_xor(z, plane) * here + jnp.bitwise_xor(lax.axis_index("grp"), off) * share + k


def low_kernel(groups, here, share, rank, more, ids_ref, tokens_ref, *refs):
    out_ref = refs[-1]
    total = refs[-2][...] if more else None
    for (start, stop), terms in groups:
        rows = [refs[i][k, :, cut : cut + stop - start] for i, k, cut, _ in terms]
        joined = rows[0] if len(rows) == 1 else jnp.concatenate(rows, axis=0)
        product = lax.dot_general(joined, tokens_ref[:, start:stop], LAST, preferred_element_type=F32)
        for n, (_, _, _, name) in enumerate(terms):
            mine = ids_ref[...] == adapter(here, share, name)
            term = jnp.where(mine, product[n * rank : (n + 1) * rank], 0.0)
            total = term if total is None else total + term
    out_ref[...] = total.astype(out_ref.dtype)


def low_rows(ids, tokens, here, share, groups, arrays, before, dtype, cost=COST):
    rank = arrays[0].shape[1]
    more = [] if before is None else [before]
    return pl.pallas_call(
        functools.partial(low_kernel, groups, here, share, rank, bool(more)),
        in_specs=[VMEM] * (2 + len(arrays) + len(more)),
        out_specs=VMEM,
        out_shape=jax.ShapeDtypeStruct((rank, tokens.shape[0]), dtype),
        compiler_params=params(24),
        cost_estimate=cost,
        name="low_rows",
    )(ids, tokens, *arrays, *more)


def join_kernel(first_ref, second_ref, out_ref):
    out_ref[: first_ref.shape[0]] = first_ref[...]
    out_ref[first_ref.shape[0] :] = second_ref[...]


def joined(first, second):
    return pl.pallas_call(
        join_kernel,
        in_specs=[VMEM] * 2,
        out_specs=VMEM,
        out_shape=jax.ShapeDtypeStruct((2 * first.shape[0], *first.shape[1:]), BF16),
        compiler_params=params(16),
        cost_estimate=COST,
        name="joined",
    )(first, second)


def ups_kernel(here, share, named, ids_ref, bits_ref, matrix_ref, first_ref, second_ref, up_ref, mask_ref):
    half, rank, _ = first_ref.shape
    signs = (1 - 2 * bits_ref[...]).astype(F32)
    ids = jnp.broadcast_to(ids_ref[...], (rank, ids_ref.shape[1])).T
    for n, name in enumerate(named):
        turned = rotate((first_ref if n < half else second_ref)[n % half].astype(F32), signs, matrix_ref[...])
        up_ref[n * rank : (n + 1) * rank, :] = jnp.concatenate(turned, axis=1).astype(BF16)
        mine = ids == adapter(here, share, name)
        mask_ref[:, n * rank : (n + 1) * rank] = jnp.where(mine, 1.0, 0.0).astype(BF16)


def rotated_ups(ids, bits, matrix, here, share, named, first, second):
    _, rank, width = first.shape
    return pl.pallas_call(
        functools.partial(ups_kernel, here, share, named),
        in_specs=[VMEM] * 5,
        out_specs=[VMEM, VMEM],
        out_shape=[
            jax.ShapeDtypeStruct((len(named) * rank, width), BF16),
            jax.ShapeDtypeStruct((ids.shape[1], len(named) * rank), BF16),
        ],
        compiler_params=params(32),
        cost_estimate=COST,
        name="rotated_ups",
    )(ids, bits, matrix, first, second)


def pick_kernel(named, here, share, ids_ref, tokens_ref, pick_ref, chosen_ref):
    rows, slots = pick_ref.shape[0], pick_ref.shape[1] // len(named)
    earlier = lax.broadcasted_iota(jnp.int32, (rows, rows), 0) < lax.broadcasted_iota(jnp.int32, (rows, rows), 1)
    earlier = jnp.where(earlier, 1.0, 0.0).astype(BF16)
    ids = jnp.broadcast_to(ids_ref[...], (8, rows))
    for k, name in enumerate(named):
        mine = ids == adapter(here, share, name)
        rank = jnp.dot(jnp.where(mine, 1.0, 0.0).astype(BF16), earlier, preferred_element_type=F32)
        rank = jnp.where(mine, rank, -1.0)
        rank = jnp.broadcast_to(rank[:1], (128, rows)).T
        for at in range(0, slots, 128):
            slot = (lax.broadcasted_iota(jnp.int32, (rows, 128), 1) + at).astype(F32)
            pick_ref[:, k * slots + at : k * slots + at + 128] = jnp.where(rank == slot, 1.0, 0.0).astype(BF16)
    rows = lax.dot_general(pick_ref[...], tokens_ref[...], FIRST, preferred_element_type=F32)
    chosen_ref[...] = rows.astype(BF16)


def picked(ids, tokens, here, share, named, slots):
    rows, features = tokens.shape
    columns = len(named) * slots
    return pl.pallas_call(
        functools.partial(pick_kernel, named, here, share),
        in_specs=[VMEM] * 2,
        out_specs=[VMEM] * 2,
        out_shape=[jax.ShapeDtypeStruct((rows, columns), BF16), jax.ShapeDtypeStruct((columns, features), BF16)],
        compiler_params=params(24),
        cost_estimate=COST,
        name="picked",
    )(ids, tokens)


def compact_kernel(chosen_ref, piece_ref, out_ref):
    share, features = piece_ref.shape[0], chosen_ref.shape[1]
    slots = chosen_ref.shape[0] // share
    for k in range(share):
        mine = slice(k * slots, (k + 1) * slots)
        product = lax.dot_general(
            piece_ref[k, :, :features], chosen_ref[mine], LAST, preferred_element_type=F32
        )
        out_ref[:, mine] = product.astype(BF16)


def compact(chosen, piece):
    return pl.pallas_call(
        compact_kernel,
        in_specs=[VMEM] * 2,
        out_specs=VMEM,
        out_shape=jax.ShapeDtypeStruct((piece.shape[1], chosen.shape[0]), BF16),
        compiler_params=params(24),
        cost_estimate=lasting(2),
        name="compact",
    )(chosen, piece)


def most_kernel(share, spots, mine_ref, theirs_ref, up_ref, mask_ref, scale_ref, bits_ref, matrix_ref, *refs):
    terms, (last_ref, out_ref) = refs[:-2], refs[-2:]
    low = (mine_ref[...].astype(F32) + theirs_ref[...].astype(F32)).astype(BF16).T
    rank, columns = low.shape[1], mask_ref.shape[1]
    signs = (1 - 2 * bits_ref[...]).astype(F32)
    spread = jnp.concatenate([low] * (columns // rank), axis=1) * mask_ref[...]
    delta = jnp.dot(spread, up_ref[...], preferred_element_type=F32)
    value = functools.reduce(jnp.add, [ref[...].astype(F32) for ref in terms]) * scale_ref[...]
    out_ref[...] = jnp.concatenate(rotate(value, signs, matrix_ref[...]), axis=1) + delta
    off = jnp.bitwise_xor(lax.axis_index("grp"), lax.axis_size("grp") - 1) * share
    for k, spot in enumerate(spots):
        at = pl.multiple_of((spot + off) * rank, rank)
        last_ref[k * rank : (k + 1) * rank] = up_ref[pl.ds(at, rank)]


def most(mine, theirs, up, mask, scale, bits, matrix, terms, here, share, spots):
    width = up.shape[1]
    return pl.pallas_call(
        functools.partial(most_kernel, share, spots),
        in_specs=[VMEM] * (7 + len(terms)),
        out_specs=[VMEM] * 2,
        out_shape=[
            jax.ShapeDtypeStruct((share * mine.shape[0], width), BF16),
            jax.ShapeDtypeStruct(terms[0].shape, F32),
        ],
        compiler_params=params(32),
        cost_estimate=COST,
        name="most",
    )(mine, theirs, up, mask, scale, bits, matrix, *terms)


def final_kernel(pick_ref, last_ref, most_ref, *refs):
    kept_refs, (out_ref, half_ref, sems) = refs[:-3], refs[-3:]
    rank, slots = kept_refs[0].shape
    share = last_ref.shape[0] // rank
    slots = slots // share
    low = functools.reduce(jnp.add, [ref[...].astype(F32) for ref in kept_refs]).astype(BF16).T
    deltas = []
    for k in range(share):
        up = last_ref[k * rank : (k + 1) * rank]
        deltas.append(jnp.dot(low[k * slots : (k + 1) * slots], up, preferred_element_type=F32).astype(BF16))
    delta = deltas[0] if share == 1 else jnp.concatenate(deltas, axis=0)
    count, rows, _ = half_ref.shape
    copies = []
    for n in range(count):
        part = slice(n * rows, (n + 1) * rows)
        result = most_ref[part] + jnp.dot(pick_ref[part], delta, preferred_element_type=F32)
        half_ref[n] = result.astype(BF16)
        copies.append(pltpu.make_async_copy(half_ref.at[n], out_ref.at[pl.ds(n * rows, rows)], sems.at[n]))
        copies[-1].start()
    for copy in copies:
        copy.wait()


def final(kept, pick, last, rest):
    return pl.pallas_call(
        final_kernel,
        in_specs=[VMEM] * (3 + len(kept)),
        out_specs=pl.BlockSpec(memory_space=pl.ANY),
        out_shape=jax.ShapeDtypeStruct(rest.shape, BF16),
        scratch_shapes=[pltpu.VMEM((2, rest.shape[0] // 2, rest.shape[1]), BF16), pltpu.SemaphoreType.DMA((2,))],
        compiler_params=params(32),
        cost_estimate=COST,
        name="final",
    )(pick, last, rest, *kept)


def local(tokens, adapter_ids, base_weight, channel_scale, adapter_down, adapter_up, sign_bits):
    planes, groups, parts = lax.axis_size("adp"), lax.axis_size("grp"), lax.axis_size("tp")
    features = tokens.shape[1]
    here, _, rank = adapter_down.shape
    width = adapter_up.shape[2]
    share = here // groups
    matrix = hadamard(sign_bits.shape[0])
    bits, scale, ids = sign_bits[None, :], channel_scale[None, :], adapter_ids.T
    down = jnp.swapaxes(adapter_down, 1, 2)

    own = lax.dynamic_slice_in_dim(down, lax.axis_index("grp") * share, share, 0)
    near = swap(own, "adp", 1)
    mine = [(0, own)]
    bit = planes // 2
    while bit > 1:
        mine += [(plane | bit, swap(piece, "adp", bit)) for plane, piece in mine]
        bit //= 2
    half = parts // 2
    offsets = (*range(1, parts, 2), *range(2, parts, 2))
    blocks = list(partials(tokens, base_weight, parts, offsets, lasting(4)))
    near, blocks[-1] = together(near, blocks[-1])
    (block,) = partials(tokens, base_weight, parts, (0,), COST, blocks[-1])
    slots = -(-2 * tokens.shape[0] // (here * planes) // 128) * 128
    lasts = [(planes - 1, groups - 1, k) for k in range(share)]
    pick, chosen = picked(ids, tokens, here, share, lasts, slots)
    close, block, pick, chosen, *far = together(near, block, pick, chosen, *(piece for _, piece in mine[1:]))
    blocks = blocks[:half] + [block] + blocks[half:]
    mine = mine[:1] + [(plane, piece) for (plane, _), piece in zip(mine[1:], far)]
    odd = [(1, near)] + [(plane | 1, swap(piece, "adp", 1)) for plane, piece in mine[1:]]

    def others(pieces):
        return [(plane, off, swap(piece, "grp", off)) for plane, piece in pieces for off in range(1, groups)]

    swapped = others(odd[:1]) + others(mine[1:]) + others(odd[1:])
    held = [(plane, 0, piece) for plane, piece in [(1, close)] + mine[1:] + odd[1:]]

    def terms(pieces, start):
        return [(start + i, k, 0, (plane, off, k)) for i, (plane, off, _) in enumerate(pieces) for k in range(share)]

    def more(low, pieces, dtype, cost=COST):
        arrays, every = [p for *_, p in pieces], terms(pieces, 0)
        if low is None:
            every += [(len(arrays), k, 0, ("plane", 0, k)) for k in range(here)]
            arrays = arrays + [down]
        return low_rows(ids, tokens, here, share, [((0, features), every)], arrays, low, dtype, cost)

    low = more(None, held[: len(mine)] + swapped[:1], F32, lasting(2))
    low, ups, *came = together(low, adapter_up, *(swap(block, "tp", 1) for block in blocks[:half]))

    def both(low):
        bit = 1
        while bit < parts // 2:
            low = add(low, swap(low, "tp", bit))
            bit *= 2
        return low, swap(low, "tp", bit)

    rest = held[len(mine) :]
    order = [0]
    bit = planes // 2
    while bit > 1:
        (plane, off, piece), other = rest[0], swap(ups, "adp", bit)
        piece, other = together(piece, other)
        rest[0], ups = (plane, off, piece), joined(ups, other)
        order += [plane | bit for plane in order]
        bit //= 2
    low = more(low, swapped[1:-1] + rest, BF16, lasting(5))
    more_ups = swap(ups, "adp", 1)
    low, other = both(low)

    sums = [[block, pair] for block, pair in zip(blocks[half:], came)]
    bit = 2
    while bit < parts:
        came = [swap(add(*terms), "tp", bit) for terms in sums[1::2]]
        sums = [terms + [pair] for terms, pair in zip(sums[0::2], came)]
        bit *= 2

    named = [("plane", plane | side, k) for side in (0, 1) for plane in order for k in range(here)]
    piece = swapped[-1][2]
    kept = compact(chosen, piece)
    kept = [kept] + [swap(kept, "tp", offset) for offset in range(1, parts)]
    up, mask = rotated_ups(ids, bits, matrix, here, share, named, ups, more_ups)
    last, rest = most(low, other, up, mask, scale, bits, matrix, sums[0], here, share, [named.index(("plane", planes - 1, k)) for k in range(share)])
    return final(kept, pick, last, rest)


def solution(mesh):
    return jax.shard_map(
        local,
        mesh=mesh,
        in_specs=(
            P(("grp", "adp"), "tp"),
            P(("grp", "adp"), None),
            P("tp", None),
            P("tp"),
            P("adp", "tp", None),
            P("adp", None, "tp"),
            P(),
        ),
        out_specs=P(("grp", "adp"), "tp"),
        check_vma=False,
    )
```

```python
import functools

import jax
import jax.numpy as jnp
import numpy as np
from jax import lax
from jax.experimental import pallas as pl
from jax.experimental.pallas import tpu as pltpu
from jax.sharding import PartitionSpec as P

VMEM = pl.BlockSpec(memory_space=pltpu.VMEM)
SMEM = pl.BlockSpec(memory_space=pltpu.SMEM)
F32, BF16 = jnp.float32, jnp.bfloat16
LAST = (((1,), (1,)), ((), ()))
FIRST = (((0,), (0,)), ((), ()))


def params(mib):
    return pltpu.CompilerParams(vmem_limit_bytes=mib << 20)


COST = pl.CostEstimate(flops=1, bytes_accessed=1, transcendentals=0)


def lasting(microseconds):
    return pl.CostEstimate(flops=int(microseconds * 1e9), bytes_accessed=1, transcendentals=0)


def hadamard(size):
    index = np.arange(size)
    shared = index[:, None] & index[None, :]
    parity = np.zeros_like(shared)
    while shared.any():
        parity, shared = parity ^ (shared & 1), shared >> 1
    return jnp.asarray(1 - 2 * parity, BF16)


def swap(x, axis, bit):
    return lax.ppermute(x, axis, [(i, i ^ bit) for i in range(lax.axis_size(axis))])


def together(*values):
    return lax.optimization_barrier(values)


def rotate(value, signs, matrix):
    head = matrix.shape[0]
    scale = signs * (1.0 / np.sqrt(head))
    turned = []
    for at in range(0, value.shape[1], head):
        signed = value[:, at : at + head] * scale
        high = signed.astype(BF16)
        rest = (signed - high.astype(F32)).astype(BF16)
        turned.append(
            jnp.dot(high, matrix, preferred_element_type=F32) + jnp.dot(rest, matrix, preferred_element_type=F32)
        )
    return turned


def partial_kernel(offsets, parts, tokens_ref, weight_ref, *refs):
    me, width = lax.axis_index("tp"), weight_ref.shape[1] // parts
    for offset, out_ref in zip(offsets, refs[-len(offsets) :]):
        at = pl.multiple_of(jnp.bitwise_xor(me, offset) * width, width)
        product = jnp.dot(tokens_ref[...], weight_ref[:, pl.ds(at, width)], preferred_element_type=F32)
        out_ref[...] = product.astype(BF16)


def partials(tokens, weight, parts, offsets, cost, *before):
    block = jax.ShapeDtypeStruct((tokens.shape[0], weight.shape[1] // parts), BF16)
    return pl.pallas_call(
        functools.partial(partial_kernel, offsets, parts),
        in_specs=[VMEM] * (2 + len(before)),
        out_specs=[VMEM] * len(offsets),
        out_shape=[block] * len(offsets),
        compiler_params=params(24),
        cost_estimate=cost,
        name="partials",
    )(tokens, weight, *before)


def add_kernel(*refs):
    total = refs[0][...].astype(F32)
    for ref in refs[1:-1]:
        total = total + ref[...].astype(F32)
    refs[-1][...] = total.astype(BF16)


def add(*terms):
    return pl.pallas_call(
        add_kernel,
        in_specs=[VMEM] * len(terms),
        out_specs=VMEM,
        out_shape=jax.ShapeDtypeStruct(terms[0].shape, BF16),
        compiler_params=params(16),
        cost_estimate=COST,
        name="add",
    )(*terms)


def adapter(here, share, name):
    z = lax.axis_index("adp")
    if name[0] == "plane":
        return jnp.bitwise_xor(z, name[1]) * here + name[2]
    plane, off, k = name
    return jnp.bitwise_xor(z, plane) * here + jnp.bitwise_xor(lax.axis_index("grp"), off) * share + k


def low_kernel(groups, here, share, rank, more, ids_ref, tokens_ref, *refs):
    out_ref = refs[-1]
    total = refs[-2][...] if more else None
    for (start, stop), terms in groups:
        rows = [refs[i][k, :, cut : cut + stop - start] for i, k, cut, _ in terms]
        joined = rows[0] if len(rows) == 1 else jnp.concatenate(rows, axis=0)
        product = lax.dot_general(joined, tokens_ref[:, start:stop], LAST, preferred_element_type=F32)
        for n, (_, _, _, name) in enumerate(terms):
            mine = ids_ref[...] == adapter(here, share, name)
            term = jnp.where(mine, product[n * rank : (n + 1) * rank], 0.0)
            total = term if total is None else total + term
    out_ref[...] = total.astype(out_ref.dtype)


def low_rows(ids, tokens, here, share, groups, arrays, before, dtype, cost=COST):
    rank = arrays[0].shape[1]
    more = [] if before is None else [before]
    return pl.pallas_call(
        functools.partial(low_kernel, groups, here, share, rank, bool(more)),
        in_specs=[VMEM] * (2 + len(arrays) + len(more)),
        out_specs=VMEM,
        out_shape=jax.ShapeDtypeStruct((rank, tokens.shape[0]), dtype),
        compiler_params=params(24),
        cost_estimate=cost,
        name="low_rows",
    )(ids, tokens, *arrays, *more)


def copy_kernel(in_ref, out_ref):
    out_ref[...] = in_ref[...]


def copied(value):
    return pl.pallas_call(
        copy_kernel,
        in_specs=[VMEM],
        out_specs=VMEM,
        out_shape=jax.ShapeDtypeStruct(value.shape, value.dtype),
        compiler_params=params(16),
        cost_estimate=COST,
        name="copied",
    )(value)


def join_kernel(first_ref, second_ref, out_ref):
    out_ref[: first_ref.shape[0]] = first_ref[...]
    out_ref[first_ref.shape[0] :] = second_ref[...]


def joined(first, second):
    return pl.pallas_call(
        join_kernel,
        in_specs=[VMEM] * 2,
        out_specs=VMEM,
        out_shape=jax.ShapeDtypeStruct((2 * first.shape[0], *first.shape[1:]), BF16),
        compiler_params=params(16),
        cost_estimate=COST,
        name="joined",
    )(first, second)


def ups_kernel(here, share, named, ids_ref, bits_ref, matrix_ref, first_ref, second_ref, up_ref, mask_ref):
    half, rank, _ = first_ref.shape
    signs = (1 - 2 * bits_ref[...]).astype(F32)
    ids = jnp.broadcast_to(ids_ref[...], (rank, ids_ref.shape[1])).T
    for n, name in enumerate(named):
        turned = rotate((first_ref if n < half else second_ref)[n % half].astype(F32), signs, matrix_ref[...])
        up_ref[n * rank : (n + 1) * rank, :] = jnp.concatenate(turned, axis=1).astype(BF16)
        mine = ids == adapter(here, share, name)
        mask_ref[:, n * rank : (n + 1) * rank] = jnp.where(mine, 1.0, 0.0).astype(BF16)


def rotated_ups(ids, bits, matrix, here, share, named, first, second):
    _, rank, width = first.shape
    return pl.pallas_call(
        functools.partial(ups_kernel, here, share, named),
        in_specs=[VMEM] * 5,
        out_specs=[VMEM, VMEM],
        out_shape=[
            jax.ShapeDtypeStruct((len(named) * rank, width), BF16),
            jax.ShapeDtypeStruct((ids.shape[1], len(named) * rank), BF16),
        ],
        compiler_params=params(32),
        cost_estimate=COST,
        name="rotated_ups",
    )(ids, bits, matrix, first, second)


def pick_kernel(named, here, share, ids_ref, tokens_ref, pick_ref, chosen_ref):
    rows, slots = pick_ref.shape[0], pick_ref.shape[1] // len(named)
    earlier = lax.broadcasted_iota(jnp.int32, (rows, rows), 0) < lax.broadcasted_iota(jnp.int32, (rows, rows), 1)
    earlier = jnp.where(earlier, 1.0, 0.0).astype(BF16)
    ids = jnp.broadcast_to(ids_ref[...], (8, rows))
    for k, name in enumerate(named):
        mine = ids == adapter(here, share, name)
        rank = jnp.dot(jnp.where(mine, 1.0, 0.0).astype(BF16), earlier, preferred_element_type=F32)
        rank = jnp.where(mine, rank, -1.0)
        rank = jnp.broadcast_to(rank[:1], (128, rows)).T
        for at in range(0, slots, 128):
            slot = (lax.broadcasted_iota(jnp.int32, (rows, 128), 1) + at).astype(F32)
            pick_ref[:, k * slots + at : k * slots + at + 128] = jnp.where(rank == slot, 1.0, 0.0).astype(BF16)
    rows = lax.dot_general(pick_ref[...], tokens_ref[...], FIRST, preferred_element_type=F32)
    chosen_ref[...] = rows.astype(BF16)


def picked(ids, tokens, here, share, named, slots):
    rows, features = tokens.shape
    columns = len(named) * slots
    return pl.pallas_call(
        functools.partial(pick_kernel, named, here, share),
        in_specs=[VMEM] * 2,
        out_specs=[VMEM] * 2,
        out_shape=[jax.ShapeDtypeStruct((rows, columns), BF16), jax.ShapeDtypeStruct((columns, features), BF16)],
        compiler_params=params(24),
        cost_estimate=COST,
        name="picked",
    )(ids, tokens)


def compact_kernel(chosen_ref, piece_ref, out_ref):
    share, features = piece_ref.shape[0], chosen_ref.shape[1]
    slots = chosen_ref.shape[0] // share
    for k in range(share):
        mine = slice(k * slots, (k + 1) * slots)
        product = lax.dot_general(
            piece_ref[k, :, :features], chosen_ref[mine], LAST, preferred_element_type=F32
        )
        out_ref[:, mine] = product.astype(BF16)


def compact(chosen, piece):
    return pl.pallas_call(
        compact_kernel,
        in_specs=[VMEM] * 2,
        out_specs=VMEM,
        out_shape=jax.ShapeDtypeStruct((piece.shape[1], chosen.shape[0]), BF16),
        compiler_params=params(24),
        cost_estimate=lasting(2),
        name="compact",
    )(chosen, piece)


def most_kernel(share, spots, mine_ref, theirs_ref, up_ref, mask_ref, scale_ref, bits_ref, matrix_ref, *refs):
    terms, (last_ref, out_ref) = refs[:-2], refs[-2:]
    low = (mine_ref[...].astype(F32) + theirs_ref[...].astype(F32)).astype(BF16).T
    rank, columns = low.shape[1], mask_ref.shape[1]
    signs = (1 - 2 * bits_ref[...]).astype(F32)
    spread = jnp.concatenate([low] * (columns // rank), axis=1) * mask_ref[...]
    delta = jnp.dot(spread, up_ref[...], preferred_element_type=F32)
    value = functools.reduce(jnp.add, [ref[...].astype(F32) for ref in terms]) * scale_ref[...]
    out_ref[...] = jnp.concatenate(rotate(value, signs, matrix_ref[...]), axis=1) + delta
    off = jnp.bitwise_xor(lax.axis_index("grp"), lax.axis_size("grp") - 1) * share
    for k, spot in enumerate(spots):
        at = pl.multiple_of((spot + off) * rank, rank)
        last_ref[k * rank : (k + 1) * rank] = up_ref[pl.ds(at, rank)]


def most(mine, theirs, up, mask, scale, bits, matrix, terms, here, share, spots):
    width = up.shape[1]
    return pl.pallas_call(
        functools.partial(most_kernel, share, spots),
        in_specs=[VMEM] * (7 + len(terms)),
        out_specs=[VMEM] * 2,
        out_shape=[
            jax.ShapeDtypeStruct((share * mine.shape[0], width), BF16),
            jax.ShapeDtypeStruct(terms[0].shape, F32),
        ],
        compiler_params=params(32),
        cost_estimate=COST,
        name="most",
    )(mine, theirs, up, mask, scale, bits, matrix, *terms)


def final_kernel(pick_ref, last_ref, most_ref, *refs):
    kept_refs, (out_ref, half_ref, sems) = refs[:-3], refs[-3:]
    rank, slots = kept_refs[0].shape
    share = last_ref.shape[0] // rank
    slots = slots // share
    low = functools.reduce(jnp.add, [ref[...].astype(F32) for ref in kept_refs]).astype(BF16).T
    deltas = []
    for k in range(share):
        up = last_ref[k * rank : (k + 1) * rank]
        deltas.append(jnp.dot(low[k * slots : (k + 1) * slots], up, preferred_element_type=F32).astype(BF16))
    delta = deltas[0] if share == 1 else jnp.concatenate(deltas, axis=0)
    count, rows, _ = half_ref.shape
    copies = []
    for n in range(count):
        part = slice(n * rows, (n + 1) * rows)
        result = most_ref[part] + jnp.dot(pick_ref[part], delta, preferred_element_type=F32)
        half_ref[n] = result.astype(BF16)
        copies.append(pltpu.make_async_copy(half_ref.at[n], out_ref.at[pl.ds(n * rows, rows)], sems.at[n]))
        copies[-1].start()
    for copy in copies:
        copy.wait()


def final(kept, pick, last, rest):
    return pl.pallas_call(
        final_kernel,
        in_specs=[VMEM] * (3 + len(kept)),
        out_specs=pl.BlockSpec(memory_space=pl.ANY),
        out_shape=jax.ShapeDtypeStruct(rest.shape, BF16),
        scratch_shapes=[pltpu.VMEM((2, rest.shape[0] // 2, rest.shape[1]), BF16), pltpu.SemaphoreType.DMA((2,))],
        compiler_params=params(32),
        cost_estimate=COST,
        name="final",
    )(pick, last, rest, *kept)


def local(tokens, adapter_ids, base_weight, channel_scale, adapter_down, adapter_up, sign_bits):
    planes, groups, parts = lax.axis_size("adp"), lax.axis_size("grp"), lax.axis_size("tp")
    features = tokens.shape[1]
    here, _, rank = adapter_down.shape
    width = adapter_up.shape[2]
    share = here // groups
    matrix = hadamard(sign_bits.shape[0])
    bits, scale, ids = sign_bits[None, :], channel_scale[None, :], adapter_ids.T
    down = jnp.swapaxes(adapter_down, 1, 2)

    own = lax.dynamic_slice_in_dim(down, lax.axis_index("grp") * share, share, 0)
    near = swap(own, "adp", 1)
    mine = [(0, copied(own))]
    bit = planes // 2
    while bit > 1:
        mine += [(plane | bit, swap(piece, "adp", bit)) for plane, piece in mine]
        bit //= 2
    half = parts // 2
    offsets = (*range(1, parts, 2), *range(2, parts, 2))
    blocks = list(partials(tokens, base_weight, parts, offsets, lasting(4)))
    near, blocks[-1] = together(near, blocks[-1])
    (block,) = partials(tokens, base_weight, parts, (0,), COST, blocks[-1])
    slots = -(-2 * tokens.shape[0] // (here * planes) // 128) * 128
    lasts = [(planes - 1, groups - 1, k) for k in range(share)]
    pick, chosen = picked(ids, tokens, here, share, lasts, slots)
    close, block, pick, chosen, *far = together(near, block, pick, chosen, *(piece for _, piece in mine[1:]))
    blocks = blocks[:half] + [block] + blocks[half:]
    mine = mine[:1] + [(plane, piece) for (plane, _), piece in zip(mine[1:], far)]
    odd = [(1, near)] + [(plane | 1, swap(piece, "adp", 1)) for plane, piece in mine[1:]]

    def others(pieces):
        return [(plane, off, swap(piece, "grp", off)) for plane, piece in pieces for off in range(1, groups)]

    swapped = others(odd[:1]) + others(mine[1:]) + others(odd[1:])
    held = [(plane, 0, piece) for plane, piece in [(1, close)] + mine[1:] + odd[1:]]

    def terms(pieces, start):
        return [(start + i, k, 0, (plane, off, k)) for i, (plane, off, _) in enumerate(pieces) for k in range(share)]

    def more(low, pieces, dtype, cost=COST):
        arrays, every = [p for *_, p in pieces], terms(pieces, 0)
        if low is None:
            every += [(len(arrays), k, 0, ("plane", 0, k)) for k in range(here)]
            arrays = arrays + [down]
        return low_rows(ids, tokens, here, share, [((0, features), every)], arrays, low, dtype, cost)

    low = more(None, held[: len(mine)] + swapped[:1], F32, lasting(2))
    low, ups, *came = together(low, adapter_up, *(swap(block, "tp", 1) for block in blocks[:half]))

    def both(low):
        bit = 1
        while bit < parts // 2:
            low = add(low, swap(low, "tp", bit))
            bit *= 2
        return low, swap(low, "tp", bit)

    rest = held[len(mine) :]
    order = [0]
    bit = planes // 2
    while bit > 1:
        (plane, off, piece), other = rest[0], swap(ups, "adp", bit)
        piece, other = together(piece, other)
        rest[0], ups = (plane, off, piece), joined(ups, other)
        order += [plane | bit for plane in order]
        bit //= 2
    low = more(low, swapped[1:-1] + rest, BF16, lasting(5))
    more_ups = swap(ups, "adp", 1)
    low, other = both(low)

    sums = [[block, pair] for block, pair in zip(blocks[half:], came)]
    bit = 2
    while bit < parts:
        came = [swap(add(*terms), "tp", bit) for terms in sums[1::2]]
        sums = [terms + [pair] for terms, pair in zip(sums[0::2], came)]
        bit *= 2

    named = [("plane", plane | side, k) for side in (0, 1) for plane in order for k in range(here)]
    piece = swapped[-1][2]
    kept = compact(chosen, piece)
    kept = [kept] + [swap(kept, "tp", offset) for offset in range(1, parts)]
    up, mask = rotated_ups(ids, bits, matrix, here, share, named, ups, more_ups)
    last, rest = most(low, other, up, mask, scale, bits, matrix, sums[0], here, share, [named.index(("plane", planes - 1, k)) for k in range(share)])
    return final(kept, pick, last, rest)


def solution(mesh):
    return jax.shard_map(
        local,
        mesh=mesh,
        in_specs=(
            P(("grp", "adp"), "tp"),
            P(("grp", "adp"), None),
            P("tp", None),
            P("tp"),
            P("adp", "tp", None),
            P("adp", None, "tp"),
            P(),
        ),
        out_specs=P(("grp", "adp"), "tp"),
        check_vma=False,
    )
```

```python
import functools

import jax
import jax.numpy as jnp
import numpy as np
from jax import lax
from jax.experimental import pallas as pl
from jax.experimental.pallas import tpu as pltpu
from jax.sharding import PartitionSpec as P

VMEM = pl.BlockSpec(memory_space=pltpu.VMEM)
SMEM = pl.BlockSpec(memory_space=pltpu.SMEM)
F32, BF16 = jnp.float32, jnp.bfloat16
LAST = (((1,), (1,)), ((), ()))
FIRST = (((0,), (0,)), ((), ()))


def params(mib):
    return pltpu.CompilerParams(vmem_limit_bytes=mib << 20)


COST = pl.CostEstimate(flops=1, bytes_accessed=1, transcendentals=0)


def lasting(microseconds):
    return pl.CostEstimate(flops=int(microseconds * 1e9), bytes_accessed=1, transcendentals=0)


def hadamard(size):
    index = np.arange(size)
    shared = index[:, None] & index[None, :]
    parity = np.zeros_like(shared)
    while shared.any():
        parity, shared = parity ^ (shared & 1), shared >> 1
    return jnp.asarray(1 - 2 * parity, BF16)


def swap(x, axis, bit):
    return lax.ppermute(x, axis, [(i, i ^ bit) for i in range(lax.axis_size(axis))])


def together(*values):
    return lax.optimization_barrier(values)


def rotate(value, signs, matrix):
    head = matrix.shape[0]
    scale = signs * (1.0 / np.sqrt(head))
    turned = []
    for at in range(0, value.shape[1], head):
        signed = value[:, at : at + head] * scale
        high = signed.astype(BF16)
        rest = (signed - high.astype(F32)).astype(BF16)
        turned.append(
            jnp.dot(high, matrix, preferred_element_type=F32) + jnp.dot(rest, matrix, preferred_element_type=F32)
        )
    return turned


def partial_kernel(offsets, parts, tokens_ref, weight_ref, *refs):
    me, width = lax.axis_index("tp"), weight_ref.shape[1] // parts
    for offset, out_ref in zip(offsets, refs[-len(offsets) :]):
        at = pl.multiple_of(jnp.bitwise_xor(me, offset) * width, width)
        product = jnp.dot(tokens_ref[...], weight_ref[:, pl.ds(at, width)], preferred_element_type=F32)
        out_ref[...] = product.astype(BF16)


def partials(tokens, weight, parts, offsets, cost, *before):
    block = jax.ShapeDtypeStruct((tokens.shape[0], weight.shape[1] // parts), BF16)
    return pl.pallas_call(
        functools.partial(partial_kernel, offsets, parts),
        in_specs=[VMEM] * (2 + len(before)),
        out_specs=[VMEM] * len(offsets),
        out_shape=[block] * len(offsets),
        compiler_params=params(24),
        cost_estimate=cost,
        name="partials",
    )(tokens, weight, *before)


def add_kernel(*refs):
    total = refs[0][...].astype(F32)
    for ref in refs[1:-1]:
        total = total + ref[...].astype(F32)
    refs[-1][...] = total.astype(BF16)


def add(*terms):
    return pl.pallas_call(
        add_kernel,
        in_specs=[VMEM] * len(terms),
        out_specs=VMEM,
        out_shape=jax.ShapeDtypeStruct(terms[0].shape, BF16),
        compiler_params=params(16),
        cost_estimate=COST,
        name="add",
    )(*terms)


def adapter(here, share, name):
    z = lax.axis_index("adp")
    if name[0] == "plane":
        return jnp.bitwise_xor(z, name[1]) * here + name[2]
    plane, off, k = name
    return jnp.bitwise_xor(z, plane) * here + jnp.bitwise_xor(lax.axis_index("grp"), off) * share + k


def low_kernel(groups, here, share, rank, more, ids_ref, tokens_ref, *refs):
    out_ref = refs[-1]
    total = refs[-2][...] if more else None
    for (start, stop), terms in groups:
        rows = [refs[i][k, :, cut : cut + stop - start] for i, k, cut, _ in terms]
        joined = rows[0] if len(rows) == 1 else jnp.concatenate(rows, axis=0)
        product = lax.dot_general(joined, tokens_ref[:, start:stop], LAST, preferred_element_type=F32)
        for n, (_, _, _, name) in enumerate(terms):
            mine = ids_ref[...] == adapter(here, share, name)
            term = jnp.where(mine, product[n * rank : (n + 1) * rank], 0.0)
            total = term if total is None else total + term
    out_ref[...] = total.astype(out_ref.dtype)


def low_rows(ids, tokens, here, share, groups, arrays, before, dtype, cost=COST):
    rank = arrays[0].shape[1]
    more = [] if before is None else [before]
    return pl.pallas_call(
        functools.partial(low_kernel, groups, here, share, rank, bool(more)),
        in_specs=[VMEM] * (2 + len(arrays) + len(more)),
        out_specs=VMEM,
        out_shape=jax.ShapeDtypeStruct((rank, tokens.shape[0]), dtype),
        compiler_params=params(24),
        cost_estimate=cost,
        name="low_rows",
    )(ids, tokens, *arrays, *more)


def copy_kernel(in_ref, out_ref):
    out_ref[...] = in_ref[...]


def copied(value):
    return pl.pallas_call(
        copy_kernel,
        in_specs=[VMEM],
        out_specs=VMEM,
        out_shape=jax.ShapeDtypeStruct(value.shape, value.dtype),
        compiler_params=params(16),
        cost_estimate=COST,
        name="copied",
    )(value)


def join_kernel(first_ref, second_ref, out_ref):
    out_ref[: first_ref.shape[0]] = first_ref[...]
    out_ref[first_ref.shape[0] :] = second_ref[...]


def joined(first, second):
    return pl.pallas_call(
        join_kernel,
        in_specs=[VMEM] * 2,
        out_specs=VMEM,
        out_shape=jax.ShapeDtypeStruct((2 * first.shape[0], *first.shape[1:]), BF16),
        compiler_params=params(16),
        cost_estimate=COST,
        name="joined",
    )(first, second)


def ups_kernel(here, share, named, ids_ref, bits_ref, matrix_ref, first_ref, second_ref, up_ref, mask_ref):
    half, rank, _ = first_ref.shape
    signs = (1 - 2 * bits_ref[...]).astype(F32)
    ids = jnp.broadcast_to(ids_ref[...], (rank, ids_ref.shape[1])).T
    for n, name in enumerate(named):
        turned = rotate((first_ref if n < half else second_ref)[n % half].astype(F32), signs, matrix_ref[...])
        up_ref[n * rank : (n + 1) * rank, :] = jnp.concatenate(turned, axis=1).astype(BF16)
        mine = ids == adapter(here, share, name)
        mask_ref[:, n * rank : (n + 1) * rank] = jnp.where(mine, 1.0, 0.0).astype(BF16)


def rotated_ups(ids, bits, matrix, here, share, named, first, second):
    _, rank, width = first.shape
    return pl.pallas_call(
        functools.partial(ups_kernel, here, share, named),
        in_specs=[VMEM] * 5,
        out_specs=[VMEM, VMEM],
        out_shape=[
            jax.ShapeDtypeStruct((len(named) * rank, width), BF16),
            jax.ShapeDtypeStruct((ids.shape[1], len(named) * rank), BF16),
        ],
        compiler_params=params(32),
        cost_estimate=COST,
        name="rotated_ups",
    )(ids, bits, matrix, first, second)


def pick_kernel(named, here, share, ids_ref, tokens_ref, pick_ref, chosen_ref):
    rows, slots = pick_ref.shape[0], pick_ref.shape[1] // len(named)
    earlier = lax.broadcasted_iota(jnp.int32, (rows, rows), 0) < lax.broadcasted_iota(jnp.int32, (rows, rows), 1)
    earlier = jnp.where(earlier, 1.0, 0.0).astype(BF16)
    ids = jnp.broadcast_to(ids_ref[...], (8, rows))
    for k, name in enumerate(named):
        mine = ids == adapter(here, share, name)
        rank = jnp.dot(jnp.where(mine, 1.0, 0.0).astype(BF16), earlier, preferred_element_type=F32)
        rank = jnp.where(mine, rank, -1.0)
        rank = jnp.broadcast_to(rank[:1], (128, rows)).T
        for at in range(0, slots, 128):
            slot = (lax.broadcasted_iota(jnp.int32, (rows, 128), 1) + at).astype(F32)
            pick_ref[:, k * slots + at : k * slots + at + 128] = jnp.where(rank == slot, 1.0, 0.0).astype(BF16)
    rows = lax.dot_general(pick_ref[...], tokens_ref[...], FIRST, preferred_element_type=F32)
    chosen_ref[...] = rows.astype(BF16)


def picked(ids, tokens, here, share, named, slots):
    rows, features = tokens.shape
    columns = len(named) * slots
    return pl.pallas_call(
        functools.partial(pick_kernel, named, here, share),
        in_specs=[VMEM] * 2,
        out_specs=[VMEM] * 2,
        out_shape=[jax.ShapeDtypeStruct((rows, columns), BF16), jax.ShapeDtypeStruct((columns, features), BF16)],
        compiler_params=params(24),
        cost_estimate=COST,
        name="picked",
    )(ids, tokens)


def compact_kernel(chosen_ref, piece_ref, out_ref):
    share, features = piece_ref.shape[0], chosen_ref.shape[1]
    slots = chosen_ref.shape[0] // share
    for k in range(share):
        mine = slice(k * slots, (k + 1) * slots)
        product = lax.dot_general(
            piece_ref[k, :, :features], chosen_ref[mine], LAST, preferred_element_type=F32
        )
        out_ref[:, mine] = product.astype(BF16)


def compact(chosen, piece):
    return pl.pallas_call(
        compact_kernel,
        in_specs=[VMEM] * 2,
        out_specs=VMEM,
        out_shape=jax.ShapeDtypeStruct((piece.shape[1], chosen.shape[0]), BF16),
        compiler_params=params(24),
        cost_estimate=lasting(2),
        name="compact",
    )(chosen, piece)


def most_kernel(share, spots, mine_ref, theirs_ref, up_ref, mask_ref, scale_ref, bits_ref, matrix_ref, *refs):
    terms, (last_ref, out_ref) = refs[:-2], refs[-2:]
    low = (mine_ref[...].astype(F32) + theirs_ref[...].astype(F32)).astype(BF16).T
    rank, columns = low.shape[1], mask_ref.shape[1]
    signs = (1 - 2 * bits_ref[...]).astype(F32)
    spread = jnp.concatenate([low] * (columns // rank), axis=1) * mask_ref[...]
    delta = jnp.dot(spread, up_ref[...], preferred_element_type=F32)
    value = functools.reduce(jnp.add, [ref[...].astype(F32) for ref in terms]) * scale_ref[...]
    out_ref[...] = jnp.concatenate(rotate(value, signs, matrix_ref[...]), axis=1) + delta
    off = jnp.bitwise_xor(lax.axis_index("grp"), lax.axis_size("grp") - 1) * share
    for k, spot in enumerate(spots):
        at = pl.multiple_of((spot + off) * rank, rank)
        last_ref[k * rank : (k + 1) * rank] = up_ref[pl.ds(at, rank)]


def most(mine, theirs, up, mask, scale, bits, matrix, terms, here, share, spots):
    width = up.shape[1]
    return pl.pallas_call(
        functools.partial(most_kernel, share, spots),
        in_specs=[VMEM] * (7 + len(terms)),
        out_specs=[VMEM] * 2,
        out_shape=[
            jax.ShapeDtypeStruct((share * mine.shape[0], width), BF16),
            jax.ShapeDtypeStruct(terms[0].shape, F32),
        ],
        compiler_params=params(32),
        cost_estimate=COST,
        name="most",
    )(mine, theirs, up, mask, scale, bits, matrix, *terms)


def final_kernel(pick_ref, last_ref, most_ref, *refs):
    kept_refs, (out_ref, half_ref, sems) = refs[:-3], refs[-3:]
    rank, slots = kept_refs[0].shape
    share = last_ref.shape[0] // rank
    slots = slots // share
    low = functools.reduce(jnp.add, [ref[...].astype(F32) for ref in kept_refs]).astype(BF16).T
    deltas = []
    for k in range(share):
        up = last_ref[k * rank : (k + 1) * rank]
        deltas.append(jnp.dot(low[k * slots : (k + 1) * slots], up, preferred_element_type=F32).astype(BF16))
    delta = deltas[0] if share == 1 else jnp.concatenate(deltas, axis=0)
    count, rows, _ = half_ref.shape
    copies = []
    for n in range(count):
        part = slice(n * rows, (n + 1) * rows)
        result = most_ref[part] + jnp.dot(pick_ref[part], delta, preferred_element_type=F32)
        half_ref[n] = result.astype(BF16)
        copies.append(pltpu.make_async_copy(half_ref.at[n], out_ref.at[pl.ds(n * rows, rows)], sems.at[n]))
        copies[-1].start()
    for copy in copies:
        copy.wait()


def final(kept, pick, last, rest):
    return pl.pallas_call(
        final_kernel,
        in_specs=[VMEM] * (3 + len(kept)),
        out_specs=pl.BlockSpec(memory_space=pl.ANY),
        out_shape=jax.ShapeDtypeStruct(rest.shape, BF16),
        scratch_shapes=[pltpu.VMEM((2, rest.shape[0] // 2, rest.shape[1]), BF16), pltpu.SemaphoreType.DMA((2,))],
        compiler_params=params(32),
        cost_estimate=COST,
        name="final",
    )(pick, last, rest, *kept)


def local(tokens, adapter_ids, base_weight, channel_scale, adapter_down, adapter_up, sign_bits):
    planes, groups, parts = lax.axis_size("adp"), lax.axis_size("grp"), lax.axis_size("tp")
    features = tokens.shape[1]
    here, _, rank = adapter_down.shape
    width = adapter_up.shape[2]
    share = here // groups
    matrix = hadamard(sign_bits.shape[0])
    bits, scale, ids = sign_bits[None, :], channel_scale[None, :], adapter_ids.T
    down = jnp.swapaxes(adapter_down, 1, 2)

    own = lax.dynamic_slice_in_dim(down, lax.axis_index("grp") * share, share, 0)
    near = swap(own, "adp", 1)
    mine = [(0, copied(own))]
    bit = planes // 2
    while bit > 1:
        mine += [(plane | bit, swap(piece, "adp", bit)) for plane, piece in mine]
        bit //= 2
    half = parts // 2
    offsets = (*range(1, parts, 2), *range(0, parts, 2))
    blocks = list(partials(tokens, base_weight, parts, offsets, lasting(4)))
    slots = -(-2 * tokens.shape[0] // (here * planes) // 128) * 128
    lasts = [(planes - 1, groups - 1, k) for k in range(share)]
    pick, chosen = picked(ids, tokens, here, share, lasts, slots)
    near, blocks[-1], pick, chosen = together(near, blocks[-1], pick, chosen)
    close, *far = together(near, *(piece for _, piece in mine[1:]))
    mine = mine[:1] + [(plane, piece) for (plane, _), piece in zip(mine[1:], far)]
    odd = [(1, near)] + [(plane | 1, swap(piece, "adp", 1)) for plane, piece in mine[1:]]

    def others(pieces):
        return [(plane, off, swap(piece, "grp", off)) for plane, piece in pieces for off in range(1, groups)]

    swapped = others(odd[:1]) + others(mine[1:]) + others(odd[1:])
    held = [(plane, 0, piece) for plane, piece in [(1, close)] + mine[1:] + odd[1:]]

    def terms(pieces, start):
        return [(start + i, k, 0, (plane, off, k)) for i, (plane, off, _) in enumerate(pieces) for k in range(share)]

    def more(low, pieces, dtype, cost=COST):
        arrays, every = [p for *_, p in pieces], terms(pieces, 0)
        if low is None:
            every += [(len(arrays), k, 0, ("plane", 0, k)) for k in range(here)]
            arrays = arrays + [down]
        return low_rows(ids, tokens, here, share, [((0, features), every)], arrays, low, dtype, cost)

    low = more(None, held[: len(mine)] + swapped[:1], F32, lasting(2))
    low, ups, *came = together(low, adapter_up, *(swap(block, "tp", 1) for block in blocks[:half]))

    def both(low):
        bit = 1
        while bit < parts // 2:
            low = add(low, swap(low, "tp", bit))
            bit *= 2
        return low, swap(low, "tp", bit)

    rest = held[len(mine) :]
    order = [0]
    bit = planes // 2
    while bit > 1:
        (plane, off, piece), other = rest[0], swap(ups, "adp", bit)
        piece, other = together(piece, other)
        rest[0], ups = (plane, off, piece), joined(ups, other)
        order += [plane | bit for plane in order]
        bit //= 2
    low = more(low, swapped[1:-1] + rest, BF16, lasting(5))
    more_ups = swap(ups, "adp", 1)
    low, other = both(low)

    sums = [[block, pair] for block, pair in zip(blocks[half:], came)]
    bit = 2
    while bit < parts:
        came = [swap(add(*terms), "tp", bit) for terms in sums[1::2]]
        sums = [terms + [pair] for terms, pair in zip(sums[0::2], came)]
        bit *= 2

    named = [("plane", plane | side, k) for side in (0, 1) for plane in order for k in range(here)]
    piece = swapped[-1][2]
    kept = compact(chosen, piece)
    kept = [kept] + [swap(kept, "tp", offset) for offset in range(1, parts)]
    up, mask = rotated_ups(ids, bits, matrix, here, share, named, ups, more_ups)
    last, rest = most(low, other, up, mask, scale, bits, matrix, sums[0], here, share, [named.index(("plane", planes - 1, k)) for k in range(share)])
    return final(kept, pick, last, rest)


def solution(mesh):
    return jax.shard_map(
        local,
        mesh=mesh,
        in_specs=(
            P(("grp", "adp"), "tp"),
            P(("grp", "adp"), None),
            P("tp", None),
            P("tp"),
            P("adp", "tp", None),
            P("adp", None, "tp"),
            P(),
        ),
        out_specs=P(("grp", "adp"), "tp"),
        check_vma=False,
    )
```

```python
import functools

import jax
import jax.numpy as jnp
import numpy as np
from jax import lax
from jax.experimental import pallas as pl
from jax.experimental.pallas import tpu as pltpu
from jax.sharding import PartitionSpec as P

VMEM = pl.BlockSpec(memory_space=pltpu.VMEM)
SMEM = pl.BlockSpec(memory_space=pltpu.SMEM)
F32, BF16 = jnp.float32, jnp.bfloat16
LAST = (((1,), (1,)), ((), ()))
FIRST = (((0,), (0,)), ((), ()))


def params(mib):
    return pltpu.CompilerParams(vmem_limit_bytes=mib << 20)


COST = pl.CostEstimate(flops=1, bytes_accessed=1, transcendentals=0)


def lasting(microseconds):
    return pl.CostEstimate(flops=int(microseconds * 1e9), bytes_accessed=1, transcendentals=0)


def hadamard(size):
    index = np.arange(size)
    shared = index[:, None] & index[None, :]
    parity = np.zeros_like(shared)
    while shared.any():
        parity, shared = parity ^ (shared & 1), shared >> 1
    return jnp.asarray(1 - 2 * parity, BF16)


def swap(x, axis, bit):
    return lax.ppermute(x, axis, [(i, i ^ bit) for i in range(lax.axis_size(axis))])


def together(*values):
    return lax.optimization_barrier(values)


def rotate(value, signs, matrix):
    head = matrix.shape[0]
    scale = signs * (1.0 / np.sqrt(head))
    turned = []
    for at in range(0, value.shape[1], head):
        signed = value[:, at : at + head] * scale
        high = signed.astype(BF16)
        rest = (signed - high.astype(F32)).astype(BF16)
        turned.append(
            jnp.dot(high, matrix, preferred_element_type=F32) + jnp.dot(rest, matrix, preferred_element_type=F32)
        )
    return turned


def partial_kernel(offsets, parts, tokens_ref, weight_ref, *refs):
    me, width = lax.axis_index("tp"), weight_ref.shape[1] // parts
    for offset, out_ref in zip(offsets, refs[-len(offsets) :]):
        at = pl.multiple_of(jnp.bitwise_xor(me, offset) * width, width)
        product = jnp.dot(tokens_ref[...], weight_ref[:, pl.ds(at, width)], preferred_element_type=F32)
        out_ref[...] = product.astype(BF16)


def partials(tokens, weight, parts, offsets, cost, *before):
    block = jax.ShapeDtypeStruct((tokens.shape[0], weight.shape[1] // parts), BF16)
    return pl.pallas_call(
        functools.partial(partial_kernel, offsets, parts),
        in_specs=[VMEM] * (2 + len(before)),
        out_specs=[VMEM] * len(offsets),
        out_shape=[block] * len(offsets),
        compiler_params=params(24),
        cost_estimate=cost,
        name="partials",
    )(tokens, weight, *before)


def add_kernel(*refs):
    total = refs[0][...].astype(F32)
    for ref in refs[1:-1]:
        total = total + ref[...].astype(F32)
    refs[-1][...] = total.astype(BF16)


def add(*terms):
    return pl.pallas_call(
        add_kernel,
        in_specs=[VMEM] * len(terms),
        out_specs=VMEM,
        out_shape=jax.ShapeDtypeStruct(terms[0].shape, BF16),
        compiler_params=params(16),
        cost_estimate=COST,
        name="add",
    )(*terms)


def adapter(here, share, name):
    z = lax.axis_index("adp")
    if name[0] == "plane":
        return jnp.bitwise_xor(z, name[1]) * here + name[2]
    plane, off, k = name
    return jnp.bitwise_xor(z, plane) * here + jnp.bitwise_xor(lax.axis_index("grp"), off) * share + k


def low_kernel(groups, here, share, rank, more, ids_ref, tokens_ref, *refs):
    out_ref = refs[-1]
    total = refs[-2][...] if more else None
    for (start, stop), terms in groups:
        rows = [refs[i][k, :, cut : cut + stop - start] for i, k, cut, _ in terms]
        joined = rows[0] if len(rows) == 1 else jnp.concatenate(rows, axis=0)
        product = lax.dot_general(joined, tokens_ref[:, start:stop], LAST, preferred_element_type=F32)
        for n, (_, _, _, name) in enumerate(terms):
            mine = ids_ref[...] == adapter(here, share, name)
            term = jnp.where(mine, product[n * rank : (n + 1) * rank], 0.0)
            total = term if total is None else total + term
    out_ref[...] = total.astype(out_ref.dtype)


def low_rows(ids, tokens, here, share, groups, arrays, before, dtype, cost=COST):
    rank = arrays[0].shape[1]
    more = [] if before is None else [before]
    return pl.pallas_call(
        functools.partial(low_kernel, groups, here, share, rank, bool(more)),
        in_specs=[VMEM] * (2 + len(arrays) + len(more)),
        out_specs=VMEM,
        out_shape=jax.ShapeDtypeStruct((rank, tokens.shape[0]), dtype),
        compiler_params=params(24),
        cost_estimate=cost,
        name="low_rows",
    )(ids, tokens, *arrays, *more)


def copy_kernel(in_ref, out_ref):
    out_ref[...] = in_ref[...]


def copied(value):
    return pl.pallas_call(
        copy_kernel,
        in_specs=[VMEM],
        out_specs=VMEM,
        out_shape=jax.ShapeDtypeStruct(value.shape, value.dtype),
        compiler_params=params(16),
        cost_estimate=COST,
        name="copied",
    )(value)


def join_kernel(first_ref, second_ref, out_ref):
    out_ref[: first_ref.shape[0]] = first_ref[...]
    out_ref[first_ref.shape[0] :] = second_ref[...]


def joined(first, second):
    return pl.pallas_call(
        join_kernel,
        in_specs=[VMEM] * 2,
        out_specs=VMEM,
        out_shape=jax.ShapeDtypeStruct((2 * first.shape[0], *first.shape[1:]), BF16),
        compiler_params=params(16),
        cost_estimate=COST,
        name="joined",
    )(first, second)


def ups_kernel(here, share, named, ids_ref, bits_ref, matrix_ref, first_ref, second_ref, up_ref, mask_ref):
    half, rank, _ = first_ref.shape
    signs = (1 - 2 * bits_ref[...]).astype(F32)
    ids = jnp.broadcast_to(ids_ref[...], (rank, ids_ref.shape[1])).T
    for n, name in enumerate(named):
        turned = rotate((first_ref if n < half else second_ref)[n % half].astype(F32), signs, matrix_ref[...])
        up_ref[n * rank : (n + 1) * rank, :] = jnp.concatenate(turned, axis=1).astype(BF16)
        mine = ids == adapter(here, share, name)
        mask_ref[:, n * rank : (n + 1) * rank] = jnp.where(mine, 1.0, 0.0).astype(BF16)


def rotated_ups(ids, bits, matrix, here, share, named, first, second):
    _, rank, width = first.shape
    return pl.pallas_call(
        functools.partial(ups_kernel, here, share, named),
        in_specs=[VMEM] * 5,
        out_specs=[VMEM, VMEM],
        out_shape=[
            jax.ShapeDtypeStruct((len(named) * rank, width), BF16),
            jax.ShapeDtypeStruct((ids.shape[1], len(named) * rank), BF16),
        ],
        compiler_params=params(32),
        cost_estimate=COST,
        name="rotated_ups",
    )(ids, bits, matrix, first, second)


def pick_kernel(named, here, share, ids_ref, tokens_ref, pick_ref, chosen_ref):
    rows, slots = pick_ref.shape[0], pick_ref.shape[1] // len(named)
    earlier = lax.broadcasted_iota(jnp.int32, (rows, rows), 0) < lax.broadcasted_iota(jnp.int32, (rows, rows), 1)
    earlier = jnp.where(earlier, 1.0, 0.0).astype(BF16)
    ids = jnp.broadcast_to(ids_ref[...], (8, rows))
    for k, name in enumerate(named):
        mine = ids == adapter(here, share, name)
        rank = jnp.dot(jnp.where(mine, 1.0, 0.0).astype(BF16), earlier, preferred_element_type=F32)
        rank = jnp.where(mine, rank, -1.0)
        rank = jnp.broadcast_to(rank[:1], (128, rows)).T
        for at in range(0, slots, 128):
            slot = (lax.broadcasted_iota(jnp.int32, (rows, 128), 1) + at).astype(F32)
            pick_ref[:, k * slots + at : k * slots + at + 128] = jnp.where(rank == slot, 1.0, 0.0).astype(BF16)
    rows = lax.dot_general(pick_ref[...], tokens_ref[...], FIRST, preferred_element_type=F32)
    chosen_ref[...] = rows.astype(BF16)


def picked(ids, tokens, here, share, named, slots):
    rows, features = tokens.shape
    columns = len(named) * slots
    return pl.pallas_call(
        functools.partial(pick_kernel, named, here, share),
        in_specs=[VMEM] * 2,
        out_specs=[VMEM] * 2,
        out_shape=[jax.ShapeDtypeStruct((rows, columns), BF16), jax.ShapeDtypeStruct((columns, features), BF16)],
        compiler_params=params(24),
        cost_estimate=COST,
        name="picked",
    )(ids, tokens)


def compact_kernel(chosen_ref, piece_ref, out_ref):
    share, features = piece_ref.shape[0], chosen_ref.shape[1]
    slots = chosen_ref.shape[0] // share
    for k in range(share):
        mine = slice(k * slots, (k + 1) * slots)
        product = lax.dot_general(
            piece_ref[k, :, :features], chosen_ref[mine], LAST, preferred_element_type=F32
        )
        out_ref[:, mine] = product.astype(BF16)


def compact(chosen, piece):
    return pl.pallas_call(
        compact_kernel,
        in_specs=[VMEM] * 2,
        out_specs=VMEM,
        out_shape=jax.ShapeDtypeStruct((piece.shape[1], chosen.shape[0]), BF16),
        compiler_params=params(24),
        cost_estimate=lasting(2),
        name="compact",
    )(chosen, piece)


def most_kernel(share, spots, mine_ref, theirs_ref, up_ref, mask_ref, scale_ref, bits_ref, matrix_ref, *refs):
    terms, (last_ref, out_ref) = refs[:-2], refs[-2:]
    low = (mine_ref[...].astype(F32) + theirs_ref[...].astype(F32)).astype(BF16).T
    rank, columns = low.shape[1], mask_ref.shape[1]
    signs = (1 - 2 * bits_ref[...]).astype(F32)
    spread = jnp.concatenate([low] * (columns // rank), axis=1) * mask_ref[...]
    delta = jnp.dot(spread, up_ref[...], preferred_element_type=F32)
    value = functools.reduce(jnp.add, [ref[...].astype(F32) for ref in terms]) * scale_ref[...]
    out_ref[...] = jnp.concatenate(rotate(value, signs, matrix_ref[...]), axis=1) + delta
    off = jnp.bitwise_xor(lax.axis_index("grp"), lax.axis_size("grp") - 1) * share
    for k, spot in enumerate(spots):
        at = pl.multiple_of((spot + off) * rank, rank)
        last_ref[k * rank : (k + 1) * rank] = up_ref[pl.ds(at, rank)]


def most(mine, theirs, up, mask, scale, bits, matrix, terms, here, share, spots):
    width = up.shape[1]
    return pl.pallas_call(
        functools.partial(most_kernel, share, spots),
        in_specs=[VMEM] * (7 + len(terms)),
        out_specs=[VMEM] * 2,
        out_shape=[
            jax.ShapeDtypeStruct((share * mine.shape[0], width), BF16),
            jax.ShapeDtypeStruct(terms[0].shape, F32),
        ],
        compiler_params=params(32),
        cost_estimate=COST,
        name="most",
    )(mine, theirs, up, mask, scale, bits, matrix, *terms)


def final_kernel(pick_ref, last_ref, most_ref, *refs):
    kept_refs, (out_ref, half_ref, sems) = refs[:-3], refs[-3:]
    rank, slots = kept_refs[0].shape
    share = last_ref.shape[0] // rank
    slots = slots // share
    low = functools.reduce(jnp.add, [ref[...].astype(F32) for ref in kept_refs]).astype(BF16).T
    deltas = []
    for k in range(share):
        up = last_ref[k * rank : (k + 1) * rank]
        deltas.append(jnp.dot(low[k * slots : (k + 1) * slots], up, preferred_element_type=F32).astype(BF16))
    delta = deltas[0] if share == 1 else jnp.concatenate(deltas, axis=0)
    count, rows, _ = half_ref.shape
    copies = []
    for n in range(count):
        part = slice(n * rows, (n + 1) * rows)
        result = most_ref[part] + jnp.dot(pick_ref[part], delta, preferred_element_type=F32)
        half_ref[n] = result.astype(BF16)
        copies.append(pltpu.make_async_copy(half_ref.at[n], out_ref.at[pl.ds(n * rows, rows)], sems.at[n]))
        copies[-1].start()
    for copy in copies:
        copy.wait()


def final(kept, pick, last, rest):
    return pl.pallas_call(
        final_kernel,
        in_specs=[VMEM] * (3 + len(kept)),
        out_specs=pl.BlockSpec(memory_space=pl.ANY),
        out_shape=jax.ShapeDtypeStruct(rest.shape, BF16),
        scratch_shapes=[pltpu.VMEM((2, rest.shape[0] // 2, rest.shape[1]), BF16), pltpu.SemaphoreType.DMA((2,))],
        compiler_params=params(32),
        cost_estimate=COST,
        name="final",
    )(pick, last, rest, *kept)


def local(tokens, adapter_ids, base_weight, channel_scale, adapter_down, adapter_up, sign_bits):
    planes, groups, parts = lax.axis_size("adp"), lax.axis_size("grp"), lax.axis_size("tp")
    features = tokens.shape[1]
    here, _, rank = adapter_down.shape
    width = adapter_up.shape[2]
    share = here // groups
    matrix = hadamard(sign_bits.shape[0])
    bits, scale, ids = sign_bits[None, :], channel_scale[None, :], adapter_ids.T
    down = jnp.swapaxes(adapter_down, 1, 2)

    own = lax.dynamic_slice_in_dim(down, lax.axis_index("grp") * share, share, 0)
    near = swap(own, "adp", 1)
    mine = [(0, copied(own))]
    bit = planes // 2
    while bit > 1:
        mine += [(plane | bit, swap(piece, "adp", bit)) for plane, piece in mine]
        bit //= 2
    half = parts // 2
    offsets = (*range(1, parts, 2), *range(0, parts, 2))
    blocks = list(partials(tokens, base_weight, parts, offsets, lasting(4)))
    slots = -(-2 * tokens.shape[0] // (here * planes) // 128) * 128
    lasts = [(planes - 1, groups - 1, k) for k in range(share)]
    pick, chosen = picked(ids, tokens, here, share, lasts, slots)
    near, blocks[-1], pick, chosen = together(near, blocks[-1], pick, chosen)
    close, *far = together(near, *(piece for _, piece in mine[1:]))
    mine = mine[:1] + [(plane, piece) for (plane, _), piece in zip(mine[1:], far)]
    odd = [(1, near)] + [(plane | 1, swap(piece, "adp", 1)) for plane, piece in mine[1:]]

    def others(pieces):
        return [(plane, off, swap(piece, "grp", off)) for plane, piece in pieces for off in range(1, groups)]

    swapped = others(odd[:1]) + others(mine[1:]) + others(odd[1:])
    held = [(plane, 0, piece) for plane, piece in [(1, close)] + mine[1:] + odd[1:]]

    def terms(pieces, start):
        return [(start + i, k, 0, (plane, off, k)) for i, (plane, off, _) in enumerate(pieces) for k in range(share)]

    def more(low, pieces, dtype, cost=COST):
        arrays, every = [p for *_, p in pieces], terms(pieces, 0)
        if low is None:
            every += [(len(arrays), k, 0, ("plane", 0, k)) for k in range(here)]
            arrays = arrays + [down]
        return low_rows(ids, tokens, here, share, [((0, features), every)], arrays, low, dtype, cost)

    low = more(None, held[: len(mine)], F32, lasting(5))
    low, ups, *came = together(low, adapter_up, *(swap(block, "tp", 1) for block in blocks[:half]))

    def both(low):
        bit = 1
        while bit < parts // 2:
            low = add(low, swap(low, "tp", bit))
            bit *= 2
        return low, swap(low, "tp", bit)

    rest = held[len(mine) :]
    order = [0]
    bit = planes // 2
    while bit > 1:
        (plane, off, piece), other = rest[0], swap(ups, "adp", bit)
        piece, other = together(piece, other)
        rest[0], ups = (plane, off, piece), joined(ups, other)
        order += [plane | bit for plane in order]
        bit //= 2
    low = more(low, swapped[:1], F32, lasting(5))
    low = more(low, swapped[1:-1] + rest, BF16, lasting(5))
    more_ups = swap(ups, "adp", 1)
    low, other = both(low)

    sums = [[block, pair] for block, pair in zip(blocks[half:], came)]
    bit = 2
    while bit < parts:
        came = [swap(add(*terms), "tp", bit) for terms in sums[1::2]]
        sums = [terms + [pair] for terms, pair in zip(sums[0::2], came)]
        bit *= 2

    named = [("plane", plane | side, k) for side in (0, 1) for plane in order for k in range(here)]
    piece = swapped[-1][2]
    kept = compact(chosen, piece)
    kept = [kept] + [swap(kept, "tp", offset) for offset in range(1, parts)]
    up, mask = rotated_ups(ids, bits, matrix, here, share, named, ups, more_ups)
    last, rest = most(low, other, up, mask, scale, bits, matrix, sums[0], here, share, [named.index(("plane", planes - 1, k)) for k in range(share)])
    return final(kept, pick, last, rest)


def solution(mesh):
    return jax.shard_map(
        local,
        mesh=mesh,
        in_specs=(
            P(("grp", "adp"), "tp"),
            P(("grp", "adp"), None),
            P("tp", None),
            P("tp"),
            P("adp", "tp", None),
            P("adp", None, "tp"),
            P(),
        ),
        out_specs=P(("grp", "adp"), "tp"),
        check_vma=False,
    )
```

```python
import functools

import jax
import jax.numpy as jnp
import numpy as np
from jax import lax
from jax.experimental import pallas as pl
from jax.experimental.pallas import tpu as pltpu
from jax.sharding import PartitionSpec as P

VMEM = pl.BlockSpec(memory_space=pltpu.VMEM)
SMEM = pl.BlockSpec(memory_space=pltpu.SMEM)
F32, BF16 = jnp.float32, jnp.bfloat16
LAST = (((1,), (1,)), ((), ()))
FIRST = (((0,), (0,)), ((), ()))


def params(mib):
    return pltpu.CompilerParams(vmem_limit_bytes=mib << 20)


COST = pl.CostEstimate(flops=1, bytes_accessed=1, transcendentals=0)


def lasting(microseconds):
    return pl.CostEstimate(flops=int(microseconds * 1e9), bytes_accessed=1, transcendentals=0)


def hadamard(size):
    index = np.arange(size)
    shared = index[:, None] & index[None, :]
    parity = np.zeros_like(shared)
    while shared.any():
        parity, shared = parity ^ (shared & 1), shared >> 1
    return jnp.asarray(1 - 2 * parity, BF16)


def swap(x, axis, bit):
    return lax.ppermute(x, axis, [(i, i ^ bit) for i in range(lax.axis_size(axis))])


def together(*values):
    return lax.optimization_barrier(values)


def rotate(value, signs, matrix):
    head = matrix.shape[0]
    scale = signs * (1.0 / np.sqrt(head))
    turned = []
    for at in range(0, value.shape[1], head):
        signed = value[:, at : at + head] * scale
        high = signed.astype(BF16)
        rest = (signed - high.astype(F32)).astype(BF16)
        turned.append(
            jnp.dot(high, matrix, preferred_element_type=F32) + jnp.dot(rest, matrix, preferred_element_type=F32)
        )
    return turned


def partial_kernel(offsets, parts, tokens_ref, weight_ref, *refs):
    me, width = lax.axis_index("tp"), weight_ref.shape[1] // parts
    for offset, out_ref in zip(offsets, refs[-len(offsets) :]):
        at = pl.multiple_of(jnp.bitwise_xor(me, offset) * width, width)
        product = jnp.dot(tokens_ref[...], weight_ref[:, pl.ds(at, width)], preferred_element_type=F32)
        out_ref[...] = product.astype(BF16)


def partials(tokens, weight, parts, offsets, cost, *before):
    block = jax.ShapeDtypeStruct((tokens.shape[0], weight.shape[1] // parts), BF16)
    return pl.pallas_call(
        functools.partial(partial_kernel, offsets, parts),
        in_specs=[VMEM] * (2 + len(before)),
        out_specs=[VMEM] * len(offsets),
        out_shape=[block] * len(offsets),
        compiler_params=params(24),
        cost_estimate=cost,
        name="partials",
    )(tokens, weight, *before)


def add_kernel(*refs):
    total = refs[0][...].astype(F32)
    for ref in refs[1:-1]:
        total = total + ref[...].astype(F32)
    refs[-1][...] = total.astype(BF16)


def add(*terms):
    return pl.pallas_call(
        add_kernel,
        in_specs=[VMEM] * len(terms),
        out_specs=VMEM,
        out_shape=jax.ShapeDtypeStruct(terms[0].shape, BF16),
        compiler_params=params(16),
        cost_estimate=COST,
        name="add",
    )(*terms)


def adapter(here, share, name):
    z = lax.axis_index("adp")
    if name[0] == "plane":
        return jnp.bitwise_xor(z, name[1]) * here + name[2]
    plane, off, k = name
    return jnp.bitwise_xor(z, plane) * here + jnp.bitwise_xor(lax.axis_index("grp"), off) * share + k


def low_kernel(groups, here, share, rank, more, ids_ref, tokens_ref, *refs):
    out_ref = refs[-1]
    total = refs[-2][...] if more else None
    for (start, stop), terms in groups:
        rows = [refs[i][k, :, cut : cut + stop - start] for i, k, cut, _ in terms]
        joined = rows[0] if len(rows) == 1 else jnp.concatenate(rows, axis=0)
        product = lax.dot_general(joined, tokens_ref[:, start:stop], LAST, preferred_element_type=F32)
        for n, (_, _, _, name) in enumerate(terms):
            mine = ids_ref[...] == adapter(here, share, name)
            term = jnp.where(mine, product[n * rank : (n + 1) * rank], 0.0)
            total = term if total is None else total + term
    out_ref[...] = total.astype(out_ref.dtype)


def low_rows(ids, tokens, here, share, groups, arrays, before, dtype, cost=COST):
    rank = arrays[0].shape[1]
    more = [] if before is None else [before]
    return pl.pallas_call(
        functools.partial(low_kernel, groups, here, share, rank, bool(more)),
        in_specs=[VMEM] * (2 + len(arrays) + len(more)),
        out_specs=VMEM,
        out_shape=jax.ShapeDtypeStruct((rank, tokens.shape[0]), dtype),
        compiler_params=params(24),
        cost_estimate=cost,
        name="low_rows",
    )(ids, tokens, *arrays, *more)


def ups_kernel(named, terms, here, share, rank, ids_ref, bits_ref, matrix_ref, *refs):
    up_ref, mask_ref = refs[-2:]
    width = up_ref.shape[1]
    signs = (1 - 2 * bits_ref[...]).astype(F32)
    for n, (i, k, cut) in enumerate(terms):
        turned = rotate(refs[i][k, :, cut : cut + width].astype(F32), signs, matrix_ref[...])
        up_ref[n * rank : (n + 1) * rank, :] = jnp.concatenate(turned, axis=1).astype(BF16)
    ids = jnp.broadcast_to(ids_ref[...], (rank, ids_ref.shape[1])).T
    mask_ref[...] = jnp.zeros_like(mask_ref)
    for n, name in enumerate(named):
        mine = ids == adapter(here, share, name)
        mask_ref[:, n * rank : (n + 1) * rank] = jnp.where(mine, 1.0, 0.0).astype(BF16)


def rotated_ups(ids, bits, matrix, here, share, named, terms, arrays, width):
    rank, rows = arrays[0].shape[1], ids.shape[1]
    columns = -(-len(named) * rank // 128) * 128
    return pl.pallas_call(
        functools.partial(ups_kernel, named, terms, here, share, rank),
        in_specs=[VMEM] * (3 + len(arrays)),
        out_specs=[VMEM, VMEM],
        out_shape=[jax.ShapeDtypeStruct((len(terms) * rank, width), BF16), jax.ShapeDtypeStruct((rows, columns), BF16)],
        compiler_params=params(32),
        cost_estimate=COST,
        name="rotated_ups",
    )(ids, bits, matrix, *arrays)


def pick_kernel(named, here, share, ids_ref, tokens_ref, pick_ref, chosen_ref):
    rows, slots = pick_ref.shape[0], pick_ref.shape[1] // len(named)
    earlier = lax.broadcasted_iota(jnp.int32, (rows, rows), 0) < lax.broadcasted_iota(jnp.int32, (rows, rows), 1)
    earlier = jnp.where(earlier, 1.0, 0.0).astype(BF16)
    ids = jnp.broadcast_to(ids_ref[...], (8, rows))
    for k, name in enumerate(named):
        mine = ids == adapter(here, share, name)
        rank = jnp.dot(jnp.where(mine, 1.0, 0.0).astype(BF16), earlier, preferred_element_type=F32)
        rank = jnp.where(mine, rank, -1.0)
        rank = jnp.broadcast_to(rank[:1], (128, rows)).T
        for at in range(0, slots, 128):
            slot = (lax.broadcasted_iota(jnp.int32, (rows, 128), 1) + at).astype(F32)
            pick_ref[:, k * slots + at : k * slots + at + 128] = jnp.where(rank == slot, 1.0, 0.0).astype(BF16)
    rows = lax.dot_general(pick_ref[...], tokens_ref[...], FIRST, preferred_element_type=F32)
    chosen_ref[...] = rows.astype(BF16)


def picked(ids, tokens, here, share, named, slots):
    rows, features = tokens.shape
    columns = len(named) * slots
    return pl.pallas_call(
        functools.partial(pick_kernel, named, here, share),
        in_specs=[VMEM] * 2,
        out_specs=[VMEM] * 2,
        out_shape=[jax.ShapeDtypeStruct((rows, columns), BF16), jax.ShapeDtypeStruct((columns, features), BF16)],
        compiler_params=params(24),
        cost_estimate=COST,
        name="picked",
    )(ids, tokens)


def compact_kernel(chosen_ref, piece_ref, out_ref):
    share, features = piece_ref.shape[0], chosen_ref.shape[1]
    slots = chosen_ref.shape[0] // share
    for k in range(share):
        mine = slice(k * slots, (k + 1) * slots)
        product = lax.dot_general(
            piece_ref[k, :, :features], chosen_ref[mine], LAST, preferred_element_type=F32
        )
        out_ref[:, mine] = product.astype(BF16)


def compact(chosen, piece):
    return pl.pallas_call(
        compact_kernel,
        in_specs=[VMEM] * 2,
        out_specs=VMEM,
        out_shape=jax.ShapeDtypeStruct((piece.shape[1], chosen.shape[0]), BF16),
        compiler_params=params(24),
        cost_estimate=lasting(2),
        name="compact",
    )(chosen, piece)


def most_kernel(mine_ref, theirs_ref, up_ref, mask_ref, near_ref, piece_ref, scale_ref, bits_ref, matrix_ref, *refs):
    terms, (last_ref, out_ref) = refs[:-2], refs[-2:]
    rank, width = piece_ref.shape[1], out_ref.shape[1]
    low = (mine_ref[...].astype(F32) + theirs_ref[...].astype(F32)).astype(BF16).T
    columns = mask_ref.shape[1]
    signs = (1 - 2 * bits_ref[...]).astype(F32)
    ups = [up_ref[...]]
    for k in range(near_ref.shape[0]):
        turned = rotate(near_ref[k].astype(F32), signs, matrix_ref[...])
        ups.append(jnp.concatenate(turned, axis=1).astype(BF16))
    missing = columns - sum(up.shape[0] for up in ups)
    if missing:
        ups.append(jnp.zeros((missing, up_ref.shape[1]), BF16))
    spread = jnp.concatenate([low] * (columns // rank), axis=1) * mask_ref[...]
    delta = jnp.dot(spread, jnp.concatenate(ups, axis=0), preferred_element_type=F32)
    value = functools.reduce(jnp.add, [ref[...].astype(F32) for ref in terms]) * scale_ref[...]
    out_ref[...] = jnp.concatenate(rotate(value, signs, matrix_ref[...]), axis=1) + delta
    for k in range(piece_ref.shape[0]):
        turned = rotate(piece_ref[k, :, piece_ref.shape[2] - width :].astype(F32), signs, matrix_ref[...])
        last_ref[k * rank : (k + 1) * rank] = jnp.concatenate(turned, axis=1).astype(BF16)


def most(mine, theirs, up, mask, near, piece, scale, bits, matrix, terms):
    return pl.pallas_call(
        most_kernel,
        in_specs=[VMEM] * (9 + len(terms)),
        out_specs=[VMEM] * 2,
        out_shape=[
            jax.ShapeDtypeStruct((piece.shape[0] * piece.shape[1], terms[0].shape[1]), BF16),
            jax.ShapeDtypeStruct(terms[0].shape, F32),
        ],
        compiler_params=params(32),
        cost_estimate=COST,
        name="most",
    )(mine, theirs, up, mask, near, piece, scale, bits, matrix, *terms)


def final_kernel(pick_ref, last_ref, most_ref, *refs):
    kept_refs, (out_ref, half_ref, sems) = refs[:-3], refs[-3:]
    rank, slots = kept_refs[0].shape
    share = last_ref.shape[0] // rank
    slots = slots // share
    low = functools.reduce(jnp.add, [ref[...].astype(F32) for ref in kept_refs]).astype(BF16).T
    deltas = []
    for k in range(share):
        up = last_ref[k * rank : (k + 1) * rank]
        deltas.append(jnp.dot(low[k * slots : (k + 1) * slots], up, preferred_element_type=F32).astype(BF16))
    delta = deltas[0] if share == 1 else jnp.concatenate(deltas, axis=0)
    count, rows, _ = half_ref.shape
    copies = []
    for n in range(count):
        part = slice(n * rows, (n + 1) * rows)
        result = most_ref[part] + jnp.dot(pick_ref[part], delta, preferred_element_type=F32)
        half_ref[n] = result.astype(BF16)
        copies.append(pltpu.make_async_copy(half_ref.at[n], out_ref.at[pl.ds(n * rows, rows)], sems.at[n]))
        copies[-1].start()
    for copy in copies:
        copy.wait()


def final(kept, pick, last, rest):
    return pl.pallas_call(
        final_kernel,
        in_specs=[VMEM] * (3 + len(kept)),
        out_specs=pl.BlockSpec(memory_space=pl.ANY),
        out_shape=jax.ShapeDtypeStruct(rest.shape, BF16),
        scratch_shapes=[pltpu.VMEM((2, rest.shape[0] // 2, rest.shape[1]), BF16), pltpu.SemaphoreType.DMA((2,))],
        compiler_params=params(32),
        cost_estimate=COST,
        name="final",
    )(pick, last, rest, *kept)


def local(tokens, adapter_ids, base_weight, channel_scale, adapter_down, adapter_up, sign_bits):
    planes, groups, parts = lax.axis_size("adp"), lax.axis_size("grp"), lax.axis_size("tp")
    features = tokens.shape[1]
    here, _, rank = adapter_down.shape
    width = adapter_up.shape[2]
    share = here // groups
    matrix = hadamard(sign_bits.shape[0])
    bits, scale, ids = sign_bits[None, :], channel_scale[None, :], adapter_ids.T
    down = jnp.swapaxes(adapter_down, 1, 2)

    start = lax.axis_index("grp") * share
    own = lax.dynamic_slice_in_dim(down, start, share, 0)
    near = swap(own, "adp", 1)
    mine = [(0, jnp.concatenate([own, lax.dynamic_slice_in_dim(adapter_up, start, share, 0)], axis=2))]
    bit = planes // 2
    while bit > 1:
        mine += [(plane | bit, swap(piece, "adp", bit)) for plane, piece in mine]
        bit //= 2
    half = parts // 2
    offsets = (*range(1, parts, 2), *range(2, parts, 2))
    blocks = list(partials(tokens, base_weight, parts, offsets, lasting(4)))
    near, blocks[-1] = together(near, blocks[-1])
    (block,) = partials(tokens, base_weight, parts, (0,), COST, blocks[-1])
    slots = -(-2 * tokens.shape[0] // (here * planes) // 128) * 128
    lasts = [(planes - 1, groups - 1, k) for k in range(share)]
    pick, chosen = picked(ids, tokens, here, share, lasts, slots)
    close, block, pick, chosen, *far = together(near, block, pick, chosen, *(piece for _, piece in mine[1:]))
    blocks = blocks[:half] + [block] + blocks[half:]
    mine = mine[:1] + [(plane, piece) for (plane, _), piece in zip(mine[1:], far)]
    odd = [(1, near)] + [(plane | 1, swap(piece, "adp", 1)) for plane, piece in mine[1:]]

    def others(pieces):
        return [(plane, off, swap(piece, "grp", off)) for plane, piece in pieces for off in range(1, groups)]

    swapped = others(odd[:1]) + others(mine[1:]) + others(odd[1:])
    held = [(plane, 0, piece) for plane, piece in [(1, close)] + mine[1:] + odd[1:]]

    def terms(pieces, start):
        return [(start + i, k, 0, (plane, off, k)) for i, (plane, off, _) in enumerate(pieces) for k in range(share)]

    def more(low, pieces, dtype, cost=COST):
        arrays, every = [p for *_, p in pieces], terms(pieces, 0)
        if low is None:
            every += [(len(arrays), k, 0, ("plane", 0, k)) for k in range(here)]
            arrays = arrays + [down]
        return low_rows(ids, tokens, here, share, [((0, features), every)], arrays, low, dtype, cost)

    low = more(None, held[: len(mine)] + swapped[:1], F32, lasting(2))
    blocks[half], *came = together(blocks[half], *(swap(block, "tp", 1) for block in blocks[:half]))

    def both(low):
        bit = 1
        while bit < parts // 2:
            low = add(low, swap(low, "tp", bit))
            bit *= 2
        return low, swap(low, "tp", bit)

    rest = held[len(mine) :]
    low = more(low, swapped[1:-1] + rest, BF16, lasting(5))
    low, up = together(low, adapter_up)
    near_up = swap(up, "adp", 1)
    low, other = both(low)

    sums = [[block, pair] for block, pair in zip(blocks[half:], came)]
    bit = 2
    while bit < parts:
        came = [swap(add(*terms), "tp", bit) for terms in sums[1::2]]
        sums = [terms + [pair] for terms, pair in zip(sums[0::2], came)]
        bit *= 2

    far = [one for one in held + swapped[:-1] if one[0] > 1]
    named = [("plane", 0, k) for k in range(here)]
    named += [(plane, off, k) for plane, off, _ in far for k in range(share)]
    ups = [(0, k, 0) for k in range(here)] + [(1 + i, k, features) for i in range(len(far)) for k in range(share)]
    named += [("plane", 1, k) for k in range(here)]
    arrays = [adapter_up] + [piece for *_, piece in far]
    up, mask = rotated_ups(ids, bits, matrix, here, share, named, ups, arrays, width)

    piece, up, mask = together(swapped[-1][2], up, mask)
    kept = compact(chosen, piece)
    kept = [kept] + [swap(kept, "tp", offset) for offset in range(1, parts)]
    last, rest = most(low, other, up, mask, near_up, piece, scale, bits, matrix, sums[0])
    return final(kept, pick, last, rest)


def solution(mesh):
    return jax.shard_map(
        local,
        mesh=mesh,
        in_specs=(
            P(("grp", "adp"), "tp"),
            P(("grp", "adp"), None),
            P("tp", None),
            P("tp"),
            P("adp", "tp", None),
            P("adp", None, "tp"),
            P(),
        ),
        out_specs=P(("grp", "adp"), "tp"),
        check_vma=False,
    )
```
